512 devices in a mesh: pos: 128 (over z, y, core), cuts: 4 (over x).
Axes of the slice: x: 4, y: 8, z: 8, core: 2. Of those that a mesh axis runs over, the one named last changes fastest.
Arguments:
- specimen: float32 [2, 4, 16384, 512], P(None, 'cuts', 'pos'), may hold values from -4 to 4
- probe: float32 [2, 128, 128], replicated, may hold values from -4 to 4
- amplitude: float32 [1024, 128, 128], P('pos'), may hold values from 0 to 2
- offsets: int32 [2, 1024], P(None, 'pos'), may hold values from 0 to 16256, as said below
- live: int32 [128], P('pos'), may hold values from 1 to 8, 512 in all
Outputs:
- slice_grad: float32 [2, 4, 16384, 512], P(None, 'cuts', 'pos')
- probe_grad: float32 [2, 128, 128], P(None, 'cuts')
The draws below stay inside these ranges and needn't reach their ends.
Inputs may be any that keep to these rules, and one draw needn't show every extreme that they name: `offsets`: position slot p belongs to index p div 8 of pos, and its row offset lies in that index's rows: from (p div 8) * 128 to that plus 128 - 1; every window lies inside the specimen (row offset at most 16256, column offset at most 384); the first slot's window starts at row 0 and column 0, the last slot's at row 16256 and column 384. `live`: the counts sum to half of all 1024 slots; some index of pos has all 8 slots used.
All inputs are finite; a program needn't handle non-finite values. No bound on the sum of `live` on one device may be relied on, other than what follows from the above.
Results may differ from the reference program's by a relative error of at most 0.00029.
Values sent between devices are 32-bit elements; how exact they have to be, the bound alone decides.
No kernel may reach another device: no remote copies, remote signals or barrier semaphores. Data moves between devices by JAX's collectives and lax.ppermute only.
A program may use at most 64 MiB of HBM per device.

```python
import math
import jax
import jax.numpy as jnp
import numpy as np
from jax import lax

W = 128
STRIPE = 128
NC = 512
POS_CAP = 8
SLICES = 4
NR = 16384
POSITIONS = 1024
N_POS = 128


def draw_offsets(key, part):
    key = jax.random.fold_in(key, 11)
    row_key, col_key = jax.random.split(key)
    owners = POSITIONS // POS_CAP
    owner = jnp.arange(POSITIONS, dtype=jnp.int32) // POS_CAP
    upper = jnp.where(owner == owners - 1, STRIPE - W + 1, STRIPE)
    row_offsets = owner * STRIPE + jax.random.randint(row_key, (POSITIONS,), 0, upper)
    col_offsets = jax.random.randint(col_key, (POSITIONS,), 0, NC - W + 1)
    row_offsets = row_offsets.at[0].set(0).at[POSITIONS - 1].set(owners * STRIPE - W)
    col_offsets = col_offsets.at[0].set(0).at[POSITIONS - 1].set(NC - W)
    return jnp.stack([row_offsets, col_offsets]).astype(jnp.int32)


def steps_of(rng, shape, pieces, least, largest):
    def one(axis_at, blocks):
        steps = jax.random.uniform(jax.random.fold_in(jax.random.fold_in(rng, 6), axis_at), (blocks,), jnp.float32, least / len(pieces), largest / len(pieces))
        return jnp.repeat(jnp.exp(steps), shape[axis_at] // blocks).reshape((-1,) + (1,) * (len(shape) - axis_at - 1))

    level = one(*pieces[0])
    for cut in pieces[1:]:
        level = level * one(*cut)
    return level


def profile(amount, total, most, skew):
    portions = [(1 << 20) // math.isqrt(standing ** skew) + 1 for standing in range(2, amount + 1)]
    surplus, given = total - most - (amount - 1), [1] * (amount - 1)
    while surplus > 0:
        candidates = [i for i in range(amount - 1) if given[i] < most]
        pool, budget = sum([portions[i] for i in candidates]), surplus
        for i in candidates:
            more = min(most - given[i], max(1, budget * portions[i] // pool), surplus)
            given[i] = given[i] + more
            surplus = surplus - more
    return np.array([most] + given)


def ragged_sizes(rng, count, total, most, slope):
    if count == 2:
        one = jax.random.randint(rng, (), max(1, total - most), min(most, total - 1) + 1)
        return jnp.stack([one, total - one])
    sizes = jnp.asarray(profile(count, total, most, slope), jnp.int32)
    twos = (count - 1) // 2
    donor, taker = sizes[1:1 + 2 * twos:2], sizes[2:2 + 2 * twos:2]
    slack = jnp.minimum(donor - 1, most - taker)
    shifted = jax.random.randint(jax.random.fold_in(rng, 1), (twos,), 0, 1 << 20) % (slack + 1)
    sizes = sizes.at[1:1 + 2 * twos:2].set(donor - shifted).at[2:2 + 2 * twos:2].set(taker + shifted)
    return sizes[jax.random.permutation(jax.random.fold_in(rng, 2), count)]


def scatter_about(rng, extent, width, bound, cuts=(), kind=jnp.bfloat16):
    entries = jax.random.normal(rng, extent, jnp.float32) * width
    if len(cuts) > 0:
        entries = steps_of(rng, extent, cuts, -0.22, 0.18) * entries
    return jnp.clip(entries, min=-bound, max=bound).astype(kind)


def setup_inputs(seed: int = 0) -> dict:
    splits = jax.random.split(jax.random.key(seed), 6)
    return {
        "specimen": scatter_about(splits[0], (2, SLICES, NR, NC), 0.7071, 4.0, ((1, 4), (2, 128)), jnp.float32),
        "probe": scatter_about(splits[1], (2, W, W), 0.7071, 4.0, (), jnp.float32),
        "amplitude": jnp.clip(2.0 * jax.random.uniform(splits[2], (POSITIONS, W, W), jnp.float32) ** steps_of(splits[2], (POSITIONS, W, W), ((0, 128),), -0.2, 0.2), 0.0, 2.0),
        "offsets": draw_offsets(jax.random.fold_in(splits[5], 71), 0),
        "live": ragged_sizes(splits[4], N_POS, N_POS * POS_CAP // 2, POS_CAP, 1).astype(jnp.int32),
    }


FRESNEL = 0.7

def make_tables(pattern):
    index = jnp.arange(pattern, dtype=jnp.int32)
    product = index[:, None] * index[None, :] % pattern
    angle = 2.0 * math.pi / pattern * product.astype(jnp.float32)
    scale = 1.0 / math.sqrt(pattern)
    four_real = jnp.cos(angle) * scale
    four_imag = -jnp.sin(angle) * scale
    signed = jnp.where(index < pattern // 2, index, index - pattern)
    phase = FRESNEL * math.pi / pattern * (signed * signed).astype(jnp.float32)
    spacing = (index[:, None] - index[None, :]) % pattern
    turns = spacing[:, :, None] * index[None, None, :] % pattern
    argument = phase[None, None, :] + 2.0 * math.pi / pattern * turns.astype(jnp.float32)
    prop_real = lax.optimization_barrier(jnp.mean(jnp.cos(argument), axis=2))
    prop_imag = lax.optimization_barrier(jnp.mean(jnp.sin(argument), axis=2))
    return (four_real, four_imag, prop_real, prop_imag)

def complex_mult(a_real, a_imag, b_real, b_imag):
    return (a_real * b_real - a_imag * b_imag, a_real * b_imag + a_imag * b_real)

def conj_mult(a_real, a_imag, b_real, b_imag):
    return (a_real * b_real + a_imag * b_imag, a_real * b_imag - a_imag * b_real)

def mat_left(table, batch):
    return jnp.einsum('mk,bkn->bmn', table, batch, precision=lax.Precision.HIGHEST)

def mat_right(batch, table):
    return jnp.einsum('bmk,kn->bmn', batch, table, precision=lax.Precision.HIGHEST)

def both_sides(wave_real, wave_imag, table_real, table_imag):
    left_real = mat_left(table_real, wave_real) - mat_left(table_imag, wave_imag)
    left_imag = mat_left(table_real, wave_imag) + mat_left(table_imag, wave_real)
    right_real = mat_right(left_real, table_real) - mat_right(left_imag, table_imag)
    right_imag = mat_right(left_real, table_imag) + mat_right(left_imag, table_real)
    return (right_real, right_imag)

def scatter_add(canvas, values, row_offsets, col_offsets):
    anchor = jnp.zeros((), jnp.int32)

    def add_one(position, current_canvas):
        corner = (anchor, row_offsets[position], col_offsets[position])
        current = lax.dynamic_slice(current_canvas, corner, values.shape[1:])
        return lax.dynamic_update_slice(current_canvas, current + values[position], corner)
    return lax.fori_loop(0, values.shape[0], add_one, canvas)

def reference(specimen, probe, amplitude, offsets, live):
    four_real, four_imag, prop_real, prop_imag = make_tables(W)
    row_offsets = offsets[0].astype(jnp.int32)
    col_offsets = offsets[1].astype(jnp.int32)
    slot_index = jnp.arange(POSITIONS, dtype=jnp.int32)
    counts = live[slot_index // POS_CAP]
    weight = (slot_index % POS_CAP < counts).astype(jnp.float32)
    anchor = jnp.zeros((), jnp.int32)

    def windows_of(layer_index):
        layer = specimen[:, layer_index]

        def window(row_at, col_at):
            return lax.dynamic_slice(layer, (anchor, row_at, col_at), (2, W, W))
        return jax.vmap(window)(row_offsets, col_offsets)
    wave_real = jnp.broadcast_to(probe[0], (POSITIONS, W, W))
    wave_imag = jnp.broadcast_to(probe[1], (POSITIONS, W, W))
    stored = []
    for layer_index in range(SLICES):
        windows = windows_of(layer_index)
        patch_real = windows[:, 0]
        patch_imag = windows[:, 1]
        stored.append((wave_real, wave_imag, patch_real, patch_imag))
        exit_real, exit_imag = complex_mult(wave_real, wave_imag, patch_real, patch_imag)
        if layer_index < SLICES - 1:
            wave_real, wave_imag = both_sides(exit_real, exit_imag, prop_real, prop_imag)
    far_real, far_imag = both_sides(exit_real, exit_imag, four_real, four_imag)
    magnitude = jnp.sqrt(far_real * far_real + far_imag * far_imag)
    factor = weight[:, None, None] * (1.0 - amplitude / jnp.maximum(magnitude, 1.0))
    back_real, back_imag = both_sides(factor * far_real, factor * far_imag, four_real, -four_imag)
    lighting = weight[:, None, None] * (probe[0] * probe[0] + probe[1] * probe[1])[None]
    illum = scatter_add(jnp.zeros((1, NR, NC), jnp.float32), lighting[:, None], row_offsets, col_offsets)[0]
    gradients = [None] * SLICES
    for layer_index in range(SLICES - 1, -1, -1):
        inc_real, inc_imag, patch_real, patch_imag = stored[layer_index]
        term_real, term_imag = conj_mult(inc_real, inc_imag, back_real, back_imag)
        values = jnp.stack([term_real, term_imag], axis=1)
        summed = scatter_add(jnp.zeros((2, NR, NC), jnp.float32), values, row_offsets, col_offsets)
        gradients[layer_index] = summed / (illum + 1.0)
        carry_real, carry_imag = conj_mult(patch_real, patch_imag, back_real, back_imag)
        if layer_index > 0:
            back_real, back_imag = both_sides(carry_real, carry_imag, prop_real, -prop_imag)
    slice_grad = jnp.stack(gradients, axis=1)
    probe_grad = jnp.stack([lax.optimization_barrier(jnp.sum(carry_real, axis=0)), lax.optimization_barrier(jnp.sum(carry_imag, axis=0))]) / math.sqrt(POSITIONS)
    return (slice_grad, probe_grad)
```

```python
import functools
import math

import jax
import jax.numpy as jnp
import numpy as np
from jax import lax
from jax.experimental import pallas as pl
from jax.experimental.pallas import tpu as pltpu
from jax.sharding import PartitionSpec as P

FRESNEL = 0.7
VMEM = pltpu.CompilerParams(vmem_limit_bytes=48 * 1024 * 1024)


def make_tables(n):
    index = np.arange(n)
    four = np.exp(-2j * math.pi / n * (index[:, None] * index[None, :] % n)) / math.sqrt(n)
    signed = np.where(index < n // 2, index, index - n)
    spacing = (index[:, None] - index[None, :]) % n
    turns = spacing[:, :, None] * index[None, None, :] % n
    phase = FRESNEL * math.pi / n * (signed * signed)
    prop = np.mean(np.exp(1j * (phase[None, None, :] + 2.0 * math.pi / n * turns)), axis=2)
    return four, prop


def split_pair(table):
    whole = np.block([[table.real, table.imag], [-table.imag, table.real]]).astype(np.float32)
    lead = whole.astype(jnp.bfloat16)
    return np.stack([lead, (whole - lead.astype(np.float32)).astype(jnp.bfloat16)])


def table_stack(n):
    four, prop = make_tables(n)
    return np.stack([split_pair(prop), split_pair(prop.conj()), split_pair(four), split_pair(four.conj())])


def parts(x):
    lead = x.astype(jnp.bfloat16)
    return lead, (x - lead.astype(jnp.float32)).astype(jnp.bfloat16)


def dot(a, b):
    return jnp.dot(a, b, preferred_element_type=jnp.float32)


def both_sides(wave, tables, which):
    real, imag = wave
    count, n, _ = real.shape
    whole = jnp.concatenate([real.reshape(count * n, n), imag.reshape(count * n, n)], axis=1)
    lead, trail = parts(whole)
    right_lead, right_trail = tables[which, 0], tables[which, 1]
    mid = dot(lead, right_lead) + (dot(trail, right_lead) + dot(lead, right_trail))
    mid = jnp.concatenate(
        [
            jnp.concatenate([mid[p * n : (p + 1) * n, h * n : (h + 1) * n] for p in range(count)], axis=1)
            for h in range(2)
        ],
        axis=0,
    )
    lead, trail = parts(mid)
    left_lead, left_trail = tables[which ^ 1, 0], tables[which ^ 1, 1]
    out = dot(left_lead, lead) + (dot(left_lead, trail) + dot(left_trail, lead))
    real = jnp.stack([out[:n, p * n : (p + 1) * n] for p in range(count)])
    imag = jnp.stack([out[n:, p * n : (p + 1) * n] for p in range(count)])
    return real, imag


def complex_mult(a, b):
    return a[0] * b[0] - a[1] * b[1], a[0] * b[1] + a[1] * b[0]


def conj_mult(a, b):
    return a[0] * b[0] + a[1] * b[1], a[0] * b[1] - a[1] * b[0]


def spot(info, slot, columns, n):
    row = info[0, slot]
    col = info[1, slot]
    top = pl.multiple_of(row // 8 * 8, 8)
    band = pl.multiple_of(jnp.minimum(col // n * n, columns - 2 * n), n)
    return (pl.ds(top, n + 8), pl.ds(band, 2 * n)), row - top, col - band


def cut_out(box, down, right):
    n = box.shape[1] // 2
    turn = lax.rem(n - right, n)
    lane = lax.broadcasted_iota(jnp.int32, (n + 8, n), 1)
    wide = jnp.where(lane < n - right, pltpu.roll(box[:, :n], turn, axis=1), pltpu.roll(box[:, n:], turn, axis=1))
    groups = pltpu.roll(wide.reshape(n // 8 + 1, 8, n), lax.rem(8 - down, 8), axis=1)
    line = lax.broadcasted_iota(jnp.int32, (n // 8, 8, n), 1)
    return jnp.where(line < 8 - down, groups[:-1], groups[1:]).reshape(n, n)


def placed(value, down, right):
    n = value.shape[0]
    groups = pltpu.roll(value.reshape(n // 8, 8, n), down, axis=1)
    empty = jnp.zeros((1, 8, n), jnp.float32)
    line = lax.broadcasted_iota(jnp.int32, (n // 8 + 1, 8, n), 1)
    tall = jnp.where(
        line >= down, jnp.concatenate([groups, empty], axis=0), jnp.concatenate([empty, groups], axis=0)
    ).reshape(n + 8, n)
    tall = pltpu.roll(tall, lax.rem(right, n), axis=1)
    lane = lax.broadcasted_iota(jnp.int32, (n + 8, n), 1)
    return jnp.concatenate([jnp.where(lane >= right, tall, 0.0), jnp.where(lane < right, tall, 0.0)], axis=1)


def light_kernel(info, probe, inner, rim, canvas):
    n = probe.shape[1]
    slots = info.shape[1]
    stripe, columns = inner.shape
    canvas[...] = jnp.zeros_like(canvas)
    power = probe[0] * probe[0] + probe[1] * probe[1]

    def one(slot, carry):
        at, down, right = spot(info, slot, columns, n)
        canvas[at] = canvas[at] + placed(power, down, right)
        return carry

    lax.fori_loop(0, jnp.minimum(info[2, 0], slots), one, 0)
    inner[...] = canvas[:stripe]
    rim[...] = canvas[stripe:]


def window_kernel(info, own, following, *rest):
    outs, ext = rest[:-1], rest[-1]
    cuts = len(outs)
    stripe, columns = own.shape[1:]
    pair, _, n, _ = outs[0].shape
    me = info[2, 1]
    ext[:, :stripe] = own[...]
    ext[:, stripe:] = following[...]
    for away in range(cuts):
        target = lax.rem(me + away, cuts)
        for which in range(pair):
            at, down, right = spot(info, target + which * cuts, columns, n)
            for part in range(2):
                outs[away][which, part] = cut_out(ext[(part, *at)], down, right)


def wave_kernel(cuts, info, probe, amplitude, tables, *rest):
    arrived, rest = rest[:cuts], rest[cuts:]
    terms, probe_out, rest = rest[:cuts], rest[cuts], rest[cuts + 1 :]
    patch, term, amp, sems = rest
    pair, _, n, _ = arrived[0].shape
    me = info[2, 1]
    live = info[2, 0]
    copies = [
        pltpu.make_async_copy(amplitude.at[me + which * cuts], amp.at[which], sems.at[which]) for which in range(pair)
    ]
    for copy in copies:
        copy.start()
    for away in range(cuts):
        patch[lax.rem(me + cuts - away, cuts)] = arrived[away][...]

    def patch_of(layer):
        return patch[layer, :, 0], patch[layer, :, 1]

    wave = tuple(jnp.broadcast_to(probe[part][None], (pair, n, n)) for part in range(2))
    incident = []
    for layer in range(cuts):
        incident.append(wave)
        wave = complex_mult(wave, patch_of(layer))
        if layer < cuts - 1:
            wave = both_sides(wave, tables, 0)
    far = both_sides(wave, tables, 2)
    for copy in copies:
        copy.wait()
    magnitude = jnp.sqrt(far[0] * far[0] + far[1] * far[1])
    slot = me + cuts * lax.broadcasted_iota(jnp.int32, (pair, n, n), 0)
    weight = (slot < live).astype(jnp.float32)
    factor = weight * (1.0 - amp[...] / jnp.maximum(magnitude, 1.0))
    back = both_sides((factor * far[0], factor * far[1]), tables, 3)
    for layer in range(cuts - 1, -1, -1):
        value = conj_mult(incident[layer], back)
        term[layer, :, 0] = value[0]
        term[layer, :, 1] = value[1]
        carry = conj_mult(patch_of(layer), back)
        if layer > 0:
            back = both_sides(carry, tables, 1)
    for part in range(2):
        probe_out[part] = jnp.sum(carry[part], axis=0)
    for away in range(cuts):
        terms[away][...] = term[lax.rem(me + away, cuts)]


def scatter_kernel(cuts, info, *rest):
    arrived, (inner, rim, canvas) = rest[:cuts], rest[cuts:]
    stripe, columns = inner.shape[1:]
    pair, _, n, _ = arrived[0].shape
    me = info[2, 1]
    canvas[...] = jnp.zeros_like(canvas)
    for away in range(cuts):
        source = lax.rem(me + cuts - away, cuts)
        for which in range(pair):
            at, down, right = spot(info, source + which * cuts, columns, n)
            for part in range(2):
                spread = placed(arrived[away][which, part], down, right)
                canvas[(part, *at)] = canvas[(part, *at)] + spread
    inner[...] = canvas[:, :stripe]
    rim[...] = canvas[:, stripe:]


def along(block, distance):
    devices = range(lax.axis_size("pos"))
    return lax.ppermute(block, "pos", [(i - distance, i) for i in devices if i - distance in devices])


def around(block, distance):
    count = lax.axis_size("cuts")
    return lax.ppermute(block, "cuts", [(i, (i + distance) % count) for i in range(count)])


def sum_over_pos(block):
    count = lax.axis_size("pos")
    step = 1
    while step < count:
        block = block + lax.ppermute(block, "pos", [(i, i ^ step) for i in range(count)])
        step *= 2
    return block


def local(specimen, probe, amplitude, offsets, live):
    n = probe.shape[1]
    stripe, columns = specimen.shape[2:]
    slots = amplitude.shape[0]
    across = lax.axis_size("pos")
    cuts = lax.axis_size("cuts")
    pair = slots // cuts
    me = lax.axis_index("cuts")
    own = specimen[:, 0]
    following = along(own, -1)
    row = offsets[0] - lax.axis_index("pos") * stripe
    extra = jnp.zeros((slots,), jnp.int32).at[0].set(live[0]).at[1].set(me)
    info = jnp.stack([row, offsets[1], extra])
    smem = pl.BlockSpec(memory_space=pltpu.SMEM)
    vmem = pl.BlockSpec(memory_space=pltpu.VMEM)
    hbm = pl.BlockSpec(memory_space=pl.ANY)
    tables = jnp.asarray(table_stack(n))

    light, light_rim = pl.pallas_call(
        light_kernel,
        out_shape=[jax.ShapeDtypeStruct((stripe, columns), jnp.float32)] * 2,
        in_specs=[smem, vmem],
        out_specs=[vmem] * 2,
        scratch_shapes=[pltpu.VMEM((stripe + n, columns), jnp.float32)],
        compiler_params=VMEM,
        name="light",
    )(info, probe)
    light_in = along(light_rim, 1)

    packet = jax.ShapeDtypeStruct((pair, 2, n, n), jnp.float32)
    windows = pl.pallas_call(
        window_kernel,
        out_shape=[packet] * cuts,
        in_specs=[smem, vmem, vmem],
        out_specs=[vmem] * cuts,
        scratch_shapes=[pltpu.VMEM((2, 2 * stripe, columns), jnp.float32)],
        compiler_params=VMEM,
        name="windows",
    )(info, own, following)
    arrived = [windows[0]] + [around(windows[away], away) for away in range(1, cuts)]

    *terms, probe_term = pl.pallas_call(
        functools.partial(wave_kernel, cuts),
        out_shape=[packet] * cuts + [jax.ShapeDtypeStruct((2, n, n), jnp.float32)],
        in_specs=[smem, vmem, hbm, vmem] + [vmem] * cuts,
        out_specs=[vmem] * (cuts + 1),
        scratch_shapes=[
            pltpu.VMEM((cuts, pair, 2, n, n), jnp.float32),
            pltpu.VMEM((cuts, pair, 2, n, n), jnp.float32),
            pltpu.VMEM((pair, n, n), jnp.float32),
            pltpu.SemaphoreType.DMA((pair,)),
        ],
        compiler_params=VMEM,
        name="waves",
    )(info, probe, amplitude, tables, *arrived)
    gathered = [terms[0]] + [around(terms[away], away) for away in range(1, cuts)]

    rows = n // cuts
    probe_part = lax.dynamic_slice_in_dim(probe_term, me * rows, rows, 1)
    for away in range(1, cuts):
        theirs = lax.dynamic_slice_in_dim(probe_term, (me + away) % cuts * rows, rows, 1)
        probe_part = probe_part + around(theirs, away)
    probe_grad = sum_over_pos(probe_part) / math.sqrt(slots * across)

    inner, rim = pl.pallas_call(
        functools.partial(scatter_kernel, cuts),
        out_shape=[jax.ShapeDtypeStruct((2, stripe, columns), jnp.float32)] * 2,
        in_specs=[smem] + [vmem] * cuts,
        out_specs=[vmem] * 2,
        scratch_shapes=[pltpu.VMEM((2, stripe + n, columns), jnp.float32)],
        compiler_params=VMEM,
        name="scatter",
    )(info, *gathered)
    rim_in = along(rim, 1)
    slice_grad = ((inner + rim_in) / (light + light_in + 1.0))[:, None]
    return slice_grad, probe_grad


def solution(mesh):
    in_specs = (P(None, "cuts", "pos", None), P(), P("pos", None, None), P(None, "pos"), P("pos"))
    out_specs = (P(None, "cuts", "pos", None), P(None, "cuts", None))
    return jax.shard_map(local, mesh=mesh, in_specs=in_specs, out_specs=out_specs, check_vma=False)
```

```python
import math

import jax
import jax.numpy as jnp
import numpy as np
from jax import lax
from jax.experimental import pallas as pl
from jax.experimental.pallas import tpu as pltpu
from jax.sharding import Mesh
from jax.sharding import PartitionSpec as P

FRESNEL = 0.7
POS = ("z", "y", "core")
VMEM = pltpu.CompilerParams(vmem_limit_bytes=48 * 1024 * 1024)


def make_tables(n):
    index = np.arange(n)
    four = np.exp(-2j * math.pi / n * (index[:, None] * index[None, :] % n)) / math.sqrt(n)
    signed = np.where(index < n // 2, index, index - n)
    spacing = (index[:, None] - index[None, :]) % n
    turns = spacing[:, :, None] * index[None, None, :] % n
    phase = FRESNEL * math.pi / n * (signed * signed)
    prop = np.mean(np.exp(1j * (phase[None, None, :] + 2.0 * math.pi / n * turns)), axis=2)
    return four, prop


def split_pair(table):
    whole = np.block([[table.real, table.imag], [-table.imag, table.real]]).astype(np.float32)
    lead = whole.astype(jnp.bfloat16)
    return np.stack([lead, (whole - lead.astype(np.float32)).astype(jnp.bfloat16)])


def table_stack(n):
    four, prop = make_tables(n)
    return np.stack([split_pair(prop), split_pair(prop.conj()), split_pair(four), split_pair(four.conj())])


def parts(x):
    lead = x.astype(jnp.bfloat16)
    return lead, (x - lead.astype(jnp.float32)).astype(jnp.bfloat16)


def dot(a, b):
    return jnp.dot(a, b, preferred_element_type=jnp.float32)


def both_sides(wave, tables, which):
    real, imag = wave
    count, n, _ = real.shape
    whole = jnp.concatenate([real.reshape(count * n, n), imag.reshape(count * n, n)], axis=1)
    lead, trail = parts(whole)
    right_lead, right_trail = tables[which, 0], tables[which, 1]
    mid = dot(lead, right_lead) + (dot(trail, right_lead) + dot(lead, right_trail))
    mid = jnp.concatenate(
        [
            jnp.concatenate([mid[p * n : (p + 1) * n, h * n : (h + 1) * n] for p in range(count)], axis=1)
            for h in range(2)
        ],
        axis=0,
    )
    lead, trail = parts(mid)
    left_lead, left_trail = tables[which ^ 1, 0], tables[which ^ 1, 1]
    out = dot(left_lead, lead) + (dot(left_lead, trail) + dot(left_trail, lead))
    real = jnp.stack([out[:n, p * n : (p + 1) * n] for p in range(count)])
    imag = jnp.stack([out[n:, p * n : (p + 1) * n] for p in range(count)])
    return real, imag


def complex_mult(a, b):
    return a[0] * b[0] - a[1] * b[1], a[0] * b[1] + a[1] * b[0]


def conj_mult(a, b):
    return a[0] * b[0] + a[1] * b[1], a[0] * b[1] - a[1] * b[0]


def spot(info, slot, columns, n):
    row = info[0, slot]
    col = info[1, slot]
    top = pl.multiple_of(row // 8 * 8, 8)
    band = pl.multiple_of(jnp.minimum(col // n * n, columns - 2 * n), n)
    return (pl.ds(top, n + 8), pl.ds(band, 2 * n)), row - top, col - band


def cut_out(box, down, right):
    n = box.shape[1] // 2
    turn = lax.rem(n - right, n)
    lane = lax.broadcasted_iota(jnp.int32, (n + 8, n), 1)
    wide = jnp.where(lane < n - right, pltpu.roll(box[:, :n], turn, axis=1), pltpu.roll(box[:, n:], turn, axis=1))
    groups = pltpu.roll(wide.reshape(n // 8 + 1, 8, n), lax.rem(8 - down, 8), axis=1)
    line = lax.broadcasted_iota(jnp.int32, (n // 8, 8, n), 1)
    return jnp.where(line < 8 - down, groups[:-1], groups[1:]).reshape(n, n)


def placed(value, down, right):
    n = value.shape[0]
    groups = pltpu.roll(value.reshape(n // 8, 8, n), down, axis=1)
    empty = jnp.zeros((1, 8, n), jnp.float32)
    line = lax.broadcasted_iota(jnp.int32, (n // 8 + 1, 8, n), 1)
    tall = jnp.where(
        line >= down, jnp.concatenate([groups, empty], axis=0), jnp.concatenate([empty, groups], axis=0)
    ).reshape(n + 8, n)
    tall = pltpu.roll(tall, lax.rem(right, n), axis=1)
    lane = lax.broadcasted_iota(jnp.int32, (n + 8, n), 1)
    return jnp.concatenate([jnp.where(lane >= right, tall, 0.0), jnp.where(lane < right, tall, 0.0)], axis=1)


def light_kernel(info, probe, own, inner, rim, copied, canvas, sem):
    copy = pltpu.make_async_copy(own, copied, sem)
    copy.start()
    n = probe.shape[1]
    stripe, columns = inner.shape
    canvas[...] = jnp.zeros_like(canvas)
    power = probe[0] * probe[0] + probe[1] * probe[1]

    def one(slot, carry):
        at, down, right = spot(info, slot, columns, n)
        canvas[at] = canvas[at] + placed(power, down, right)
        return carry

    lax.fori_loop(0, jnp.minimum(info[2, 0], info.shape[1]), one, 0)
    inner[...] = canvas[:stripe]
    rim[...] = canvas[stripe:]
    copy.wait()


def window_kernel(info, own, following, out, ext):
    cuts, pair, _, n, _ = out.shape
    stripe, columns = own.shape[1:]
    ext[:, :stripe] = own[...]
    ext[:, stripe:] = following[...]
    for target in range(cuts):
        for which in range(pair):
            at, down, right = spot(info, target + which * cuts, columns, n)
            for part in range(2):
                out[target, which, part] = cut_out(ext[(part, *at)], down, right)


def wave_kernel(info, probe, amplitude, tables, patch, terms, probe_out, amp, sems):
    cuts, pair, _, n, _ = patch.shape
    me = info[2, 1]
    live = info[2, 0]
    copies = [
        pltpu.make_async_copy(amplitude.at[me + which * cuts], amp.at[which], sems.at[which]) for which in range(pair)
    ]
    for copy in copies:
        copy.start()

    def patch_of(layer):
        return patch[layer, :, 0], patch[layer, :, 1]

    wave = tuple(jnp.broadcast_to(probe[part][None], (pair, n, n)) for part in range(2))
    incident = []
    for layer in range(cuts):
        incident.append(wave)
        wave = complex_mult(wave, patch_of(layer))
        if layer < cuts - 1:
            wave = both_sides(wave, tables, 0)
    far = both_sides(wave, tables, 2)
    for copy in copies:
        copy.wait()
    magnitude = jnp.sqrt(far[0] * far[0] + far[1] * far[1])
    slot = me + cuts * lax.broadcasted_iota(jnp.int32, (pair, n, n), 0)
    weight = (slot < live).astype(jnp.float32)
    factor = weight * (1.0 - amp[...] / jnp.maximum(magnitude, 1.0))
    back = both_sides((factor * far[0], factor * far[1]), tables, 3)
    for layer in range(cuts - 1, -1, -1):
        value = conj_mult(incident[layer], back)
        terms[layer, :, 0] = value[0]
        terms[layer, :, 1] = value[1]
        carry = conj_mult(patch_of(layer), back)
        if layer > 0:
            back = both_sides(carry, tables, 1)
    rows = n // cuts
    for part in range(2):
        total = jnp.sum(carry[part], axis=0)
        for piece in range(probe_out.shape[0]):
            at = piece % cuts * rows
            probe_out[piece, part * rows : (part + 1) * rows] = total[at : at + rows]


def scatter_kernel(info, arrived, light_rim, inner, rim, canvas):
    cuts, pair, _, n, _ = arrived.shape
    stripe, columns = inner.shape[1:]
    canvas[...] = jnp.zeros_like(canvas)
    for source in range(cuts):
        for which in range(pair):
            at, down, right = spot(info, source + which * cuts, columns, n)
            for part in range(2):
                spread = placed(arrived[source, which, part], down, right)
                canvas[(part, *at)] = canvas[(part, *at)] + spread
    inner[...] = canvas[:, :stripe]
    rim[:2] = canvas[:, stripe:]
    rim[2] = light_rim[...]


def along(block, distance):
    devices = range(lax.axis_size(POS))
    return lax.ppermute(block, POS, [(i - distance, i) for i in devices if i - distance in devices])


def swap(block, axes):
    return lax.all_to_all(block, axes, 0, 0)


def sum_over_grid(block, axes):
    count = lax.axis_size(axes)
    rows, columns = block.shape
    part = jnp.sum(swap(block.reshape(count, rows // count, columns), axes), axis=0)
    return swap(jnp.broadcast_to(part[None], (count, *part.shape)), axes).reshape(rows, columns)


def local(specimen, probe, amplitude, offsets, live):
    n = probe.shape[1]
    stripe, columns = specimen.shape[2:]
    slots = amplitude.shape[0]
    across = lax.axis_size(POS)
    cuts = lax.axis_size("cuts")
    pair = slots // cuts
    me = lax.axis_index("cuts")
    own = specimen[:, 0]
    following = along(own, -1)
    row = offsets[0] - lax.axis_index(POS) * stripe
    extra = jnp.zeros((slots,), jnp.int32).at[0].set(live[0]).at[1].set(me)
    info = jnp.stack([row, offsets[1], extra])
    smem = pl.BlockSpec(memory_space=pltpu.SMEM)
    vmem = pl.BlockSpec(memory_space=pltpu.VMEM)
    hbm = pl.BlockSpec(memory_space=pltpu.HBM)
    tables = jnp.asarray(table_stack(n))
    stripe_shape = jax.ShapeDtypeStruct((2, stripe, columns), jnp.float32)
    plane_shape = jax.ShapeDtypeStruct((stripe, columns), jnp.float32)
    packet = jax.ShapeDtypeStruct((cuts, pair, 2, n, n), jnp.float32)

    light, light_rim, own = pl.pallas_call(
        light_kernel,
        out_shape=[plane_shape, plane_shape, stripe_shape],
        in_specs=[smem, vmem, hbm],
        out_specs=[vmem] * 3,
        scratch_shapes=[pltpu.VMEM((stripe + n, columns), jnp.float32), pltpu.SemaphoreType.DMA],
        compiler_params=VMEM,
        name="light",
    )(info, probe, own)

    windows = pl.pallas_call(
        window_kernel,
        out_shape=packet,
        in_specs=[smem, vmem, vmem],
        out_specs=vmem,
        scratch_shapes=[pltpu.VMEM((2, 2 * stripe, columns), jnp.float32)],
        compiler_params=VMEM,
        name="windows",
    )(info, own, following)
    patches = swap(windows, "cuts")

    shares = 2 * cuts
    terms, probe_parts = pl.pallas_call(
        wave_kernel,
        out_shape=[packet, jax.ShapeDtypeStruct((shares, 2 * n // cuts, n), jnp.float32)],
        in_specs=[smem, vmem, hbm, vmem, vmem],
        out_specs=[vmem] * 2,
        scratch_shapes=[pltpu.VMEM((pair, n, n), jnp.float32), pltpu.SemaphoreType.DMA((pair,))],
        compiler_params=VMEM,
        name="waves",
    )(info, probe, amplitude, tables, patches)
    probe_part = jnp.sum(swap(probe_parts, ("core", "cuts")), axis=0)
    gathered = swap(terms, "cuts")

    inner, rim = pl.pallas_call(
        scatter_kernel,
        out_shape=[stripe_shape, jax.ShapeDtypeStruct((3, stripe, columns), jnp.float32)],
        in_specs=[smem, vmem, vmem],
        out_specs=[vmem] * 2,
        scratch_shapes=[pltpu.VMEM((2, stripe + n, columns), jnp.float32)],
        compiler_params=VMEM,
        name="scatter",
    )(info, gathered, light_rim)
    rim_in = along(rim, 1)
    slice_grad = ((inner + rim_in[:2]) / (light + rim_in[2] + 1.0))[:, None]
    probe_grad = sum_over_grid(probe_part, ("z", "y")).reshape(2, n // cuts, n) / math.sqrt(slots * across)
    return slice_grad, probe_grad


def solution(mesh):
    across, cuts = mesh.devices.shape
    y = min(8, across // 2)
    split = Mesh(mesh.devices.reshape(across // 2 // y, y, 2, cuts), ("z", "y", "core", "cuts"))
    in_specs = (P(None, "cuts", POS, None), P(), P(POS, None, None), P(None, POS), P(POS))
    out_specs = (P(None, "cuts", POS, None), P(None, "cuts", None))
    return jax.shard_map(local, mesh=split, in_specs=in_specs, out_specs=out_specs, check_vma=False)
```

```python
import math

import jax
import jax.numpy as jnp
import numpy as np
from jax import lax
from jax.experimental import pallas as pl
from jax.experimental.pallas import tpu as pltpu
from jax.sharding import Mesh
from jax.sharding import PartitionSpec as P

FRESNEL = 0.7
POS = ("z", "y", "core")
VMEM = pltpu.CompilerParams(vmem_limit_bytes=48 * 1024 * 1024)


def make_tables(n):
    index = np.arange(n)
    four = np.exp(-2j * math.pi / n * (index[:, None] * index[None, :] % n)) / math.sqrt(n)
    signed = np.where(index < n // 2, index, index - n)
    spacing = (index[:, None] - index[None, :]) % n
    turns = spacing[:, :, None] * index[None, None, :] % n
    phase = FRESNEL * math.pi / n * (signed * signed)
    prop = np.mean(np.exp(1j * (phase[None, None, :] + 2.0 * math.pi / n * turns)), axis=2)
    return four, prop


def split_pair(table):
    whole = np.block([[table.real, table.imag], [-table.imag, table.real]]).astype(np.float32)
    lead = whole.astype(jnp.bfloat16)
    return np.stack([lead, (whole - lead.astype(np.float32)).astype(jnp.bfloat16)])


def table_stack(n):
    four, prop = make_tables(n)
    return np.stack([split_pair(prop), split_pair(prop.conj()), split_pair(four), split_pair(four.conj())])


def parts(x):
    lead = x.astype(jnp.bfloat16)
    return lead, (x - lead.astype(jnp.float32)).astype(jnp.bfloat16)


def dot(a, b):
    return jnp.dot(a, b, preferred_element_type=jnp.float32)


def both_sides(wave, tables, which):
    real, imag = wave
    count, n, _ = real.shape
    whole = jnp.concatenate([real.reshape(count * n, n), imag.reshape(count * n, n)], axis=1)
    lead, trail = parts(whole)
    right_lead, right_trail = tables[which, 0], tables[which, 1]
    mid = dot(lead, right_lead) + (dot(trail, right_lead) + dot(lead, right_trail))
    mid = jnp.concatenate(
        [
            jnp.concatenate([mid[p * n : (p + 1) * n, h * n : (h + 1) * n] for p in range(count)], axis=1)
            for h in range(2)
        ],
        axis=0,
    )
    lead, trail = parts(mid)
    left_lead, left_trail = tables[which ^ 1, 0], tables[which ^ 1, 1]
    out = dot(left_lead, lead) + (dot(left_lead, trail) + dot(left_trail, lead))
    real = jnp.stack([out[:n, p * n : (p + 1) * n] for p in range(count)])
    imag = jnp.stack([out[n:, p * n : (p + 1) * n] for p in range(count)])
    return real, imag


def complex_mult(a, b):
    return a[0] * b[0] - a[1] * b[1], a[0] * b[1] + a[1] * b[0]


def conj_mult(a, b):
    return a[0] * b[0] + a[1] * b[1], a[0] * b[1] - a[1] * b[0]


def spot(info, slot, columns, n):
    row = info[0, slot]
    col = info[1, slot]
    top = pl.multiple_of(row // 8 * 8, 8)
    band = pl.multiple_of(jnp.minimum(col // n * n, columns - 2 * n), n)
    return (pl.ds(top, n + 8), pl.ds(band, 2 * n)), row - top, col - band


def cut_out(box, down, right):
    n = box.shape[1] // 2
    turn = lax.rem(n - right, n)
    lane = lax.broadcasted_iota(jnp.int32, (n + 8, n), 1)
    wide = jnp.where(lane < n - right, pltpu.roll(box[:, :n], turn, axis=1), pltpu.roll(box[:, n:], turn, axis=1))
    groups = pltpu.roll(wide.reshape(n // 8 + 1, 8, n), lax.rem(8 - down, 8), axis=1)
    line = lax.broadcasted_iota(jnp.int32, (n // 8, 8, n), 1)
    return jnp.where(line < 8 - down, groups[:-1], groups[1:]).reshape(n, n)


def placed(value, down, right):
    n = value.shape[0]
    groups = pltpu.roll(value.reshape(n // 8, 8, n), down, axis=1)
    empty = jnp.zeros((1, 8, n), jnp.float32)
    line = lax.broadcasted_iota(jnp.int32, (n // 8 + 1, 8, n), 1)
    tall = jnp.where(
        line >= down, jnp.concatenate([groups, empty], axis=0), jnp.concatenate([empty, groups], axis=0)
    ).reshape(n + 8, n)
    tall = pltpu.roll(tall, lax.rem(right, n), axis=1)
    lane = lax.broadcasted_iota(jnp.int32, (n + 8, n), 1)
    return jnp.concatenate([jnp.where(lane >= right, tall, 0.0), jnp.where(lane < right, tall, 0.0)], axis=1)


def light_kernel(info, probe, own, inner, rim, copied, canvas, sem):
    copy = pltpu.make_async_copy(own, copied, sem)
    copy.start()
    n = probe.shape[1]
    stripe, columns = inner.shape
    canvas[...] = jnp.zeros_like(canvas)
    power = probe[0] * probe[0] + probe[1] * probe[1]

    def one(slot, carry):
        at, down, right = spot(info, slot, columns, n)
        canvas[at] = canvas[at] + placed(power, down, right)
        return carry

    lax.fori_loop(0, jnp.minimum(info[2, 0], info.shape[1]), one, 0)
    inner[...] = canvas[:stripe]
    rim[...] = canvas[stripe:]
    copy.wait()


def window_kernel(info, own, following, out, ext):
    cuts, pair, _, n, _ = out.shape
    stripe, columns = own.shape[1:]
    ext[:, :stripe] = own[...]
    ext[:, stripe:] = following[...]
    for target in range(cuts):
        for which in range(pair):
            at, down, right = spot(info, target + which * cuts, columns, n)
            for part in range(2):
                out[target, which, part] = cut_out(ext[(part, *at)], down, right)


def wave_kernel(info, probe, amplitude, tables, patch, *rest):
    cuts, pair, _, n, _ = patch.shape
    sent, (probe_out, terms, amp, sems) = rest[:cuts], rest[cuts:]
    me = info[2, 1]
    live = info[2, 0]
    copies = [
        pltpu.make_async_copy(amplitude.at[me + which * cuts], amp.at[which], sems.at[which]) for which in range(pair)
    ]
    for copy in copies:
        copy.start()

    def patch_of(layer):
        return patch[layer, :, 0], patch[layer, :, 1]

    wave = tuple(jnp.broadcast_to(probe[part][None], (pair, n, n)) for part in range(2))
    incident = []
    for layer in range(cuts):
        incident.append(wave)
        wave = complex_mult(wave, patch_of(layer))
        if layer < cuts - 1:
            wave = both_sides(wave, tables, 0)
    far = both_sides(wave, tables, 2)
    for copy in copies:
        copy.wait()
    magnitude = jnp.sqrt(far[0] * far[0] + far[1] * far[1])
    slot = me + cuts * lax.broadcasted_iota(jnp.int32, (pair, n, n), 0)
    weight = (slot < live).astype(jnp.float32)
    factor = weight * (1.0 - amp[...] / jnp.maximum(magnitude, 1.0))
    back = both_sides((factor * far[0], factor * far[1]), tables, 3)
    for layer in range(cuts - 1, -1, -1):
        value = conj_mult(incident[layer], back)
        terms[layer, :, 0] = value[0]
        terms[layer, :, 1] = value[1]
        carry = conj_mult(patch_of(layer), back)
        if layer > 0:
            back = both_sides(carry, tables, 1)
    for away in range(cuts):
        sent[away][...] = terms[lax.rem(me + away, cuts)]
    rows = n // cuts
    for part in range(2):
        total = jnp.sum(carry[part], axis=0)
        for piece in range(probe_out.shape[0]):
            at = piece % cuts * rows
            probe_out[piece, part * rows : (part + 1) * rows] = total[at : at + rows]


def scatter_kernel(info, light_rim, *rest):
    arrived, (inner, rim, canvas) = rest[:-3], rest[-3:]
    cuts = len(arrived)
    pair, _, n, _ = arrived[0].shape
    stripe, columns = inner.shape[1:]
    me = info[2, 1]
    canvas[...] = jnp.zeros_like(canvas)
    for away in range(cuts):
        source = lax.rem(me + cuts - away, cuts)
        for which in range(pair):
            at, down, right = spot(info, source + which * cuts, columns, n)
            for part in range(2):
                spread = placed(arrived[away][which, part], down, right)
                canvas[(part, *at)] = canvas[(part, *at)] + spread
    inner[...] = canvas[:, :stripe]
    rim[:2] = canvas[:, stripe:]
    rim[2] = light_rim[...]


def along(block, distance):
    devices = range(lax.axis_size(POS))
    return lax.ppermute(block, POS, [(i - distance, i) for i in devices if i - distance in devices])


def around(block, distance):
    count = lax.axis_size("cuts")
    return lax.ppermute(block, "cuts", [(i, (i + distance) % count) for i in range(count)])


def swap(block, axes):
    return lax.all_to_all(block, axes, 0, 0)


def summed_rows(block, axes):
    count = lax.axis_size(axes)
    rows, columns = block.shape
    return jnp.sum(swap(block.reshape(count, rows // count, columns), axes), axis=0)


def all_rows(part, axes):
    count = lax.axis_size(axes)
    return swap(jnp.broadcast_to(part[None], (count, *part.shape)), axes)


def after(block, *first):
    return lax.optimization_barrier((block, *first))[0]


def local(specimen, probe, amplitude, offsets, live):
    n = probe.shape[1]
    stripe, columns = specimen.shape[2:]
    slots = amplitude.shape[0]
    across = lax.axis_size(POS)
    cuts = lax.axis_size("cuts")
    pair = slots // cuts
    me = lax.axis_index("cuts")
    own = specimen[:, 0]
    following = along(own, -1)
    row = offsets[0] - lax.axis_index(POS) * stripe
    extra = jnp.zeros((slots,), jnp.int32).at[0].set(live[0]).at[1].set(me)
    info = jnp.stack([row, offsets[1], extra])
    smem = pl.BlockSpec(memory_space=pltpu.SMEM)
    vmem = pl.BlockSpec(memory_space=pltpu.VMEM)
    hbm = pl.BlockSpec(memory_space=pltpu.HBM)
    tables = jnp.asarray(table_stack(n))
    stripe_shape = jax.ShapeDtypeStruct((2, stripe, columns), jnp.float32)
    plane_shape = jax.ShapeDtypeStruct((stripe, columns), jnp.float32)
    packet = jax.ShapeDtypeStruct((cuts, pair, 2, n, n), jnp.float32)

    light, light_rim, own = pl.pallas_call(
        light_kernel,
        out_shape=[plane_shape, plane_shape, stripe_shape],
        in_specs=[smem, vmem, hbm],
        out_specs=[vmem] * 3,
        scratch_shapes=[pltpu.VMEM((stripe + n, columns), jnp.float32), pltpu.SemaphoreType.DMA],
        compiler_params=VMEM,
        name="light",
    )(info, probe, own)

    windows = pl.pallas_call(
        window_kernel,
        out_shape=packet,
        in_specs=[smem, vmem, vmem],
        out_specs=vmem,
        scratch_shapes=[pltpu.VMEM((2, 2 * stripe, columns), jnp.float32)],
        compiler_params=VMEM,
        name="windows",
    )(info, own, following)
    patches = swap(windows, "cuts")

    shares = 2 * cuts
    packet = jax.ShapeDtypeStruct((pair, 2, n, n), jnp.float32)
    *terms, probe_parts = pl.pallas_call(
        wave_kernel,
        out_shape=[packet] * cuts + [jax.ShapeDtypeStruct((shares, 2 * n // cuts, n), jnp.float32)],
        in_specs=[smem, vmem, hbm, vmem, vmem],
        out_specs=[vmem] * (cuts + 1),
        scratch_shapes=[
            pltpu.VMEM((cuts, pair, 2, n, n), jnp.float32),
            pltpu.VMEM((pair, n, n), jnp.float32),
            pltpu.SemaphoreType.DMA((pair,)),
        ],
        compiler_params=VMEM,
        name="waves",
    )(info, probe, amplitude, tables, patches)
    probe_part = jnp.sum(swap(probe_parts, ("core", "cuts")), axis=0)
    terms = lax.optimization_barrier((*terms, probe_part))[:cuts]
    gathered = [terms[0]] + [around(terms[away], away) for away in range(1, cuts)]

    probe_rows = summed_rows(probe_part, ("z", "y"))

    inner, rim = pl.pallas_call(
        scatter_kernel,
        out_shape=[stripe_shape, jax.ShapeDtypeStruct((3, stripe, columns), jnp.float32)],
        in_specs=[smem] + [vmem] * (cuts + 1),
        out_specs=[vmem] * 2,
        scratch_shapes=[pltpu.VMEM((2, stripe + n, columns), jnp.float32)],
        compiler_params=VMEM,
        name="scatter",
    )(after(info, probe_rows), light_rim, *gathered)
    rim_in = along(rim, 1)
    slice_grad = ((inner + rim_in[:2]) / (light + rim_in[2] + 1.0))[:, None]
    probe_grad = all_rows(after(probe_rows, rim), ("z", "y")).reshape(2, n // cuts, n) / math.sqrt(slots * across)
    return slice_grad, probe_grad


def solution(mesh):
    across, cuts = mesh.devices.shape
    y = min(8, across // 2)
    split = Mesh(mesh.devices.reshape(across // 2 // y, y, 2, cuts), ("z", "y", "core", "cuts"))
    in_specs = (P(None, "cuts", POS, None), P(), P(POS, None, None), P(None, POS), P(POS))
    out_specs = (P(None, "cuts", POS, None), P(None, "cuts", None))
    return jax.shard_map(local, mesh=split, in_specs=in_specs, out_specs=out_specs, check_vma=False)
```

```python
import functools
import math

import jax
import jax.numpy as jnp
import numpy as np
from jax import lax
from jax.experimental import pallas as pl
from jax.experimental.pallas import tpu as pltpu
from jax.sharding import Mesh
from jax.sharding import PartitionSpec as P

FRESNEL = 0.7
POS = ("z", "y", "core")
VMEM = pltpu.CompilerParams(vmem_limit_bytes=16 * 1024 * 1024)


def make_tables(n):
    index = np.arange(n)
    four = np.exp(-2j * math.pi / n * (index[:, None] * index[None, :] % n)) / math.sqrt(n)
    signed = np.where(index < n // 2, index, index - n)
    spacing = (index[:, None] - index[None, :]) % n
    turns = spacing[:, :, None] * index[None, None, :] % n
    phase = FRESNEL * math.pi / n * (signed * signed)
    prop = np.mean(np.exp(1j * (phase[None, None, :] + 2.0 * math.pi / n * turns)), axis=2)
    return four, prop


def split_pair(table):
    whole = np.block([[table.real, table.imag], [-table.imag, table.real]]).astype(np.float32)
    lead = whole.astype(jnp.bfloat16)
    return np.stack([lead, (whole - lead.astype(np.float32)).astype(jnp.bfloat16)])


def table_stack(n):
    four, prop = make_tables(n)
    return np.stack([split_pair(prop), split_pair(prop.conj()), split_pair(four), split_pair(four.conj())])


def parts(x):
    lead = x.astype(jnp.bfloat16)
    return lead, (x - lead.astype(jnp.float32)).astype(jnp.bfloat16)


def dot(a, b):
    return jnp.dot(a, b, preferred_element_type=jnp.float32)


def both_sides(wave, tables, which):
    real, imag = wave
    n = real.shape[1]
    right_lead, right_trail = tables[which, 0], tables[which, 1]
    left_lead, left_trail = tables[which ^ 1, 0], tables[which ^ 1, 1]
    halves = []
    for p in range(real.shape[0]):
        lead, trail = parts(jnp.concatenate([real[p], imag[p]], axis=1))
        mid = dot(lead, right_lead) + (dot(trail, right_lead) + dot(lead, right_trail))
        halves.append(parts(jnp.concatenate([mid[:, :n], mid[:, n:]], axis=0)))
    outs = []
    for lead, trail in halves:
        both = dot(left_lead, jnp.concatenate([lead, trail], axis=1))
        outs.append(both[:, :n] + (both[:, n:] + dot(left_trail, lead)))
    return jnp.stack([out[:n] for out in outs]), jnp.stack([out[n:] for out in outs])


def complex_mult(a, b):
    return a[0] * b[0] - a[1] * b[1], a[0] * b[1] + a[1] * b[0]


def conj_mult(a, b):
    return a[0] * b[0] + a[1] * b[1], a[0] * b[1] - a[1] * b[0]


def spot(info, slot, columns, n):
    row = info[0, slot]
    col = info[1, slot]
    top = pl.multiple_of(row // 8 * 8, 8)
    band = pl.multiple_of(jnp.minimum(col // n * n, columns - 2 * n), n)
    return (pl.ds(top, n + 8), pl.ds(band, 2 * n)), row - top, col - band


def cut_out(box, down, right):
    n = box.shape[1] // 2
    turn = lax.rem(n - right, n)
    lane = lax.broadcasted_iota(jnp.int32, (n + 8, n), 1)
    wide = jnp.where(lane < n - right, pltpu.roll(box[:, :n], turn, axis=1), pltpu.roll(box[:, n:], turn, axis=1))
    groups = pltpu.roll(wide.reshape(n // 8 + 1, 8, n), lax.rem(8 - down, 8), axis=1)
    line = lax.broadcasted_iota(jnp.int32, (n // 8, 8, n), 1)
    return jnp.where(line < 8 - down, groups[:-1], groups[1:]).reshape(n, n)


def placed(value, down, right):
    n = value.shape[0]
    groups = pltpu.roll(value.reshape(n // 8, 8, n), down, axis=1)
    empty = jnp.zeros((1, 8, n), jnp.float32)
    line = lax.broadcasted_iota(jnp.int32, (n // 8 + 1, 8, n), 1)
    tall = jnp.where(
        line >= down, jnp.concatenate([groups, empty], axis=0), jnp.concatenate([empty, groups], axis=0)
    ).reshape(n + 8, n)
    tall = pltpu.roll(tall, lax.rem(right, n), axis=1)
    lane = lax.broadcasted_iota(jnp.int32, (n + 8, n), 1)
    return jnp.concatenate([jnp.where(lane >= right, tall, 0.0), jnp.where(lane < right, tall, 0.0)], axis=1)


def stage_kernel(own, probe, own_copy, probe_copy):
    own_copy[...] = own[...]
    probe_copy[...] = probe[...]


def light_kernel(info, former, probe, light, canvas):
    n = probe.shape[1]
    stripe, columns = light.shape
    power = probe[0] * probe[0] + probe[1] * probe[1]

    def fill(source):
        canvas[...] = jnp.zeros_like(canvas)

        def one(slot, carry):
            at, down, right = spot(source, slot, columns, n)
            canvas[at] = canvas[at] + placed(power, down, right)
            return carry

        lax.fori_loop(0, jnp.minimum(source[2, 0], source.shape[1]), one, 0)

    fill(former)
    light[...] = canvas[stripe:]
    fill(info)
    light[...] += canvas[:stripe]


def window_kernel(info, own, following, out, ext):
    cuts, pair, _, n, _ = out.shape
    stripe, columns = own.shape[1:]
    ext[:, :stripe] = own[...]
    ext[:, stripe:] = following[...]
    for target in range(cuts):
        for which in range(pair):
            at, down, right = spot(info, target + which * cuts, columns, n)
            for part in range(2):
                out[target, which, part] = cut_out(ext[(part, *at)], down, right)


def wave_kernel(scale, info, probe, amplitude, tables, patch, *rest):
    cuts, pair, _, n, _ = patch.shape
    sent, (probe_out, terms, amp, sems) = rest[:cuts], rest[cuts:]
    me = info[2, 1]
    live = info[2, 0]
    copies = [
        pltpu.make_async_copy(amplitude.at[me + which * cuts], amp.at[which], sems.at[which]) for which in range(pair)
    ]
    for copy in copies:
        copy.start()

    def patch_of(layer):
        return patch[layer, :, 0], patch[layer, :, 1]

    wave = tuple(jnp.broadcast_to(probe[part][None], (pair, n, n)) for part in range(2))
    incident = []
    for layer in range(cuts):
        incident.append(wave)
        wave = complex_mult(wave, patch_of(layer))
        if layer < cuts - 1:
            wave = both_sides(wave, tables, 0)
    far = both_sides(wave, tables, 2)
    for copy in copies:
        copy.wait()
    magnitude = jnp.sqrt(far[0] * far[0] + far[1] * far[1])
    slot = me + cuts * lax.broadcasted_iota(jnp.int32, (pair, n, n), 0)
    weight = (slot < live).astype(jnp.float32)
    factor = weight * (1.0 - amp[...] / jnp.maximum(magnitude, 1.0))
    back = both_sides((factor * far[0], factor * far[1]), tables, 3)
    for layer in range(cuts - 1, -1, -1):
        value = conj_mult(incident[layer], back)
        terms[layer, :, 0] = value[0]
        terms[layer, :, 1] = value[1]
        carry = conj_mult(patch_of(layer), back)
        if layer > 0:
            back = both_sides(carry, tables, 1)
    for away in range(cuts):
        sent[away][...] = terms[lax.rem(me + away, cuts)]
    rows = n // cuts
    share = probe_out.shape[1]
    total = [jnp.sum(carry[part], axis=0) * scale for part in range(2)]
    for cut in range(cuts):
        block = jnp.concatenate([total[part][cut * rows : (cut + 1) * rows] for part in range(2)], axis=0)
        for group in range(2 * rows // share):
            probe_out[group * cuts + cut] = block[group * share : (group + 1) * share]


def scatter_kernel(info, *rest):
    arrived, (inner, rim, canvas) = rest[:-3], rest[-3:]
    cuts = len(arrived)
    pair, _, n, _ = arrived[0].shape
    stripe, columns = inner.shape[1:]
    me = info[2, 1]
    canvas[...] = jnp.zeros_like(canvas)
    for away in range(cuts):
        source = lax.rem(me + cuts - away, cuts)
        for which in range(pair):
            at, down, right = spot(info, source + which * cuts, columns, n)
            for part in range(2):
                spread = placed(arrived[away][which, part], down, right)
                canvas[(part, *at)] = canvas[(part, *at)] + spread
    inner[...] = canvas[:, :stripe]
    rim[...] = canvas[:, stripe:]


def final_kernel(inner, rim, light, rows, slice_grad, probe_grad):
    whole = light[...] + 1.0
    for part in range(2):
        slice_grad[part, 0] = (inner[part] + rim[part]) / whole
    probe_grad[...] = rows[...].reshape(probe_grad.shape)


def along(block, distance):
    devices = range(lax.axis_size(POS))
    return lax.ppermute(block, POS, [(i - distance, i) for i in devices if i - distance in devices])


def around(block, distance):
    count = lax.axis_size("cuts")
    return lax.ppermute(block, "cuts", [(i, (i + distance) % count) for i in range(count)])


def swap(block, axes):
    return lax.all_to_all(block, axes, 0, 0)


def copies(block, axes):
    return swap(jnp.broadcast_to(block[None], (lax.axis_size(axes), *block.shape)), axes)


def after(block, *first):
    return lax.optimization_barrier((block, *first))[0]


def local(specimen, probe, amplitude, offsets, live):
    n = probe.shape[1]
    stripe, columns = specimen.shape[2:]
    slots = amplitude.shape[0]
    across = lax.axis_size(POS)
    cuts = lax.axis_size("cuts")
    pair = slots // cuts
    me = lax.axis_index("cuts")
    own = specimen[:, 0]
    following = along(own, -1)
    row = offsets[0] - lax.axis_index(POS) * stripe
    extra = jnp.zeros((slots,), jnp.int32).at[0].set(live[0]).at[1].set(me)
    info = jnp.stack([row, offsets[1], extra])
    smem = pl.BlockSpec(memory_space=pltpu.SMEM)
    vmem = pl.BlockSpec(memory_space=pltpu.VMEM)
    hbm = pl.BlockSpec(memory_space=pltpu.HBM)
    tables = jnp.asarray(table_stack(n))
    stripe_shape = jax.ShapeDtypeStruct((2, stripe, columns), jnp.float32)
    plane_shape = jax.ShapeDtypeStruct((stripe, columns), jnp.float32)
    packet = jax.ShapeDtypeStruct((cuts, pair, 2, n, n), jnp.float32)

    own, probe = pl.pallas_call(
        stage_kernel,
        out_shape=[stripe_shape, jax.ShapeDtypeStruct(probe.shape, jnp.float32)],
        in_specs=[vmem] * 2,
        out_specs=[vmem] * 2,
        compiler_params=VMEM,
        name="stage",
    )(own, probe)
    light = pl.pallas_call(
        light_kernel,
        out_shape=plane_shape,
        in_specs=[smem, smem, vmem],
        out_specs=vmem,
        scratch_shapes=[pltpu.VMEM((stripe + n, columns), jnp.float32)],
        compiler_params=VMEM,
        name="light",
    )(info, along(info, 1), probe)

    windows = pl.pallas_call(
        window_kernel,
        out_shape=packet,
        in_specs=[smem, vmem, vmem],
        out_specs=vmem,
        scratch_shapes=[pltpu.VMEM((2, 2 * stripe, columns), jnp.float32)],
        compiler_params=VMEM,
        name="windows",
    )(after(info, light), own, following)
    patches = swap(windows, "cuts")

    shares = lax.axis_size(("z", "cuts"))
    packet = jax.ShapeDtypeStruct((pair, 2, n, n), jnp.float32)
    *terms, probe_parts = pl.pallas_call(
        functools.partial(wave_kernel, 1.0 / math.sqrt(slots * across)),
        out_shape=[packet] * cuts + [jax.ShapeDtypeStruct((shares, 2 * n // shares, n), jnp.float32)],
        in_specs=[smem, vmem, hbm, vmem, vmem],
        out_specs=[vmem] * (cuts + 1),
        scratch_shapes=[
            pltpu.VMEM((cuts, pair, 2, n, n), jnp.float32),
            pltpu.VMEM((pair, n, n), jnp.float32),
            pltpu.SemaphoreType.DMA((pair,)),
        ],
        compiler_params=VMEM,
        name="waves",
    )(info, probe, amplitude, tables, patches)
    probe_rows = jnp.sum(swap(probe_parts, ("z", "cuts")), axis=0)
    gathered = [terms[0]] + [around(terms[away], away) for away in range(1, cuts)]
    probe_rows = jnp.sum(copies(probe_rows, ("y", "core")), axis=0)

    inner, rim = pl.pallas_call(
        scatter_kernel,
        out_shape=[stripe_shape] * 2,
        in_specs=[smem] + [vmem] * cuts,
        out_specs=[vmem] * 2,
        scratch_shapes=[pltpu.VMEM((2, stripe + n, columns), jnp.float32)],
        compiler_params=VMEM,
        name="scatter",
    )(after(info, probe_rows), *gathered)
    rim_in = along(rim, 1)
    probe_rows = copies(after(probe_rows, rim), "z")
    slice_grad, probe_grad = pl.pallas_call(
        final_kernel,
        out_shape=[
            jax.ShapeDtypeStruct((2, 1, stripe, columns), jnp.float32),
            jax.ShapeDtypeStruct((2, n // cuts, n), jnp.float32),
        ],
        in_specs=[vmem] * 4,
        out_specs=[vmem] * 2,
        compiler_params=VMEM,
        name="final",
    )(inner, rim_in, light, probe_rows)
    return slice_grad, probe_grad


def solution(mesh):
    across, cuts = mesh.devices.shape
    y = min(8, across // 2)
    split = Mesh(mesh.devices.reshape(across // 2 // y, y, 2, cuts), ("z", "y", "core", "cuts"))
    in_specs = (P(None, "cuts", POS, None), P(), P(POS, None, None), P(None, POS), P(POS))
    out_specs = (P(None, "cuts", POS, None), P(None, "cuts", None))
    return jax.shard_map(local, mesh=split, in_specs=in_specs, out_specs=out_specs, check_vma=False)
```

```python
import functools
import math

import jax
import jax.numpy as jnp
import numpy as np
from jax import lax
from jax.experimental import pallas as pl
from jax.experimental.pallas import tpu as pltpu
from jax.sharding import Mesh
from jax.sharding import PartitionSpec as P

FRESNEL = 0.7
POS = ("z", "y", "core")
VMEM = pltpu.CompilerParams(vmem_limit_bytes=16 * 1024 * 1024)


def make_tables(n):
    index = np.arange(n)
    four = np.exp(-2j * math.pi / n * (index[:, None] * index[None, :] % n)) / math.sqrt(n)
    signed = np.where(index < n // 2, index, index - n)
    spacing = (index[:, None] - index[None, :]) % n
    turns = spacing[:, :, None] * index[None, None, :] % n
    phase = FRESNEL * math.pi / n * (signed * signed)
    prop = np.mean(np.exp(1j * (phase[None, None, :] + 2.0 * math.pi / n * turns)), axis=2)
    return four, prop


def split_pair(table):
    whole = np.block([[table.real, table.imag], [-table.imag, table.real]]).astype(np.float32)
    lead = whole.astype(jnp.bfloat16)
    return np.stack([lead, (whole - lead.astype(np.float32)).astype(jnp.bfloat16)])


def table_stack(n):
    four, prop = make_tables(n)
    return np.stack([split_pair(prop), split_pair(prop.conj()), split_pair(four), split_pair(four.conj())])


def parts(x):
    lead = x.astype(jnp.bfloat16)
    return lead, (x - lead.astype(jnp.float32)).astype(jnp.bfloat16)


def dot(a, b):
    return jnp.dot(a, b, preferred_element_type=jnp.float32)


def both_sides(wave, tables, which):
    real, imag = wave
    n = real.shape[1]
    right_lead, right_trail = tables[which, 0], tables[which, 1]
    left_lead, left_trail = tables[which ^ 1, 0], tables[which ^ 1, 1]
    halves = []
    for p in range(real.shape[0]):
        lead, trail = parts(jnp.concatenate([real[p], imag[p]], axis=1))
        mid = dot(lead, right_lead) + (dot(trail, right_lead) + dot(lead, right_trail))
        halves.append(parts(jnp.concatenate([mid[:, :n], mid[:, n:]], axis=0)))
    outs = []
    for lead, trail in halves:
        both = dot(left_lead, jnp.concatenate([lead, trail], axis=1))
        outs.append(both[:, :n] + (both[:, n:] + dot(left_trail, lead)))
    return jnp.stack([out[:n] for out in outs]), jnp.stack([out[n:] for out in outs])


def complex_mult(a, b):
    return a[0] * b[0] - a[1] * b[1], a[0] * b[1] + a[1] * b[0]


def conj_mult(a, b):
    return a[0] * b[0] + a[1] * b[1], a[0] * b[1] - a[1] * b[0]


def spot(info, slot, columns, n):
    row = info[0, slot]
    col = info[1, slot]
    top = pl.multiple_of(row // 8 * 8, 8)
    band = pl.multiple_of(jnp.minimum(col // n * n, columns - 2 * n), n)
    return (pl.ds(top, n + 8), pl.ds(band, 2 * n)), row - top, col - band


def cut_out(box, down, right):
    n = box.shape[1] // 2
    turn = lax.rem(n - right, n)
    lane = lax.broadcasted_iota(jnp.int32, (n + 8, n), 1)
    wide = jnp.where(lane < n - right, pltpu.roll(box[:, :n], turn, axis=1), pltpu.roll(box[:, n:], turn, axis=1))
    groups = pltpu.roll(wide.reshape(n // 8 + 1, 8, n), lax.rem(8 - down, 8), axis=1)
    line = lax.broadcasted_iota(jnp.int32, (n // 8, 8, n), 1)
    return jnp.where(line < 8 - down, groups[:-1], groups[1:]).reshape(n, n)


def placed(value, down, right):
    n = value.shape[0]
    groups = pltpu.roll(value.reshape(n // 8, 8, n), down, axis=1)
    empty = jnp.zeros((1, 8, n), jnp.float32)
    line = lax.broadcasted_iota(jnp.int32, (n // 8 + 1, 8, n), 1)
    tall = jnp.where(
        line >= down, jnp.concatenate([groups, empty], axis=0), jnp.concatenate([empty, groups], axis=0)
    ).reshape(n + 8, n)
    tall = pltpu.roll(tall, lax.rem(right, n), axis=1)
    lane = lax.broadcasted_iota(jnp.int32, (n + 8, n), 1)
    return jnp.concatenate([jnp.where(lane >= right, tall, 0.0), jnp.where(lane < right, tall, 0.0)], axis=1)


def stage_kernel(own, probe, own_copy, probe_copy):
    own_copy[...] = own[...]
    probe_copy[...] = probe[...]


def light_kernel(info, former, probe, light, canvas):
    n = probe.shape[1]
    stripe, columns = light.shape
    power = probe[0] * probe[0] + probe[1] * probe[1]

    def fill(source):
        canvas[...] = jnp.zeros_like(canvas)

        def one(slot, carry):
            at, down, right = spot(source, slot, columns, n)
            canvas[at] = canvas[at] + placed(power, down, right)
            return carry

        lax.fori_loop(0, jnp.minimum(source[2, 0], source.shape[1]), one, 0)

    fill(former)
    light[...] = canvas[stripe:]
    fill(info)
    light[...] += canvas[:stripe]


def window_kernel(info, own, following, out, ext):
    cuts, pair, _, n, _ = out.shape
    stripe, columns = own.shape[1:]
    ext[:, :stripe] = own[...]
    ext[:, stripe:] = following[...]
    for target in range(cuts):
        for which in range(pair):
            at, down, right = spot(info, target + which * cuts, columns, n)
            for part in range(2):
                out[target, which, part] = cut_out(ext[(part, *at)], down, right)


def wave_kernel(scale, info, probe, amplitude, tables, patch, *rest):
    cuts, pair, _, n, _ = patch.shape
    sent, (probe_out, terms, amp, sems) = rest[:cuts], rest[cuts:]
    me = info[2, 1]
    live = info[2, 0]
    copies = [
        pltpu.make_async_copy(amplitude.at[me + which * cuts], amp.at[which], sems.at[which]) for which in range(pair)
    ]
    for copy in copies:
        copy.start()

    def patch_of(layer):
        return patch[layer, :, 0], patch[layer, :, 1]

    wave = tuple(jnp.broadcast_to(probe[part][None], (pair, n, n)) for part in range(2))
    incident = []
    for layer in range(cuts):
        incident.append(wave)
        wave = complex_mult(wave, patch_of(layer))
        if layer < cuts - 1:
            wave = both_sides(wave, tables, 0)
    far = both_sides(wave, tables, 2)
    for copy in copies:
        copy.wait()
    magnitude = jnp.sqrt(far[0] * far[0] + far[1] * far[1])
    slot = me + cuts * lax.broadcasted_iota(jnp.int32, (pair, n, n), 0)
    weight = (slot < live).astype(jnp.float32)
    factor = weight * (1.0 - amp[...] / jnp.maximum(magnitude, 1.0))
    back = both_sides((factor * far[0], factor * far[1]), tables, 3)
    for layer in range(cuts - 1, -1, -1):
        value = conj_mult(incident[layer], back)
        terms[layer, :, 0] = value[0]
        terms[layer, :, 1] = value[1]
        carry = conj_mult(patch_of(layer), back)
        if layer > 0:
            back = both_sides(carry, tables, 1)
    for away in range(cuts):
        sent[away][...] = terms[lax.rem(me + away, cuts)]
    rows = n // cuts
    share = probe_out.shape[1]
    total = [jnp.sum(carry[part], axis=0) * scale for part in range(2)]
    for cut in range(cuts):
        block = jnp.concatenate([total[part][cut * rows : (cut + 1) * rows] for part in range(2)], axis=0)
        for group in range(2 * rows // share):
            probe_out[group * cuts + cut] = block[group * share : (group + 1) * share]


def scatter_kernel(info, *rest):
    arrived, (inner, rim, canvas) = rest[:-3], rest[-3:]
    cuts = len(arrived)
    pair, _, n, _ = arrived[0].shape
    stripe, columns = inner.shape[1:]
    me = info[2, 1]
    canvas[...] = jnp.zeros_like(canvas)
    for away in range(cuts):
        source = lax.rem(me + cuts - away, cuts)
        for which in range(pair):
            at, down, right = spot(info, source + which * cuts, columns, n)
            for part in range(2):
                spread = placed(arrived[away][which, part], down, right)
                canvas[(part, *at)] = canvas[(part, *at)] + spread
    inner[...] = canvas[:, :stripe]
    rim[...] = canvas[:, stripe:]


def final_kernel(inner, rim, light, rows, slice_grad, probe_grad):
    whole = light[...] + 1.0
    for part in range(2):
        slice_grad[part, 0] = (inner[part] + rim[part]) / whole
    probe_grad[...] = rows[...].reshape(probe_grad.shape)


def along(block, distance):
    devices = range(lax.axis_size(POS))
    return lax.ppermute(block, POS, [(i - distance, i) for i in devices if i - distance in devices])


def around(block, distance):
    count = lax.axis_size("cuts")
    return lax.ppermute(block, "cuts", [(i, (i + distance) % count) for i in range(count)])


def swap(block, axes):
    return lax.all_to_all(block, axes, 0, 0)


def copies(block, axes):
    return swap(jnp.broadcast_to(block[None], (lax.axis_size(axes), *block.shape)), axes)


def after(block, *first):
    return lax.optimization_barrier((block, *first))[0]


def local(specimen, probe, amplitude, offsets, live):
    n = probe.shape[1]
    stripe, columns = specimen.shape[2:]
    slots = amplitude.shape[0]
    across = lax.axis_size(POS)
    cuts = lax.axis_size("cuts")
    pair = slots // cuts
    me = lax.axis_index("cuts")
    own = specimen[:, 0]
    following = along(own, -1)
    row = offsets[0] - lax.axis_index(POS) * stripe
    extra = jnp.zeros((slots,), jnp.int32).at[0].set(live[0]).at[1].set(me)
    info = jnp.stack([row, offsets[1], extra])
    smem = pl.BlockSpec(memory_space=pltpu.SMEM)
    vmem = pl.BlockSpec(memory_space=pltpu.VMEM)
    hbm = pl.BlockSpec(memory_space=pltpu.HBM)
    tables = jnp.asarray(table_stack(n))
    stripe_shape = jax.ShapeDtypeStruct((2, stripe, columns), jnp.float32)
    plane_shape = jax.ShapeDtypeStruct((stripe, columns), jnp.float32)
    packet = jax.ShapeDtypeStruct((cuts, pair, 2, n, n), jnp.float32)

    former = along(info, 1)
    own, probe = pl.pallas_call(
        stage_kernel,
        out_shape=[stripe_shape, jax.ShapeDtypeStruct(probe.shape, jnp.float32)],
        in_specs=[vmem] * 2,
        out_specs=[vmem] * 2,
        compiler_params=VMEM,
        name="stage",
    )(own, probe)
    windows = pl.pallas_call(
        window_kernel,
        out_shape=packet,
        in_specs=[smem, vmem, vmem],
        out_specs=vmem,
        scratch_shapes=[pltpu.VMEM((2, 2 * stripe, columns), jnp.float32)],
        compiler_params=VMEM,
        name="windows",
    )(info, own, following)
    patches = swap(windows, "cuts")

    shares = lax.axis_size(("z", "cuts"))
    packet = jax.ShapeDtypeStruct((pair, 2, n, n), jnp.float32)
    *terms, probe_parts = pl.pallas_call(
        functools.partial(wave_kernel, 1.0 / math.sqrt(slots * across)),
        out_shape=[packet] * cuts + [jax.ShapeDtypeStruct((shares, 2 * n // shares, n), jnp.float32)],
        in_specs=[smem, vmem, hbm, vmem, vmem],
        out_specs=[vmem] * (cuts + 1),
        scratch_shapes=[
            pltpu.VMEM((cuts, pair, 2, n, n), jnp.float32),
            pltpu.VMEM((pair, n, n), jnp.float32),
            pltpu.SemaphoreType.DMA((pair,)),
        ],
        compiler_params=VMEM,
        name="waves",
    )(info, probe, amplitude, tables, patches)
    probe_rows = jnp.sum(swap(probe_parts, ("z", "cuts")), axis=0)
    later = after(info, probe_rows)
    light = pl.pallas_call(
        light_kernel,
        out_shape=plane_shape,
        in_specs=[smem, smem, vmem],
        out_specs=vmem,
        scratch_shapes=[pltpu.VMEM((stripe + n, columns), jnp.float32)],
        compiler_params=VMEM,
        name="light",
    )(later, former, probe)
    gathered = [terms[0]] + [around(terms[away], away) for away in range(1, cuts)]
    probe_rows = jnp.sum(copies(probe_rows, ("y", "core")), axis=0)

    inner, rim = pl.pallas_call(
        scatter_kernel,
        out_shape=[stripe_shape] * 2,
        in_specs=[smem] + [vmem] * cuts,
        out_specs=[vmem] * 2,
        scratch_shapes=[pltpu.VMEM((2, stripe + n, columns), jnp.float32)],
        compiler_params=VMEM,
        name="scatter",
    )(after(info, probe_rows, light), *gathered)
    rim_in = along(rim, 1)
    probe_rows = copies(after(probe_rows, rim), "z")
    slice_grad, probe_grad = pl.pallas_call(
        final_kernel,
        out_shape=[
            jax.ShapeDtypeStruct((2, 1, stripe, columns), jnp.float32),
            jax.ShapeDtypeStruct((2, n // cuts, n), jnp.float32),
        ],
        in_specs=[vmem] * 4,
        out_specs=[vmem] * 2,
        compiler_params=VMEM,
        name="final",
    )(inner, rim_in, light, probe_rows)
    return slice_grad, probe_grad


def solution(mesh):
    across, cuts = mesh.devices.shape
    y = min(8, across // 2)
    split = Mesh(mesh.devices.reshape(across // 2 // y, y, 2, cuts), ("z", "y", "core", "cuts"))
    in_specs = (P(None, "cuts", POS, None), P(), P(POS, None, None), P(None, POS), P(POS))
    out_specs = (P(None, "cuts", POS, None), P(None, "cuts", None))
    return jax.shard_map(local, mesh=split, in_specs=in_specs, out_specs=out_specs, check_vma=False)
```

```python
import functools
import math

import jax
import jax.numpy as jnp
import numpy as np
from jax import lax
from jax.experimental import pallas as pl
from jax.experimental.pallas import tpu as pltpu
from jax.sharding import Mesh
from jax.sharding import PartitionSpec as P

FRESNEL = 0.7
POS = ("z", "y", "core")
VMEM = pltpu.CompilerParams(vmem_limit_bytes=16 * 1024 * 1024)


def make_tables(n):
    index = np.arange(n)
    four = np.exp(-2j * math.pi / n * (index[:, None] * index[None, :] % n)) / math.sqrt(n)
    signed = np.where(index < n // 2, index, index - n)
    spacing = (index[:, None] - index[None, :]) % n
    turns = spacing[:, :, None] * index[None, None, :] % n
    phase = FRESNEL * math.pi / n * (signed * signed)
    prop = np.mean(np.exp(1j * (phase[None, None, :] + 2.0 * math.pi / n * turns)), axis=2)
    return four, prop


def split_pair(table):
    whole = np.block([[table.real, table.imag], [-table.imag, table.real]]).astype(np.float32)
    lead = whole.astype(jnp.bfloat16)
    return np.stack([lead, (whole - lead.astype(np.float32)).astype(jnp.bfloat16)])


def table_stack(n):
    four, prop = make_tables(n)
    return np.stack([split_pair(prop), split_pair(prop.conj()), split_pair(four), split_pair(four.conj())])


def parts(x):
    lead = x.astype(jnp.bfloat16)
    return lead, (x - lead.astype(jnp.float32)).astype(jnp.bfloat16)


def dot(a, b):
    return jnp.dot(a, b, preferred_element_type=jnp.float32)


def both_sides(wave, tables, which):
    real, imag = wave
    n = real.shape[1]
    right_lead, right_trail = tables[which, 0], tables[which, 1]
    left_lead, left_trail = tables[which ^ 1, 0], tables[which ^ 1, 1]
    halves = []
    for p in range(real.shape[0]):
        lead, trail = parts(jnp.concatenate([real[p], imag[p]], axis=1))
        mid = dot(lead, right_lead) + (dot(trail, right_lead) + dot(lead, right_trail))
        halves.append(parts(jnp.concatenate([mid[:, :n], mid[:, n:]], axis=0)))
    outs = []
    for lead, trail in halves:
        both = dot(left_lead, jnp.concatenate([lead, trail], axis=1))
        outs.append(both[:, :n] + (both[:, n:] + dot(left_trail, lead)))
    return jnp.stack([out[:n] for out in outs]), jnp.stack([out[n:] for out in outs])


def complex_mult(a, b):
    return a[0] * b[0] - a[1] * b[1], a[0] * b[1] + a[1] * b[0]


def conj_mult(a, b):
    return a[0] * b[0] + a[1] * b[1], a[0] * b[1] - a[1] * b[0]


def spot(info, slot, columns, n):
    row = info[0, slot]
    col = info[1, slot]
    top = pl.multiple_of(row // 8 * 8, 8)
    band = pl.multiple_of(jnp.minimum(col // n * n, columns - 2 * n), n)
    return (pl.ds(top, n + 8), pl.ds(band, 2 * n)), row - top, col - band


def cut_out(box, down, right):
    n = box.shape[1] // 2
    turn = lax.rem(n - right, n)
    lane = lax.broadcasted_iota(jnp.int32, (n + 8, n), 1)
    wide = jnp.where(lane < n - right, pltpu.roll(box[:, :n], turn, axis=1), pltpu.roll(box[:, n:], turn, axis=1))
    groups = pltpu.roll(wide.reshape(n // 8 + 1, 8, n), lax.rem(8 - down, 8), axis=1)
    line = lax.broadcasted_iota(jnp.int32, (n // 8, 8, n), 1)
    return jnp.where(line < 8 - down, groups[:-1], groups[1:]).reshape(n, n)


def placed(value, down, right):
    n = value.shape[0]
    groups = pltpu.roll(value.reshape(n // 8, 8, n), down, axis=1)
    empty = jnp.zeros((1, 8, n), jnp.float32)
    line = lax.broadcasted_iota(jnp.int32, (n // 8 + 1, 8, n), 1)
    tall = jnp.where(
        line >= down, jnp.concatenate([groups, empty], axis=0), jnp.concatenate([empty, groups], axis=0)
    ).reshape(n + 8, n)
    tall = pltpu.roll(tall, lax.rem(right, n), axis=1)
    lane = lax.broadcasted_iota(jnp.int32, (n + 8, n), 1)
    return jnp.concatenate([jnp.where(lane >= right, tall, 0.0), jnp.where(lane < right, tall, 0.0)], axis=1)


def stage_kernel(own, probe, own_copy, probe_copy):
    own_copy[...] = own[...]
    probe_copy[...] = probe[...]


def light_kernel(info, former, probe, light, canvas):
    n = probe.shape[1]
    stripe, columns = light.shape
    power = probe[0] * probe[0] + probe[1] * probe[1]

    def fill(source):
        canvas[...] = jnp.zeros_like(canvas)

        def one(slot, carry):
            at, down, right = spot(source, slot, columns, n)
            canvas[at] = canvas[at] + placed(power, down, right)
            return carry

        lax.fori_loop(0, jnp.minimum(source[2, 0], source.shape[1]), one, 0)

    fill(former)
    light[...] = canvas[stripe:]
    fill(info)
    light[...] += canvas[:stripe]


def window_kernel(info, own, following, out, ext):
    cuts, pair, _, n, _ = out.shape
    stripe, columns = own.shape[1:]
    ext[:, :stripe] = own[...]
    ext[:, stripe:] = following[...]
    for target in range(cuts):
        for which in range(pair):
            at, down, right = spot(info, target + which * cuts, columns, n)
            for part in range(2):
                out[target, which, part] = cut_out(ext[(part, *at)], down, right)


def wave_kernel(scale, info, probe, amplitude, tables, patch, *rest):
    cuts, pair, _, n, _ = patch.shape
    sent, (probe_out, terms, amp, sems) = rest[:cuts], rest[cuts:]
    me = info[2, 1]
    live = info[2, 0]
    copies = [
        pltpu.make_async_copy(amplitude.at[me + which * cuts], amp.at[which], sems.at[which]) for which in range(pair)
    ]
    for copy in copies:
        copy.start()

    def patch_of(layer):
        return patch[layer, :, 0], patch[layer, :, 1]

    wave = tuple(jnp.broadcast_to(probe[part][None], (pair, n, n)) for part in range(2))
    incident = []
    for layer in range(cuts):
        incident.append(wave)
        wave = complex_mult(wave, patch_of(layer))
        if layer < cuts - 1:
            wave = both_sides(wave, tables, 0)
    far = both_sides(wave, tables, 2)
    for copy in copies:
        copy.wait()
    magnitude = jnp.sqrt(far[0] * far[0] + far[1] * far[1])
    slot = me + cuts * lax.broadcasted_iota(jnp.int32, (pair, n, n), 0)
    weight = (slot < live).astype(jnp.float32)
    factor = weight * (1.0 - amp[...] / jnp.maximum(magnitude, 1.0))
    back = both_sides((factor * far[0], factor * far[1]), tables, 3)
    for layer in range(cuts - 1, -1, -1):
        value = conj_mult(incident[layer], back)
        terms[layer, :, 0] = value[0]
        terms[layer, :, 1] = value[1]
        carry = conj_mult(patch_of(layer), back)
        if layer > 0:
            back = both_sides(carry, tables, 1)
    for away in range(cuts):
        sent[away][...] = terms[lax.rem(me + away, cuts)]
    rows = n // cuts
    share = probe_out.shape[1]
    total = [jnp.sum(carry[part], axis=0) * scale for part in range(2)]
    for cut in range(cuts):
        block = jnp.concatenate([total[part][cut * rows : (cut + 1) * rows] for part in range(2)], axis=0)
        for group in range(2 * rows // share):
            probe_out[group * cuts + cut] = block[group * share : (group + 1) * share]


def scatter_kernel(info, *rest):
    arrived, (inner, rim, canvas) = rest[:-3], rest[-3:]
    cuts = len(arrived)
    pair, _, n, _ = arrived[0].shape
    stripe, columns = inner.shape[1:]
    me = info[2, 1]
    canvas[...] = jnp.zeros_like(canvas)
    for away in range(cuts):
        source = lax.rem(me + cuts - away, cuts)
        for which in range(pair):
            at, down, right = spot(info, source + which * cuts, columns, n)
            for part in range(2):
                spread = placed(arrived[away][which, part], down, right)
                canvas[(part, *at)] = canvas[(part, *at)] + spread
    inner[...] = canvas[:, :stripe]
    rim[...] = canvas[:, stripe:]


def total_kernel(rows, out):
    out[...] = jnp.broadcast_to(jnp.sum(rows[...], axis=0)[None], out.shape)


def final_kernel(inner, rim, light, rows, slice_grad, probe_grad):
    whole = light[...] + 1.0
    for part in range(2):
        slice_grad[part, 0] = (inner[part] + rim[part]) / whole
    probe_grad[...] = rows[...].reshape(probe_grad.shape)


def along(block, distance):
    devices = range(lax.axis_size(POS))
    return lax.ppermute(block, POS, [(i - distance, i) for i in devices if i - distance in devices])


def around(block, distance):
    count = lax.axis_size("cuts")
    return lax.ppermute(block, "cuts", [(i, (i + distance) % count) for i in range(count)])


def swap(block, axes):
    return lax.all_to_all(block, axes, 0, 0)


def copies(block, axes):
    return swap(jnp.broadcast_to(block[None], (lax.axis_size(axes), *block.shape)), axes)


def after(block, *first):
    return lax.optimization_barrier((block, *first))[0]


def local(specimen, probe, amplitude, offsets, live):
    n = probe.shape[1]
    stripe, columns = specimen.shape[2:]
    slots = amplitude.shape[0]
    across = lax.axis_size(POS)
    cuts = lax.axis_size("cuts")
    pair = slots // cuts
    me = lax.axis_index("cuts")
    own = specimen[:, 0]
    following = along(own, -1)
    row = offsets[0] - lax.axis_index(POS) * stripe
    extra = jnp.zeros((slots,), jnp.int32).at[0].set(live[0]).at[1].set(me)
    info = jnp.stack([row, offsets[1], extra])
    smem = pl.BlockSpec(memory_space=pltpu.SMEM)
    vmem = pl.BlockSpec(memory_space=pltpu.VMEM)
    hbm = pl.BlockSpec(memory_space=pltpu.HBM)
    tables = jnp.asarray(table_stack(n))
    stripe_shape = jax.ShapeDtypeStruct((2, stripe, columns), jnp.float32)
    plane_shape = jax.ShapeDtypeStruct((stripe, columns), jnp.float32)
    packet = jax.ShapeDtypeStruct((cuts, pair, 2, n, n), jnp.float32)

    former = along(info, 1)
    own, probe = pl.pallas_call(
        stage_kernel,
        out_shape=[stripe_shape, jax.ShapeDtypeStruct(probe.shape, jnp.float32)],
        in_specs=[vmem] * 2,
        out_specs=[vmem] * 2,
        compiler_params=VMEM,
        name="stage",
    )(own, probe)
    windows = pl.pallas_call(
        window_kernel,
        out_shape=packet,
        in_specs=[smem, vmem, vmem],
        out_specs=vmem,
        scratch_shapes=[pltpu.VMEM((2, 2 * stripe, columns), jnp.float32)],
        compiler_params=VMEM,
        name="windows",
    )(after(info, former), own, following)
    patches = swap(windows, "cuts")

    shares = lax.axis_size(("z", "cuts"))
    packet = jax.ShapeDtypeStruct((pair, 2, n, n), jnp.float32)
    *terms, probe_parts = pl.pallas_call(
        functools.partial(wave_kernel, 1.0 / math.sqrt(slots * across)),
        out_shape=[packet] * cuts + [jax.ShapeDtypeStruct((shares, 2 * n // shares, n), jnp.float32)],
        in_specs=[smem, vmem, hbm, vmem, vmem],
        out_specs=[vmem] * (cuts + 1),
        scratch_shapes=[
            pltpu.VMEM((cuts, pair, 2, n, n), jnp.float32),
            pltpu.VMEM((pair, n, n), jnp.float32),
            pltpu.SemaphoreType.DMA((pair,)),
        ],
        compiler_params=VMEM,
        name="waves",
    )(info, probe, amplitude, tables, patches)
    probe_rows = jnp.sum(swap(probe_parts, ("z", "cuts")), axis=0)
    gathered = [terms[0]] + [around(terms[away], away) for away in range(1, cuts)]
    later = after(info, probe_rows)
    light = pl.pallas_call(
        light_kernel,
        out_shape=plane_shape,
        in_specs=[smem, smem, vmem],
        out_specs=vmem,
        scratch_shapes=[pltpu.VMEM((stripe + n, columns), jnp.float32)],
        compiler_params=VMEM,
        name="light",
    )(later, former, probe)
    layers = lax.axis_size("z")
    probe_rows = pl.pallas_call(
        total_kernel,
        out_shape=jax.ShapeDtypeStruct((layers, *probe_rows.shape), jnp.float32),
        in_specs=[vmem],
        out_specs=vmem,
        compiler_params=VMEM,
        cost_estimate=pl.CostEstimate(flops=10**11, bytes_accessed=10**8, transcendentals=0),
        name="total",
    )(after(copies(probe_rows, ("y", "core")), light))

    inner, rim = pl.pallas_call(
        scatter_kernel,
        out_shape=[stripe_shape] * 2,
        in_specs=[smem] + [vmem] * cuts,
        out_specs=[vmem] * 2,
        scratch_shapes=[pltpu.VMEM((2, stripe + n, columns), jnp.float32)],
        compiler_params=VMEM,
        name="scatter",
    )(later, *gathered)
    rim_in = along(rim, 1)
    probe_rows = swap(probe_rows, "z")
    slice_grad, probe_grad = pl.pallas_call(
        final_kernel,
        out_shape=[
            jax.ShapeDtypeStruct((2, 1, stripe, columns), jnp.float32),
            jax.ShapeDtypeStruct((2, n // cuts, n), jnp.float32),
        ],
        in_specs=[vmem] * 4,
        out_specs=[vmem] * 2,
        compiler_params=VMEM,
        name="final",
    )(inner, rim_in, light, probe_rows)
    return slice_grad, probe_grad


def solution(mesh):
    across, cuts = mesh.devices.shape
    y = min(8, across // 2)
    split = Mesh(mesh.devices.reshape(across // 2 // y, y, 2, cuts), ("z", "y", "core", "cuts"))
    in_specs = (P(None, "cuts", POS, None), P(), P(POS, None, None), P(None, POS), P(POS))
    out_specs = (P(None, "cuts", POS, None), P(None, "cuts", None))
    return jax.shard_map(local, mesh=split, in_specs=in_specs, out_specs=out_specs, check_vma=False)
```

```python
import functools
import math

import jax
import jax.numpy as jnp
import numpy as np
from jax import lax
from jax.experimental import pallas as pl
from jax.experimental.pallas import tpu as pltpu
from jax.sharding import Mesh
from jax.sharding import PartitionSpec as P

FRESNEL = 0.7
POS = ("z", "y", "core")
VMEM = pltpu.CompilerParams(vmem_limit_bytes=16 * 1024 * 1024)


def make_tables(n):
    index = np.arange(n)
    four = np.exp(-2j * math.pi / n * (index[:, None] * index[None, :] % n)) / math.sqrt(n)
    signed = np.where(index < n // 2, index, index - n)
    spacing = (index[:, None] - index[None, :]) % n
    turns = spacing[:, :, None] * index[None, None, :] % n
    phase = FRESNEL * math.pi / n * (signed * signed)
    prop = np.mean(np.exp(1j * (phase[None, None, :] + 2.0 * math.pi / n * turns)), axis=2)
    return four, prop


def split_pair(table):
    whole = np.block([[table.real, table.imag], [-table.imag, table.real]]).astype(np.float32)
    lead = whole.astype(jnp.bfloat16)
    return np.stack([lead, (whole - lead.astype(np.float32)).astype(jnp.bfloat16)])


def table_stack(n):
    four, prop = make_tables(n)
    return np.stack([split_pair(prop), split_pair(prop.conj()), split_pair(four), split_pair(four.conj())])


def parts(x):
    lead = x.astype(jnp.bfloat16)
    return lead, (x - lead.astype(jnp.float32)).astype(jnp.bfloat16)


def dot(a, b):
    return jnp.dot(a, b, preferred_element_type=jnp.float32)


def both_sides(wave, tables, which):
    real, imag = wave
    n = real.shape[1]
    right_lead, right_trail = tables[which, 0], tables[which, 1]
    left_lead, left_trail = tables[which ^ 1, 0], tables[which ^ 1, 1]
    halves = []
    for p in range(real.shape[0]):
        lead, trail = parts(jnp.concatenate([real[p], imag[p]], axis=1))
        mid = dot(lead, right_lead) + (dot(trail, right_lead) + dot(lead, right_trail))
        halves.append(parts(jnp.concatenate([mid[:, :n], mid[:, n:]], axis=0)))
    outs = []
    for lead, trail in halves:
        both = dot(left_lead, jnp.concatenate([lead, trail], axis=1))
        outs.append(both[:, :n] + (both[:, n:] + dot(left_trail, lead)))
    return jnp.stack([out[:n] for out in outs]), jnp.stack([out[n:] for out in outs])


def complex_mult(a, b):
    return a[0] * b[0] - a[1] * b[1], a[0] * b[1] + a[1] * b[0]


def conj_mult(a, b):
    return a[0] * b[0] + a[1] * b[1], a[0] * b[1] - a[1] * b[0]


def scalars(info):
    values = info[...]
    return [[values[line, slot] for slot in range(values.shape[1])] for line in range(values.shape[0])]


def choose(values, index):
    chosen = values[0]
    for position in range(1, len(values)):
        chosen = jnp.where(index == position, values[position], chosen)
    return chosen


def spot(row, col, columns, n):
    top = pl.multiple_of(row // 8 * 8, 8)
    band = pl.multiple_of(jnp.minimum(col // n * n, columns - 2 * n), n)
    return (pl.ds(top, n + 8), pl.ds(band, 2 * n)), row - top, col - band


def cut_out(box, down, right):
    n = box.shape[1] // 2
    turn = lax.rem(n - right, n)
    lane = lax.broadcasted_iota(jnp.int32, (n + 8, n), 1)
    wide = jnp.where(lane < n - right, pltpu.roll(box[:, :n], turn, axis=1), pltpu.roll(box[:, n:], turn, axis=1))
    groups = pltpu.roll(wide.reshape(n // 8 + 1, 8, n), lax.rem(8 - down, 8), axis=1)
    line = lax.broadcasted_iota(jnp.int32, (n // 8, 8, n), 1)
    return jnp.where(line < 8 - down, groups[:-1], groups[1:]).reshape(n, n)


def placed(value, down, right):
    n = value.shape[0]
    groups = pltpu.roll(value.reshape(n // 8, 8, n), down, axis=1)
    empty = jnp.zeros((1, 8, n), jnp.float32)
    line = lax.broadcasted_iota(jnp.int32, (n // 8 + 1, 8, n), 1)
    tall = jnp.where(
        line >= down, jnp.concatenate([groups, empty], axis=0), jnp.concatenate([empty, groups], axis=0)
    ).reshape(n + 8, n)
    tall = pltpu.roll(tall, lax.rem(right, n), axis=1)
    lane = lax.broadcasted_iota(jnp.int32, (n + 8, n), 1)
    return jnp.concatenate([jnp.where(lane >= right, tall, 0.0), jnp.where(lane < right, tall, 0.0)], axis=1)


def stage_kernel(own, probe, own_copy, probe_copy):
    own_copy[...] = own[...]
    probe_copy[...] = probe[...]


def light_kernel(info, former, probe, light, canvas):
    n = probe.shape[1]
    stripe, columns = light.shape
    power = probe[0] * probe[0] + probe[1] * probe[1]

    def fill(source):
        rows, cols, (live, *_) = scalars(source)
        canvas[...] = jnp.zeros_like(canvas)
        for slot in range(len(rows)):

            @pl.when(slot < live)
            def _():
                at, down, right = spot(rows[slot], cols[slot], columns, n)
                canvas[at] = canvas[at] + placed(power, down, right)

    fill(former)
    light[...] = canvas[stripe:]
    fill(info)
    light[...] += canvas[:stripe]


def window_kernel(info, own, following, out, ext):
    cuts, pair, _, n, _ = out.shape
    stripe, columns = own.shape[1:]
    rows, cols, _ = scalars(info)
    ext[:, :stripe] = own[...]
    ext[:, stripe:] = following[...]
    for target in range(cuts):
        for which in range(pair):
            slot = target + which * cuts
            at, down, right = spot(rows[slot], cols[slot], columns, n)
            for part in range(2):
                out[target, which, part] = cut_out(ext[(part, *at)], down, right)


def wave_kernel(scale, info, probe, amplitude, tables, patch, *rest):
    cuts, pair, _, n, _ = patch.shape
    sent, (probe_out, terms, amp, sems) = rest[:cuts], rest[cuts:]
    _, _, (live, me, *_) = scalars(info)
    copies = [
        pltpu.make_async_copy(amplitude.at[me + which * cuts], amp.at[which], sems.at[which]) for which in range(pair)
    ]
    for copy in copies:
        copy.start()

    def patch_of(layer):
        return patch[layer, :, 0], patch[layer, :, 1]

    wave = tuple(jnp.broadcast_to(probe[part][None], (pair, n, n)) for part in range(2))
    incident = []
    for layer in range(cuts):
        incident.append(wave)
        wave = complex_mult(wave, patch_of(layer))
        if layer < cuts - 1:
            wave = both_sides(wave, tables, 0)
    far = both_sides(wave, tables, 2)
    for copy in copies:
        copy.wait()
    magnitude = jnp.sqrt(far[0] * far[0] + far[1] * far[1])
    slot = me + cuts * lax.broadcasted_iota(jnp.int32, (pair, n, n), 0)
    weight = (slot < live).astype(jnp.float32)
    factor = weight * (1.0 - amp[...] / jnp.maximum(magnitude, 1.0))
    back = both_sides((factor * far[0], factor * far[1]), tables, 3)
    for layer in range(cuts - 1, -1, -1):
        value = conj_mult(incident[layer], back)
        terms[layer, :, 0] = value[0]
        terms[layer, :, 1] = value[1]
        carry = conj_mult(patch_of(layer), back)
        if layer > 0:
            back = both_sides(carry, tables, 1)
    for away in range(cuts):
        sent[away][...] = terms[lax.rem(me + away, cuts)]
    rows = n // cuts
    share = probe_out.shape[1]
    total = [jnp.sum(carry[part], axis=0) * scale for part in range(2)]
    for cut in range(cuts):
        block = jnp.concatenate([total[part][cut * rows : (cut + 1) * rows] for part in range(2)], axis=0)
        for group in range(2 * rows // share):
            probe_out[group * cuts + cut] = block[group * share : (group + 1) * share]


def scatter_kernel(info, *rest):
    arrived, (inner, rim, canvas) = rest[:-3], rest[-3:]
    cuts = len(arrived)
    pair, _, n, _ = arrived[0].shape
    stripe, columns = inner.shape[1:]
    rows, cols, (_, me, *_) = scalars(info)
    canvas[...] = jnp.zeros_like(canvas)
    for away in range(cuts):
        source = lax.rem(me + cuts - away, cuts)
        for which in range(pair):
            mine = slice(which * cuts, (which + 1) * cuts)
            at, down, right = spot(choose(rows[mine], source), choose(cols[mine], source), columns, n)
            for part in range(2):
                spread = placed(arrived[away][which, part], down, right)
                canvas[(part, *at)] = canvas[(part, *at)] + spread
    inner[...] = canvas[:, :stripe]
    rim[...] = canvas[:, stripe:]


def total_kernel(rows, out):
    out[...] = jnp.broadcast_to(jnp.sum(rows[...], axis=0)[None], out.shape)


def final_kernel(inner, rim, light, rows, slice_grad, probe_grad):
    whole = light[...] + 1.0
    for part in range(2):
        slice_grad[part, 0] = (inner[part] + rim[part]) / whole
    probe_grad[...] = rows[...].reshape(probe_grad.shape)


def along(block, distance):
    devices = range(lax.axis_size(POS))
    return lax.ppermute(block, POS, [(i - distance, i) for i in devices if i - distance in devices])


def around(block, distance):
    count = lax.axis_size("cuts")
    return lax.ppermute(block, "cuts", [(i, (i + distance) % count) for i in range(count)])


def swap(block, axes):
    return lax.all_to_all(block, axes, 0, 0)


def after(block, *first):
    return lax.optimization_barrier((block, *first))[0]


def local(specimen, probe, amplitude, offsets, live):
    n = probe.shape[1]
    stripe, columns = specimen.shape[2:]
    slots = amplitude.shape[0]
    across = lax.axis_size(POS)
    cuts = lax.axis_size("cuts")
    pair = slots // cuts
    me = lax.axis_index("cuts")
    own = specimen[:, 0]
    following = along(own, -1)
    row = offsets[0] - lax.axis_index(POS) * stripe
    extra = jnp.zeros((slots,), jnp.int32).at[0].set(live[0]).at[1].set(me)
    info = jnp.stack([row, offsets[1], extra])
    vmem = pl.BlockSpec(memory_space=pltpu.VMEM)
    hbm = pl.BlockSpec(memory_space=pltpu.HBM)
    tables = jnp.asarray(table_stack(n))
    stripe_shape = jax.ShapeDtypeStruct((2, stripe, columns), jnp.float32)
    plane_shape = jax.ShapeDtypeStruct((stripe, columns), jnp.float32)
    packet = jax.ShapeDtypeStruct((cuts, pair, 2, n, n), jnp.float32)

    former = along(info, 1)
    own, probe = pl.pallas_call(
        stage_kernel,
        out_shape=[stripe_shape, jax.ShapeDtypeStruct(probe.shape, jnp.float32)],
        in_specs=[vmem] * 2,
        out_specs=[vmem] * 2,
        compiler_params=VMEM,
        name="stage",
    )(own, probe)
    windows = pl.pallas_call(
        window_kernel,
        out_shape=packet,
        in_specs=[vmem] * 3,
        out_specs=vmem,
        scratch_shapes=[pltpu.VMEM((2, 2 * stripe, columns), jnp.float32)],
        compiler_params=VMEM,
        name="windows",
    )(after(info, former), own, following)
    patches = swap(windows, "cuts")

    shares = lax.axis_size(("z", "cuts"))
    packet = jax.ShapeDtypeStruct((pair, 2, n, n), jnp.float32)
    *terms, probe_parts = pl.pallas_call(
        functools.partial(wave_kernel, 1.0 / math.sqrt(slots * across)),
        out_shape=[packet] * cuts + [jax.ShapeDtypeStruct((shares, 2 * n // shares, n), jnp.float32)],
        in_specs=[vmem, vmem, hbm, vmem, vmem],
        out_specs=[vmem] * (cuts + 1),
        scratch_shapes=[
            pltpu.VMEM((cuts, pair, 2, n, n), jnp.float32),
            pltpu.VMEM((pair, n, n), jnp.float32),
            pltpu.SemaphoreType.DMA((pair,)),
        ],
        compiler_params=VMEM,
        name="waves",
    )(info, probe, amplitude, tables, patches)
    def total(rows, axes, **kwargs):
        return pl.pallas_call(
            total_kernel,
            out_shape=jax.ShapeDtypeStruct((lax.axis_size(axes), *rows.shape[1:]), jnp.float32),
            in_specs=[vmem],
            out_specs=vmem,
            compiler_params=VMEM,
            name="total",
            **kwargs,
        )(rows)

    probe_rows = total(swap(probe_parts, ("z", "cuts")), ("y", "core"))
    gathered = [terms[0]] + [around(terms[away], away) for away in range(1, cuts)]
    later = after(info, probe_rows)
    light = pl.pallas_call(
        light_kernel,
        out_shape=plane_shape,
        in_specs=[vmem] * 3,
        out_specs=vmem,
        scratch_shapes=[pltpu.VMEM((stripe + n, columns), jnp.float32)],
        compiler_params=VMEM,
        name="light",
    )(later, former, probe)
    estimate = pl.CostEstimate(flops=10**11, bytes_accessed=10**8, transcendentals=0)
    probe_rows = total(after(swap(probe_rows, ("y", "core")), light), "z", cost_estimate=estimate)

    inner, rim = pl.pallas_call(
        scatter_kernel,
        out_shape=[stripe_shape] * 2,
        in_specs=[vmem] * (cuts + 1),
        out_specs=[vmem] * 2,
        scratch_shapes=[pltpu.VMEM((2, stripe + n, columns), jnp.float32)],
        compiler_params=VMEM,
        name="scatter",
    )(later, *gathered)
    rim_in = along(rim, 1)
    probe_rows = swap(probe_rows, "z")
    slice_grad, probe_grad = pl.pallas_call(
        final_kernel,
        out_shape=[
            jax.ShapeDtypeStruct((2, 1, stripe, columns), jnp.float32),
            jax.ShapeDtypeStruct((2, n // cuts, n), jnp.float32),
        ],
        in_specs=[vmem] * 4,
        out_specs=[vmem] * 2,
        compiler_params=VMEM,
        name="final",
    )(inner, rim_in, light, probe_rows)
    return slice_grad, probe_grad


def solution(mesh):
    across, cuts = mesh.devices.shape
    y = min(8, across // 2)
    split = Mesh(mesh.devices.reshape(across // 2 // y, y, 2, cuts), ("z", "y", "core", "cuts"))
    in_specs = (P(None, "cuts", POS, None), P(), P(POS, None, None), P(None, POS), P(POS))
    out_specs = (P(None, "cuts", POS, None), P(None, "cuts", None))
    return jax.shard_map(local, mesh=split, in_specs=in_specs, out_specs=out_specs, check_vma=False)
```

```python
import functools
import math

import jax
import jax.numpy as jnp
import numpy as np
from jax import lax
from jax.experimental import pallas as pl
from jax.experimental.pallas import tpu as pltpu
from jax.sharding import Mesh
from jax.sharding import PartitionSpec as P

FRESNEL = 0.7
POS = ("z", "y", "core")
VMEM = pltpu.CompilerParams(vmem_limit_bytes=16 * 1024 * 1024)


def make_tables(n):
    index = np.arange(n)
    four = np.exp(-2j * math.pi / n * (index[:, None] * index[None, :] % n)) / math.sqrt(n)
    signed = np.where(index < n // 2, index, index - n)
    spacing = (index[:, None] - index[None, :]) % n
    turns = spacing[:, :, None] * index[None, None, :] % n
    phase = FRESNEL * math.pi / n * (signed * signed)
    prop = np.mean(np.exp(1j * (phase[None, None, :] + 2.0 * math.pi / n * turns)), axis=2)
    return four, prop


def split_pair(table):
    whole = np.block([[table.real, table.imag], [-table.imag, table.real]]).astype(np.float32)
    lead = whole.astype(jnp.bfloat16)
    return np.stack([lead, (whole - lead.astype(np.float32)).astype(jnp.bfloat16)])


def table_stack(n):
    four, prop = make_tables(n)
    return np.stack([split_pair(prop), split_pair(prop.conj()), split_pair(four), split_pair(four.conj())])


def parts(x):
    lead = x.astype(jnp.bfloat16)
    return lead, (x - lead.astype(jnp.float32)).astype(jnp.bfloat16)


def dot(a, b):
    return jnp.dot(a, b, preferred_element_type=jnp.float32)


def both_sides(wave, tables, which):
    real, imag = wave
    n = real.shape[1]
    right_lead, right_trail = tables[which, 0], tables[which, 1]
    left_lead, left_trail = tables[which ^ 1, 0], tables[which ^ 1, 1]
    halves = []
    for p in range(real.shape[0]):
        lead, trail = parts(jnp.concatenate([real[p], imag[p]], axis=1))
        mid = dot(lead, right_lead) + (dot(trail, right_lead) + dot(lead, right_trail))
        halves.append(parts(jnp.concatenate([mid[:, :n], mid[:, n:]], axis=0)))
    outs = []
    for lead, trail in halves:
        both = dot(left_lead, jnp.concatenate([lead, trail], axis=1))
        outs.append(both[:, :n] + (both[:, n:] + dot(left_trail, lead)))
    return jnp.stack([out[:n] for out in outs]), jnp.stack([out[n:] for out in outs])


def complex_mult(a, b):
    return a[0] * b[0] - a[1] * b[1], a[0] * b[1] + a[1] * b[0]


def conj_mult(a, b):
    return a[0] * b[0] + a[1] * b[1], a[0] * b[1] - a[1] * b[0]


def scalars(info):
    values = info[...]
    return [[values[line, slot] for slot in range(values.shape[1])] for line in range(values.shape[0])]


def choose(values, index):
    chosen = values[0]
    for position in range(1, len(values)):
        chosen = jnp.where(index == position, values[position], chosen)
    return chosen


def spot(row, col, columns, n):
    top = pl.multiple_of(row // 8 * 8, 8)
    band = pl.multiple_of(jnp.minimum(col // n * n, columns - 2 * n), n)
    return (pl.ds(top, n + 8), pl.ds(band, 2 * n)), row - top, col - band


def cut_out(box, down, right):
    n = box.shape[1] // 2
    turn = lax.rem(n - right, n)
    lane = lax.broadcasted_iota(jnp.int32, (n + 8, n), 1)
    wide = jnp.where(lane < n - right, pltpu.roll(box[:, :n], turn, axis=1), pltpu.roll(box[:, n:], turn, axis=1))
    groups = pltpu.roll(wide.reshape(n // 8 + 1, 8, n), lax.rem(8 - down, 8), axis=1)
    line = lax.broadcasted_iota(jnp.int32, (n // 8, 8, n), 1)
    return jnp.where(line < 8 - down, groups[:-1], groups[1:]).reshape(n, n)


def placed(value, down, right):
    n = value.shape[0]
    groups = pltpu.roll(value.reshape(n // 8, 8, n), down, axis=1)
    empty = jnp.zeros((1, 8, n), jnp.float32)
    line = lax.broadcasted_iota(jnp.int32, (n // 8 + 1, 8, n), 1)
    tall = jnp.where(
        line >= down, jnp.concatenate([groups, empty], axis=0), jnp.concatenate([empty, groups], axis=0)
    ).reshape(n + 8, n)
    tall = pltpu.roll(tall, lax.rem(right, n), axis=1)
    lane = lax.broadcasted_iota(jnp.int32, (n + 8, n), 1)
    return jnp.concatenate([jnp.where(lane >= right, tall, 0.0), jnp.where(lane < right, tall, 0.0)], axis=1)


def stage_kernel(own, probe, own_copy, probe_copy):
    own_copy[...] = own[...]
    probe_copy[...] = probe[...]


def light_kernel(info, former, probe, light, canvas):
    n = probe.shape[1]
    stripe, columns = light.shape
    power = probe[0] * probe[0] + probe[1] * probe[1]

    def fill(source):
        rows, cols, (live, *_) = scalars(source)
        canvas[...] = jnp.zeros_like(canvas)
        for slot in range(len(rows)):

            @pl.when(slot < live)
            def _():
                at, down, right = spot(rows[slot], cols[slot], columns, n)
                canvas[at] = canvas[at] + placed(power, down, right)

    fill(former)
    light[...] = canvas[stripe:]
    fill(info)
    light[...] += canvas[:stripe]


def window_kernel(info, own, following, out, ext):
    cuts, pair, _, n, _ = out.shape
    stripe, columns = own.shape[1:]
    rows, cols, _ = scalars(info)
    ext[:, :stripe] = own[...]
    ext[:, stripe:] = following[...]
    for target in range(cuts):
        for which in range(pair):
            slot = target + which * cuts
            at, down, right = spot(rows[slot], cols[slot], columns, n)
            for part in range(2):
                out[target, which, part] = cut_out(ext[(part, *at)], down, right)


def wave_kernel(scale, info, probe, amplitude, tables, patch, *rest):
    cuts, pair, _, n, _ = patch.shape
    sent, (probe_out, terms, amp, sems) = rest[:cuts], rest[cuts:]
    _, _, (live, me, *_) = scalars(info)
    copies = [
        pltpu.make_async_copy(amplitude.at[me + which * cuts], amp.at[which], sems.at[which]) for which in range(pair)
    ]
    for copy in copies:
        copy.start()

    def patch_of(layer):
        return patch[layer, :, 0], patch[layer, :, 1]

    wave = tuple(jnp.broadcast_to(probe[part][None], (pair, n, n)) for part in range(2))
    incident = []
    for layer in range(cuts):
        incident.append(wave)
        wave = complex_mult(wave, patch_of(layer))
        if layer < cuts - 1:
            wave = both_sides(wave, tables, 0)
    far = both_sides(wave, tables, 2)
    for copy in copies:
        copy.wait()
    magnitude = jnp.sqrt(far[0] * far[0] + far[1] * far[1])
    slot = me + cuts * lax.broadcasted_iota(jnp.int32, (pair, n, n), 0)
    weight = (slot < live).astype(jnp.float32)
    factor = weight * (1.0 - amp[...] / jnp.maximum(magnitude, 1.0))
    back = both_sides((factor * far[0], factor * far[1]), tables, 3)
    for layer in range(cuts - 1, -1, -1):
        value = conj_mult(incident[layer], back)
        terms[layer, :, 0] = value[0]
        terms[layer, :, 1] = value[1]
        carry = conj_mult(patch_of(layer), back)
        if layer > 0:
            back = both_sides(carry, tables, 1)
    for away in range(cuts):
        sent[away][...] = terms[lax.rem(me + away, cuts)]
    rows = n // cuts
    share = probe_out.shape[1]
    total = [jnp.sum(carry[part], axis=0) * scale for part in range(2)]
    for cut in range(cuts):
        block = jnp.concatenate([total[part][cut * rows : (cut + 1) * rows] for part in range(2)], axis=0)
        for group in range(2 * rows // share):
            probe_out[group * cuts + cut] = block[group * share : (group + 1) * share]


def scatter_kernel(info, *rest):
    arrived, (inner, rim, canvas) = rest[:-3], rest[-3:]
    cuts = len(arrived)
    pair, _, n, _ = arrived[0].shape
    stripe, columns = inner.shape[1:]
    rows, cols, (_, me, *_) = scalars(info)
    canvas[...] = jnp.zeros_like(canvas)
    for away in range(cuts):
        source = lax.rem(me + cuts - away, cuts)
        for which in range(pair):
            mine = slice(which * cuts, (which + 1) * cuts)
            at, down, right = spot(choose(rows[mine], source), choose(cols[mine], source), columns, n)
            for part in range(2):
                spread = placed(arrived[away][which, part], down, right)
                canvas[(part, *at)] = canvas[(part, *at)] + spread
    inner[...] = canvas[:, :stripe]
    rim[...] = canvas[:, stripe:]


def total_kernel(rows, out):
    out[...] = jnp.broadcast_to(jnp.sum(rows[...], axis=0)[None], out.shape)


def final_kernel(inner, rim, light, rows, slice_grad, probe_grad):
    whole = light[...] + 1.0
    for part in range(2):
        slice_grad[part, 0] = (inner[part] + rim[part]) / whole
    probe_grad[...] = rows[...].reshape(probe_grad.shape)


def along(block, distance):
    devices = range(lax.axis_size(POS))
    return lax.ppermute(block, POS, [(i - distance, i) for i in devices if i - distance in devices])


def around(block, distance):
    count = lax.axis_size("cuts")
    return lax.ppermute(block, "cuts", [(i, (i + distance) % count) for i in range(count)])


def swap(block, axes):
    return lax.all_to_all(block, axes, 0, 0)


def after(block, *first):
    return lax.optimization_barrier((block, *first))[0]


def local(specimen, probe, amplitude, offsets, live):
    n = probe.shape[1]
    stripe, columns = specimen.shape[2:]
    slots = amplitude.shape[0]
    across = lax.axis_size(POS)
    cuts = lax.axis_size("cuts")
    pair = slots // cuts
    me = lax.axis_index("cuts")
    own = specimen[:, 0]
    following = along(own, -1)
    row = offsets[0] - lax.axis_index(POS) * stripe
    extra = jnp.zeros((slots,), jnp.int32).at[0].set(live[0]).at[1].set(me)
    info = jnp.stack([row, offsets[1], extra])
    vmem = pl.BlockSpec(memory_space=pltpu.VMEM)
    hbm = pl.BlockSpec(memory_space=pltpu.HBM)
    tables = jnp.asarray(table_stack(n))
    stripe_shape = jax.ShapeDtypeStruct((2, stripe, columns), jnp.float32)
    plane_shape = jax.ShapeDtypeStruct((stripe, columns), jnp.float32)
    packet = jax.ShapeDtypeStruct((cuts, pair, 2, n, n), jnp.float32)

    former = along(info, 1)
    own, probe = pl.pallas_call(
        stage_kernel,
        out_shape=[stripe_shape, jax.ShapeDtypeStruct(probe.shape, jnp.float32)],
        in_specs=[vmem] * 2,
        out_specs=[vmem] * 2,
        compiler_params=VMEM,
        name="stage",
    )(own, probe)
    light = pl.pallas_call(
        light_kernel,
        out_shape=plane_shape,
        in_specs=[vmem] * 3,
        out_specs=vmem,
        scratch_shapes=[pltpu.VMEM((stripe + n, columns), jnp.float32)],
        compiler_params=VMEM,
        name="light",
    )(info, former, probe)

    windows = pl.pallas_call(
        window_kernel,
        out_shape=packet,
        in_specs=[vmem] * 3,
        out_specs=vmem,
        scratch_shapes=[pltpu.VMEM((2, 2 * stripe, columns), jnp.float32)],
        compiler_params=VMEM,
        name="windows",
    )(after(info, light), own, following)
    patches = swap(windows, "cuts")

    shares = lax.axis_size(("z", "cuts"))
    packet = jax.ShapeDtypeStruct((pair, 2, n, n), jnp.float32)
    *terms, probe_parts = pl.pallas_call(
        functools.partial(wave_kernel, 1.0 / math.sqrt(slots * across)),
        out_shape=[packet] * cuts + [jax.ShapeDtypeStruct((shares, 2 * n // shares, n), jnp.float32)],
        in_specs=[vmem, vmem, hbm, vmem, vmem],
        out_specs=[vmem] * (cuts + 1),
        scratch_shapes=[
            pltpu.VMEM((cuts, pair, 2, n, n), jnp.float32),
            pltpu.VMEM((pair, n, n), jnp.float32),
            pltpu.SemaphoreType.DMA((pair,)),
        ],
        compiler_params=VMEM,
        name="waves",
    )(info, probe, amplitude, tables, patches)
    def total(rows, axes, **kwargs):
        return pl.pallas_call(
            total_kernel,
            out_shape=jax.ShapeDtypeStruct((lax.axis_size(axes), *rows.shape[1:]), jnp.float32),
            in_specs=[vmem],
            out_specs=vmem,
            compiler_params=VMEM,
            name="total",
            **kwargs,
        )(rows)

    probe_rows = total(swap(probe_parts, ("z", "cuts")), ("y", "core"))
    gathered = [terms[0]] + [around(terms[away], away) for away in range(1, cuts)]
    later = after(info, probe_rows)
    estimate = pl.CostEstimate(flops=10**11, bytes_accessed=10**8, transcendentals=0)
    probe_rows = total(swap(probe_rows, ("y", "core")), "z", cost_estimate=estimate)

    inner, rim = pl.pallas_call(
        scatter_kernel,
        out_shape=[stripe_shape] * 2,
        in_specs=[vmem] * (cuts + 1),
        out_specs=[vmem] * 2,
        scratch_shapes=[pltpu.VMEM((2, stripe + n, columns), jnp.float32)],
        compiler_params=VMEM,
        name="scatter",
    )(later, *gathered)
    rim_in = along(rim, 1)
    probe_rows = swap(probe_rows, "z")
    slice_grad, probe_grad = pl.pallas_call(
        final_kernel,
        out_shape=[
            jax.ShapeDtypeStruct((2, 1, stripe, columns), jnp.float32),
            jax.ShapeDtypeStruct((2, n // cuts, n), jnp.float32),
        ],
        in_specs=[vmem] * 4,
        out_specs=[vmem] * 2,
        compiler_params=VMEM,
        name="final",
    )(inner, rim_in, light, probe_rows)
    return slice_grad, probe_grad


def solution(mesh):
    across, cuts = mesh.devices.shape
    y = min(8, across // 2)
    split = Mesh(mesh.devices.reshape(across // 2 // y, y, 2, cuts), ("z", "y", "core", "cuts"))
    in_specs = (P(None, "cuts", POS, None), P(), P(POS, None, None), P(None, POS), P(POS))
    out_specs = (P(None, "cuts", POS, None), P(None, "cuts", None))
    return jax.shard_map(local, mesh=split, in_specs=in_specs, out_specs=out_specs, check_vma=False)
```

```python
import functools
import math

import jax
import jax.numpy as jnp
import numpy as np
from jax import lax
from jax.experimental import pallas as pl
from jax.experimental.pallas import tpu as pltpu
from jax.sharding import Mesh
from jax.sharding import PartitionSpec as P

FRESNEL = 0.7
POS = ("z", "y", "core")
VMEM = pltpu.CompilerParams(vmem_limit_bytes=16 * 1024 * 1024)


def make_tables(n):
    index = np.arange(n)
    four = np.exp(-2j * math.pi / n * (index[:, None] * index[None, :] % n)) / math.sqrt(n)
    signed = np.where(index < n // 2, index, index - n)
    spacing = (index[:, None] - index[None, :]) % n
    turns = spacing[:, :, None] * index[None, None, :] % n
    phase = FRESNEL * math.pi / n * (signed * signed)
    prop = np.mean(np.exp(1j * (phase[None, None, :] + 2.0 * math.pi / n * turns)), axis=2)
    return four, prop


def split_pair(table):
    whole = np.block([[table.real, table.imag], [-table.imag, table.real]]).astype(np.float32)
    lead = whole.astype(jnp.bfloat16)
    return np.stack([lead, (whole - lead.astype(np.float32)).astype(jnp.bfloat16)])


def table_stack(n):
    four, prop = make_tables(n)
    return np.stack([split_pair(prop), split_pair(prop.conj()), split_pair(four), split_pair(four.conj())])


def parts(x):
    lead = x.astype(jnp.bfloat16)
    return lead, (x - lead.astype(jnp.float32)).astype(jnp.bfloat16)


def dot(a, b):
    return jnp.dot(a, b, preferred_element_type=jnp.float32)


def both_sides(wave, tables, which):
    real, imag = wave
    n = real.shape[1]
    right_lead, right_trail = tables[which, 0], tables[which, 1]
    left_lead, left_trail = tables[which ^ 1, 0], tables[which ^ 1, 1]
    halves = []
    for p in range(real.shape[0]):
        lead, trail = parts(jnp.concatenate([real[p], imag[p]], axis=1))
        mid = dot(lead, right_lead) + (dot(trail, right_lead) + dot(lead, right_trail))
        halves.append(parts(jnp.concatenate([mid[:, :n], mid[:, n:]], axis=0)))
    outs = []
    for lead, trail in halves:
        both = dot(left_lead, jnp.concatenate([lead, trail], axis=1))
        outs.append(both[:, :n] + (both[:, n:] + dot(left_trail, lead)))
    return jnp.stack([out[:n] for out in outs]), jnp.stack([out[n:] for out in outs])


def complex_mult(a, b):
    return a[0] * b[0] - a[1] * b[1], a[0] * b[1] + a[1] * b[0]


def conj_mult(a, b):
    return a[0] * b[0] + a[1] * b[1], a[0] * b[1] - a[1] * b[0]


def scalars(info, slots):
    return [[info[line, slot] for slot in range(slots)] for line in range(3)]


def choose(values, index):
    chosen = values[0]
    for position in range(1, len(values)):
        chosen = jnp.where(index == position, values[position], chosen)
    return chosen


def spot(row, col, columns, n):
    top = pl.multiple_of(row // 8 * 8, 8)
    band = pl.multiple_of(jnp.minimum(col // n * n, columns - 2 * n), n)
    return (pl.ds(top, n + 8), pl.ds(band, 2 * n)), row - top, col - band


def cut_out(box, down, right):
    n = box.shape[1] // 2
    turn = lax.rem(n - right, n)
    lane = lax.broadcasted_iota(jnp.int32, (n + 8, n), 1)
    wide = jnp.where(lane < n - right, pltpu.roll(box[:, :n], turn, axis=1), pltpu.roll(box[:, n:], turn, axis=1))
    groups = pltpu.roll(wide.reshape(n // 8 + 1, 8, n), lax.rem(8 - down, 8), axis=1)
    line = lax.broadcasted_iota(jnp.int32, (n // 8, 8, n), 1)
    return jnp.where(line < 8 - down, groups[:-1], groups[1:]).reshape(n, n)


def placed(value, down, right):
    n = value.shape[0]
    groups = pltpu.roll(value.reshape(n // 8, 8, n), down, axis=1)
    empty = jnp.zeros((1, 8, n), jnp.float32)
    line = lax.broadcasted_iota(jnp.int32, (n // 8 + 1, 8, n), 1)
    tall = jnp.where(
        line >= down, jnp.concatenate([groups, empty], axis=0), jnp.concatenate([empty, groups], axis=0)
    ).reshape(n + 8, n)
    tall = pltpu.roll(tall, lax.rem(right, n), axis=1)
    lane = lax.broadcasted_iota(jnp.int32, (n + 8, n), 1)
    return jnp.concatenate([jnp.where(lane >= right, tall, 0.0), jnp.where(lane < right, tall, 0.0)], axis=1)


def stage_kernel(own, probe, own_copy, probe_copy):
    own_copy[...] = own[...]
    probe_copy[...] = probe[...]


def lit(slots, places, probe, canvas):
    n = probe.shape[1]
    columns = canvas.shape[1]
    power = probe[0] * probe[0] + probe[1] * probe[1]
    rows, cols, (live, *_) = scalars(places, slots)
    canvas[...] = jnp.zeros_like(canvas)
    for slot in range(slots):

        @pl.when(slot < live)
        def _():
            at, down, right = spot(rows[slot], cols[slot], columns, n)
            canvas[at] = canvas[at] + placed(power, down, right)


def light_kernel(slots, info, probe, light, canvas):
    lit(slots, info[...], probe, canvas)
    light[...] = canvas[: light.shape[0]]


def window_kernel(info, own, following, out, ext):
    cuts, pair, _, n, _ = out.shape
    stripe, columns = own.shape[1:]
    rows, cols, _ = scalars(info[...], cuts * pair)
    ext[:, :stripe] = own[...]
    ext[:, stripe:] = following[...]
    for target in range(cuts):
        for which in range(pair):
            slot = target + which * cuts
            at, down, right = spot(rows[slot], cols[slot], columns, n)
            for part in range(2):
                out[target, which, part] = cut_out(ext[(part, *at)], down, right)


def wave_kernel(scale, info, probe, amplitude, tables, patch, *rest):
    cuts, pair, _, n, _ = patch.shape
    sent, (probe_out, terms, amp, sems) = rest[:cuts], rest[cuts:]
    _, _, (live, me, *_) = scalars(info[...], cuts * pair)
    copies = [
        pltpu.make_async_copy(amplitude.at[me + which * cuts], amp.at[which], sems.at[which]) for which in range(pair)
    ]
    for copy in copies:
        copy.start()

    def patch_of(layer):
        return patch[layer, :, 0], patch[layer, :, 1]

    wave = tuple(jnp.broadcast_to(probe[part][None], (pair, n, n)) for part in range(2))
    incident = []
    for layer in range(cuts):
        incident.append(wave)
        wave = complex_mult(wave, patch_of(layer))
        if layer < cuts - 1:
            wave = both_sides(wave, tables, 0)
    far = both_sides(wave, tables, 2)
    for copy in copies:
        copy.wait()
    magnitude = jnp.sqrt(far[0] * far[0] + far[1] * far[1])
    slot = me + cuts * lax.broadcasted_iota(jnp.int32, (pair, n, n), 0)
    weight = (slot < live).astype(jnp.float32)
    factor = weight * (1.0 - amp[...] / jnp.maximum(magnitude, 1.0))
    back = both_sides((factor * far[0], factor * far[1]), tables, 3)
    for layer in range(cuts - 1, -1, -1):
        value = conj_mult(incident[layer], back)
        terms[layer, :, 0] = value[0]
        terms[layer, :, 1] = value[1]
        carry = conj_mult(patch_of(layer), back)
        if layer > 0:
            back = both_sides(carry, tables, 1)
    for away in range(cuts):
        sent[away][...] = terms[lax.rem(me + away, cuts)]
    rows = n // cuts
    share = probe_out.shape[1]
    total = [jnp.sum(carry[part], axis=0) * scale for part in range(2)]
    for cut in range(cuts):
        block = jnp.concatenate([total[part][cut * rows : (cut + 1) * rows] for part in range(2)], axis=0)
        for group in range(2 * rows // share):
            probe_out[group * cuts + cut] = block[group * share : (group + 1) * share]


def scatter_kernel(info, *rest):
    arrived, (inner, rim, canvas) = rest[:-3], rest[-3:]
    cuts = len(arrived)
    pair, _, n, _ = arrived[0].shape
    stripe, columns = inner.shape[1:]
    rows, cols, (_, me, *_) = scalars(info[...], cuts * pair)
    canvas[...] = jnp.zeros_like(canvas)
    for away in range(cuts):
        source = lax.rem(me + cuts - away, cuts)
        for which in range(pair):
            mine = slice(which * cuts, (which + 1) * cuts)
            at, down, right = spot(choose(rows[mine], source), choose(cols[mine], source), columns, n)
            for part in range(2):
                spread = placed(arrived[away][which, part], down, right)
                canvas[(part, *at)] = canvas[(part, *at)] + spread
    inner[...] = canvas[:, :stripe]
    rim[:, :n] = canvas[:, stripe:]
    rim[:, n:] = jnp.zeros_like(rim[:, n:])
    rim[0, n:, :n] = info[...].astype(jnp.float32)


def total_kernel(rows, out):
    out[...] = jnp.broadcast_to(jnp.sum(rows[...], axis=0)[None], out.shape)


def final_kernel(slots, inner, rim, light, probe, rows, slice_grad, probe_grad, canvas):
    n = probe.shape[1]
    stripe = light.shape[0]
    lit(slots, rim[0, n:, :n].astype(jnp.int32), probe, canvas)
    whole = light[...] + canvas[stripe:] + 1.0
    for part in range(2):
        slice_grad[part, 0] = (inner[part] + rim[part, :n]) / whole
    probe_grad[...] = rows[...].reshape(probe_grad.shape)


def along(block, distance):
    devices = range(lax.axis_size(POS))
    return lax.ppermute(block, POS, [(i - distance, i) for i in devices if i - distance in devices])


def around(block, distance):
    count = lax.axis_size("cuts")
    return lax.ppermute(block, "cuts", [(i, (i + distance) % count) for i in range(count)])


def swap(block, axes):
    return lax.all_to_all(block, axes, 0, 0)


def after(block, *first):
    return lax.optimization_barrier((block, *first))[0]


def local(specimen, probe, amplitude, offsets, live):
    n = probe.shape[1]
    stripe, columns = specimen.shape[2:]
    slots = amplitude.shape[0]
    across = lax.axis_size(POS)
    cuts = lax.axis_size("cuts")
    pair = slots // cuts
    me = lax.axis_index("cuts")
    own = specimen[:, 0]
    following = along(own, -1)
    row = offsets[0] - lax.axis_index(POS) * stripe
    extra = jnp.zeros((slots,), jnp.int32).at[0].set(live[0]).at[1].set(me)
    info = jnp.pad(jnp.stack([row, offsets[1], extra]), ((0, 5), (0, n - slots)))
    vmem = pl.BlockSpec(memory_space=pltpu.VMEM)
    hbm = pl.BlockSpec(memory_space=pltpu.HBM)
    tables = jnp.asarray(table_stack(n))
    stripe_shape = jax.ShapeDtypeStruct((2, stripe, columns), jnp.float32)
    plane_shape = jax.ShapeDtypeStruct((stripe, columns), jnp.float32)
    packet = jax.ShapeDtypeStruct((cuts, pair, 2, n, n), jnp.float32)

    own, probe = pl.pallas_call(
        stage_kernel,
        out_shape=[stripe_shape, jax.ShapeDtypeStruct(probe.shape, jnp.float32)],
        in_specs=[vmem] * 2,
        out_specs=[vmem] * 2,
        compiler_params=VMEM,
        name="stage",
    )(own, probe)
    light = pl.pallas_call(
        functools.partial(light_kernel, slots),
        out_shape=plane_shape,
        in_specs=[vmem] * 2,
        out_specs=vmem,
        scratch_shapes=[pltpu.VMEM((stripe + n, columns), jnp.float32)],
        compiler_params=VMEM,
        name="light",
    )(info, probe)

    windows = pl.pallas_call(
        window_kernel,
        out_shape=packet,
        in_specs=[vmem] * 3,
        out_specs=vmem,
        scratch_shapes=[pltpu.VMEM((2, 2 * stripe, columns), jnp.float32)],
        compiler_params=VMEM,
        name="windows",
    )(after(info, light), own, following)
    patches = swap(windows, "cuts")

    shares = lax.axis_size(("z", "cuts"))
    packet = jax.ShapeDtypeStruct((pair, 2, n, n), jnp.float32)
    *terms, probe_parts = pl.pallas_call(
        functools.partial(wave_kernel, 1.0 / math.sqrt(slots * across)),
        out_shape=[packet] * cuts + [jax.ShapeDtypeStruct((shares, 2 * n // shares, n), jnp.float32)],
        in_specs=[vmem, vmem, hbm, vmem, vmem],
        out_specs=[vmem] * (cuts + 1),
        scratch_shapes=[
            pltpu.VMEM((cuts, pair, 2, n, n), jnp.float32),
            pltpu.VMEM((pair, n, n), jnp.float32),
            pltpu.SemaphoreType.DMA((pair,)),
        ],
        compiler_params=VMEM,
        name="waves",
    )(info, probe, amplitude, tables, patches)
    def total(rows, axes, **kwargs):
        return pl.pallas_call(
            total_kernel,
            out_shape=jax.ShapeDtypeStruct((lax.axis_size(axes), *rows.shape[1:]), jnp.float32),
            in_specs=[vmem],
            out_specs=vmem,
            compiler_params=VMEM,
            name="total",
            **kwargs,
        )(rows)

    probe_rows = total(swap(probe_parts, ("z", "cuts")), ("y", "core"))
    gathered = [terms[0]] + [around(terms[away], away) for away in range(1, cuts)]
    later = after(info, probe_rows)
    estimate = pl.CostEstimate(flops=10**11, bytes_accessed=10**8, transcendentals=0)
    probe_rows = total(swap(probe_rows, ("y", "core")), "z", cost_estimate=estimate)

    inner, rim = pl.pallas_call(
        scatter_kernel,
        out_shape=[stripe_shape, jax.ShapeDtypeStruct((2, n + 8, columns), jnp.float32)],
        in_specs=[vmem] * (cuts + 1),
        out_specs=[vmem] * 2,
        scratch_shapes=[pltpu.VMEM((2, stripe + n, columns), jnp.float32)],
        compiler_params=VMEM,
        name="scatter",
    )(later, *gathered)
    rim_in = along(rim, 1)
    probe_rows = swap(probe_rows, "z")
    slice_grad, probe_grad = pl.pallas_call(
        functools.partial(final_kernel, slots),
        out_shape=[
            jax.ShapeDtypeStruct((2, 1, stripe, columns), jnp.float32),
            jax.ShapeDtypeStruct((2, n // cuts, n), jnp.float32),
        ],
        in_specs=[vmem] * 5,
        out_specs=[vmem] * 2,
        scratch_shapes=[pltpu.VMEM((stripe + n, columns), jnp.float32)],
        compiler_params=VMEM,
        name="final",
    )(inner, rim_in, light, probe, probe_rows)
    return slice_grad, probe_grad


def solution(mesh):
    across, cuts = mesh.devices.shape
    y = min(8, across // 2)
    split = Mesh(mesh.devices.reshape(across // 2 // y, y, 2, cuts), ("z", "y", "core", "cuts"))
    in_specs = (P(None, "cuts", POS, None), P(), P(POS, None, None), P(None, POS), P(POS))
    out_specs = (P(None, "cuts", POS, None), P(None, "cuts", None))
    return jax.shard_map(local, mesh=split, in_specs=in_specs, out_specs=out_specs, check_vma=False)
```

```python
import functools
import math

import jax
import jax.numpy as jnp
import numpy as np
from jax import lax
from jax.experimental import pallas as pl
from jax.experimental.pallas import tpu as pltpu
from jax.sharding import Mesh
from jax.sharding import PartitionSpec as P

FRESNEL = 0.7
POS = ("z", "y", "core")
VMEM = pltpu.CompilerParams(vmem_limit_bytes=16 * 1024 * 1024)


def make_tables(n):
    index = np.arange(n)
    four = np.exp(-2j * math.pi / n * (index[:, None] * index[None, :] % n)) / math.sqrt(n)
    signed = np.where(index < n // 2, index, index - n)
    spacing = (index[:, None] - index[None, :]) % n
    turns = spacing[:, :, None] * index[None, None, :] % n
    phase = FRESNEL * math.pi / n * (signed * signed)
    prop = np.mean(np.exp(1j * (phase[None, None, :] + 2.0 * math.pi / n * turns)), axis=2)
    return four, prop


def split_pair(table):
    whole = np.block([[table.real, table.imag], [-table.imag, table.real]]).astype(np.float32)
    lead = whole.astype(jnp.bfloat16)
    return np.stack([lead, (whole - lead.astype(np.float32)).astype(jnp.bfloat16)])


def table_stack(n):
    four, prop = make_tables(n)
    return np.stack([split_pair(prop), split_pair(prop.conj()), split_pair(four), split_pair(four.conj())])


def parts(x):
    lead = x.astype(jnp.bfloat16)
    return lead, (x - lead.astype(jnp.float32)).astype(jnp.bfloat16)


def dot(a, b):
    return jnp.dot(a, b, preferred_element_type=jnp.float32)


def both_sides(wave, tables, which):
    real, imag = wave
    n = real.shape[1]
    right_lead, right_trail = tables[which, 0], tables[which, 1]
    left_lead, left_trail = tables[which ^ 1, 0], tables[which ^ 1, 1]
    halves = []
    for p in range(real.shape[0]):
        lead, trail = parts(jnp.concatenate([real[p], imag[p]], axis=1))
        mid = dot(lead, right_lead) + (dot(trail, right_lead) + dot(lead, right_trail))
        halves.append(parts(jnp.concatenate([mid[:, :n], mid[:, n:]], axis=0)))
    outs = []
    for lead, trail in halves:
        both = dot(left_lead, jnp.concatenate([lead, trail], axis=1))
        outs.append(both[:, :n] + (both[:, n:] + dot(left_trail, lead)))
    return jnp.stack([out[:n] for out in outs]), jnp.stack([out[n:] for out in outs])


def complex_mult(a, b):
    return a[0] * b[0] - a[1] * b[1], a[0] * b[1] + a[1] * b[0]


def conj_mult(a, b):
    return a[0] * b[0] + a[1] * b[1], a[0] * b[1] - a[1] * b[0]


def scalars(info, slots):
    return [[info[line, slot] for slot in range(slots)] for line in range(3)]


def choose(values, index):
    chosen = values[0]
    for position in range(1, len(values)):
        chosen = jnp.where(index == position, values[position], chosen)
    return chosen


def spot(row, col, columns, n):
    top = pl.multiple_of(row // 8 * 8, 8)
    band = pl.multiple_of(jnp.minimum(col // n * n, columns - 2 * n), n)
    return (pl.ds(top, n + 8), pl.ds(band, 2 * n)), row - top, col - band


def cut_out(box, down, right):
    n = box.shape[1] // 2
    turn = lax.rem(n - right, n)
    lane = lax.broadcasted_iota(jnp.int32, (n + 8, n), 1)
    wide = jnp.where(lane < n - right, pltpu.roll(box[:, :n], turn, axis=1), pltpu.roll(box[:, n:], turn, axis=1))
    groups = pltpu.roll(wide.reshape(n // 8 + 1, 8, n), lax.rem(8 - down, 8), axis=1)
    line = lax.broadcasted_iota(jnp.int32, (n // 8, 8, n), 1)
    return jnp.where(line < 8 - down, groups[:-1], groups[1:]).reshape(n, n)


def placed(value, down, right):
    n = value.shape[0]
    groups = pltpu.roll(value.reshape(n // 8, 8, n), down, axis=1)
    empty = jnp.zeros((1, 8, n), jnp.float32)
    line = lax.broadcasted_iota(jnp.int32, (n // 8 + 1, 8, n), 1)
    tall = jnp.where(
        line >= down, jnp.concatenate([groups, empty], axis=0), jnp.concatenate([empty, groups], axis=0)
    ).reshape(n + 8, n)
    tall = pltpu.roll(tall, lax.rem(right, n), axis=1)
    lane = lax.broadcasted_iota(jnp.int32, (n + 8, n), 1)
    return jnp.concatenate([jnp.where(lane >= right, tall, 0.0), jnp.where(lane < right, tall, 0.0)], axis=1)


def stage_kernel(own, probe, own_copy, probe_copy):
    own_copy[...] = own[...]
    probe_copy[...] = probe[...]


def lit(slots, places, probe, canvas):
    n = probe.shape[1]
    columns = canvas.shape[1]
    power = probe[0] * probe[0] + probe[1] * probe[1]
    rows, cols, (live, *_) = scalars(places, slots)
    canvas[...] = jnp.zeros_like(canvas)
    for slot in range(slots):

        @pl.when(slot < live)
        def _():
            at, down, right = spot(rows[slot], cols[slot], columns, n)
            canvas[at] = canvas[at] + placed(power, down, right)


def light_kernel(slots, info, probe, light, canvas):
    lit(slots, info[...], probe, canvas)
    light[...] = canvas[: light.shape[0]]


def window_kernel(info, own, following, out, ext):
    cuts, pair, _, n, _ = out.shape
    stripe, columns = own.shape[1:]
    rows, cols, _ = scalars(info[...], cuts * pair)
    ext[:, :stripe] = own[...]
    ext[:, stripe:] = following[...]
    for target in range(cuts):
        for which in range(pair):
            slot = target + which * cuts
            at, down, right = spot(rows[slot], cols[slot], columns, n)
            for part in range(2):
                out[target, which, part] = cut_out(ext[(part, *at)], down, right)


def wave_kernel(scale, info, probe, amplitude, tables, patch, *rest):
    cuts, pair, _, n, _ = patch.shape
    sent, (probe_out, terms, amp, sems) = rest[:cuts], rest[cuts:]
    _, _, (live, me, *_) = scalars(info[...], cuts * pair)
    copies = [
        pltpu.make_async_copy(amplitude.at[me + which * cuts], amp.at[which], sems.at[which]) for which in range(pair)
    ]
    for copy in copies:
        copy.start()

    def patch_of(layer):
        return patch[layer, :, 0], patch[layer, :, 1]

    wave = tuple(jnp.broadcast_to(probe[part][None], (pair, n, n)) for part in range(2))
    incident = []
    for layer in range(cuts):
        incident.append(wave)
        wave = complex_mult(wave, patch_of(layer))
        if layer < cuts - 1:
            wave = both_sides(wave, tables, 0)
    far = both_sides(wave, tables, 2)
    for copy in copies:
        copy.wait()
    magnitude = jnp.sqrt(far[0] * far[0] + far[1] * far[1])
    slot = me + cuts * lax.broadcasted_iota(jnp.int32, (pair, n, n), 0)
    weight = (slot < live).astype(jnp.float32)
    factor = weight * (1.0 - amp[...] / jnp.maximum(magnitude, 1.0))
    back = both_sides((factor * far[0], factor * far[1]), tables, 3)
    for layer in range(cuts - 1, -1, -1):
        value = conj_mult(incident[layer], back)
        terms[layer, :, 0] = value[0]
        terms[layer, :, 1] = value[1]
        carry = conj_mult(patch_of(layer), back)
        if layer > 0:
            back = both_sides(carry, tables, 1)
    for away in range(cuts):
        sent[away][...] = terms[lax.rem(me + away, cuts)]
    rows = n // cuts
    share = probe_out.shape[1]
    total = [jnp.sum(carry[part], axis=0) * scale for part in range(2)]
    for cut in range(cuts):
        block = jnp.concatenate([total[part][cut * rows : (cut + 1) * rows] for part in range(2)], axis=0)
        for group in range(2 * rows // share):
            probe_out[group * cuts + cut] = block[group * share : (group + 1) * share]


def scatter_kernel(info, *rest):
    arrived, (inner, rim, canvas) = rest[:-3], rest[-3:]
    cuts = len(arrived)
    pair, _, n, _ = arrived[0].shape
    stripe, columns = inner.shape[1:]
    rows, cols, (_, me, *_) = scalars(info[...], cuts * pair)
    canvas[...] = jnp.zeros_like(canvas)
    for away in range(cuts):
        source = lax.rem(me + cuts - away, cuts)
        for which in range(pair):
            mine = slice(which * cuts, (which + 1) * cuts)
            at, down, right = spot(choose(rows[mine], source), choose(cols[mine], source), columns, n)
            for part in range(2):
                spread = placed(arrived[away][which, part], down, right)
                canvas[(part, *at)] = canvas[(part, *at)] + spread
    inner[...] = canvas[:, :stripe]
    rim[:, :n] = canvas[:, stripe:]
    rim[:, n:] = jnp.zeros_like(rim[:, n:])
    rim[0, n:, :n] = info[...].astype(jnp.float32)


def total_kernel(rows, out):
    out[...] = jnp.broadcast_to(jnp.sum(rows[...], axis=0)[None], out.shape)


def final_kernel(slots, inner, rim, light, probe, rows, slice_grad, probe_grad, canvas):
    n = probe.shape[1]
    stripe = light.shape[0]
    lit(slots, rim[0, n:, :n].astype(jnp.int32), probe, canvas)
    whole = light[...] + canvas[stripe:] + 1.0
    for part in range(2):
        slice_grad[part, 0] = (inner[part] + rim[part, :n]) / whole
    probe_grad[...] = rows[...].reshape(probe_grad.shape)


def along(block, distance):
    devices = range(lax.axis_size(POS))
    return lax.ppermute(block, POS, [(i - distance, i) for i in devices if i - distance in devices])


def around(block, distance):
    count = lax.axis_size("cuts")
    return lax.ppermute(block, "cuts", [(i, (i + distance) % count) for i in range(count)])


def swap(block, axes):
    return lax.all_to_all(block, axes, 0, 0)


def after(block, *first):
    return lax.optimization_barrier((block, *first))[0]


def local(specimen, probe, amplitude, offsets, live):
    n = probe.shape[1]
    stripe, columns = specimen.shape[2:]
    slots = amplitude.shape[0]
    across = lax.axis_size(POS)
    cuts = lax.axis_size("cuts")
    pair = slots // cuts
    me = lax.axis_index("cuts")
    own = specimen[:, 0]
    following = along(own, -1)
    row = offsets[0] - lax.axis_index(POS) * stripe
    extra = jnp.zeros((slots,), jnp.int32).at[0].set(live[0]).at[1].set(me)
    info = jnp.pad(jnp.stack([row, offsets[1], extra]), ((0, 5), (0, n - slots)))
    vmem = pl.BlockSpec(memory_space=pltpu.VMEM)
    hbm = pl.BlockSpec(memory_space=pltpu.HBM)
    tables = jnp.asarray(table_stack(n))
    stripe_shape = jax.ShapeDtypeStruct((2, stripe, columns), jnp.float32)
    plane_shape = jax.ShapeDtypeStruct((stripe, columns), jnp.float32)
    packet = jax.ShapeDtypeStruct((cuts, pair, 2, n, n), jnp.float32)

    own, probe = pl.pallas_call(
        stage_kernel,
        out_shape=[stripe_shape, jax.ShapeDtypeStruct(probe.shape, jnp.float32)],
        in_specs=[vmem] * 2,
        out_specs=[vmem] * 2,
        compiler_params=VMEM,
        name="stage",
    )(own, probe)
    light = pl.pallas_call(
        functools.partial(light_kernel, slots),
        out_shape=plane_shape,
        in_specs=[vmem] * 2,
        out_specs=vmem,
        scratch_shapes=[pltpu.VMEM((stripe + n, columns), jnp.float32)],
        compiler_params=VMEM,
        name="light",
    )(info, probe)

    windows = pl.pallas_call(
        window_kernel,
        out_shape=packet,
        in_specs=[vmem] * 3,
        out_specs=vmem,
        scratch_shapes=[pltpu.VMEM((2, 2 * stripe, columns), jnp.float32)],
        compiler_params=VMEM,
        name="windows",
    )(after(info, light), own, following)
    patches = swap(windows, "cuts")

    shares = lax.axis_size(("z", "cuts"))
    packet = jax.ShapeDtypeStruct((pair, 2, n, n), jnp.float32)
    *terms, probe_parts = pl.pallas_call(
        functools.partial(wave_kernel, 1.0 / math.sqrt(slots * across)),
        out_shape=[packet] * cuts + [jax.ShapeDtypeStruct((shares, 2 * n // shares, n), jnp.float32)],
        in_specs=[vmem, vmem, hbm, vmem, vmem],
        out_specs=[vmem] * (cuts + 1),
        scratch_shapes=[
            pltpu.VMEM((cuts, pair, 2, n, n), jnp.float32),
            pltpu.VMEM((pair, n, n), jnp.float32),
            pltpu.SemaphoreType.DMA((pair,)),
        ],
        compiler_params=VMEM,
        name="waves",
    )(info, probe, amplitude, tables, patches)
    def total(rows, axes, **kwargs):
        return pl.pallas_call(
            total_kernel,
            out_shape=jax.ShapeDtypeStruct((lax.axis_size(axes), *rows.shape[1:]), jnp.float32),
            in_specs=[vmem],
            out_specs=vmem,
            compiler_params=VMEM,
            name="total",
            **kwargs,
        )(rows)

    gathered = [terms[0]] + [around(terms[away], away) for away in range(1, cuts)]
    probe_rows = swap(probe_parts, ("z", "cuts"))
    probe_rows, gathered[2] = lax.optimization_barrier((probe_rows, gathered[2]))
    probe_rows = total(probe_rows, ("y", "core"))
    later = after(info, probe_rows)
    estimate = pl.CostEstimate(flops=10**11, bytes_accessed=10**8, transcendentals=0)
    probe_rows = total(swap(probe_rows, ("y", "core")), "z", cost_estimate=estimate)

    inner, rim = pl.pallas_call(
        scatter_kernel,
        out_shape=[stripe_shape, jax.ShapeDtypeStruct((2, n + 8, columns), jnp.float32)],
        in_specs=[vmem] * (cuts + 1),
        out_specs=[vmem] * 2,
        scratch_shapes=[pltpu.VMEM((2, stripe + n, columns), jnp.float32)],
        compiler_params=VMEM,
        name="scatter",
    )(later, *gathered)
    rim_in = along(rim, 1)
    probe_rows = swap(probe_rows, "z")
    slice_grad, probe_grad = pl.pallas_call(
        functools.partial(final_kernel, slots),
        out_shape=[
            jax.ShapeDtypeStruct((2, 1, stripe, columns), jnp.float32),
            jax.ShapeDtypeStruct((2, n // cuts, n), jnp.float32),
        ],
        in_specs=[vmem] * 5,
        out_specs=[vmem] * 2,
        scratch_shapes=[pltpu.VMEM((stripe + n, columns), jnp.float32)],
        compiler_params=VMEM,
        name="final",
    )(inner, rim_in, light, probe, probe_rows)
    return slice_grad, probe_grad


def solution(mesh):
    across, cuts = mesh.devices.shape
    y = min(8, across // 2)
    split = Mesh(mesh.devices.reshape(across // 2 // y, y, 2, cuts), ("z", "y", "core", "cuts"))
    in_specs = (P(None, "cuts", POS, None), P(), P(POS, None, None), P(None, POS), P(POS))
    out_specs = (P(None, "cuts", POS, None), P(None, "cuts", None))
    return jax.shard_map(local, mesh=split, in_specs=in_specs, out_specs=out_specs, check_vma=False)
```

```python
import functools
import math

import jax
import jax.numpy as jnp
import numpy as np
from jax import lax
from jax.experimental import pallas as pl
from jax.experimental.pallas import tpu as pltpu
from jax.sharding import Mesh
from jax.sharding import PartitionSpec as P

FRESNEL = 0.7
POS = ("z", "y", "core")
VMEM = pltpu.CompilerParams(vmem_limit_bytes=16 * 1024 * 1024)


def make_tables(n):
    index = np.arange(n)
    four = np.exp(-2j * math.pi / n * (index[:, None] * index[None, :] % n)) / math.sqrt(n)
    signed = np.where(index < n // 2, index, index - n)
    spacing = (index[:, None] - index[None, :]) % n
    turns = spacing[:, :, None] * index[None, None, :] % n
    phase = FRESNEL * math.pi / n * (signed * signed)
    prop = np.mean(np.exp(1j * (phase[None, None, :] + 2.0 * math.pi / n * turns)), axis=2)
    return four, prop


def split_pair(table):
    whole = np.block([[table.real, table.imag], [-table.imag, table.real]]).astype(np.float32)
    lead = whole.astype(jnp.bfloat16)
    return np.stack([lead, (whole - lead.astype(np.float32)).astype(jnp.bfloat16)])


def table_stack(n):
    four, prop = make_tables(n)
    return np.stack([split_pair(prop), split_pair(prop.conj()), split_pair(four), split_pair(four.conj())])


def parts(x):
    lead = x.astype(jnp.bfloat16)
    return lead, (x - lead.astype(jnp.float32)).astype(jnp.bfloat16)


def dot(a, b):
    return jnp.dot(a, b, preferred_element_type=jnp.float32)


def both_sides(wave, tables, which):
    real, imag = wave
    n = real.shape[1]
    right_lead, right_trail = tables[which, 0], tables[which, 1]
    left_lead, left_trail = tables[which ^ 1, 0], tables[which ^ 1, 1]
    halves = []
    for p in range(real.shape[0]):
        lead, trail = parts(jnp.concatenate([real[p], imag[p]], axis=1))
        mid = dot(lead, right_lead) + (dot(trail, right_lead) + dot(lead, right_trail))
        halves.append(parts(jnp.concatenate([mid[:, :n], mid[:, n:]], axis=0)))
    outs = []
    for lead, trail in halves:
        both = dot(left_lead, jnp.concatenate([lead, trail], axis=1))
        outs.append(both[:, :n] + (both[:, n:] + dot(left_trail, lead)))
    return jnp.stack([out[:n] for out in outs]), jnp.stack([out[n:] for out in outs])


def complex_mult(a, b):
    return a[0] * b[0] - a[1] * b[1], a[0] * b[1] + a[1] * b[0]


def conj_mult(a, b):
    return a[0] * b[0] + a[1] * b[1], a[0] * b[1] - a[1] * b[0]


def scalars(info, slots):
    return [[info[line, slot] for slot in range(slots)] for line in range(3)]


def choose(values, index):
    chosen = values[0]
    for position in range(1, len(values)):
        chosen = jnp.where(index == position, values[position], chosen)
    return chosen


def spot(row, col, columns, n):
    top = pl.multiple_of(row // 8 * 8, 8)
    band = pl.multiple_of(jnp.minimum(col // n * n, columns - 2 * n), n)
    return (pl.ds(top, n + 8), pl.ds(band, 2 * n)), row - top, col - band


def cut_out(box, down, right):
    n = box.shape[1] // 2
    turn = lax.rem(n - right, n)
    lane = lax.broadcasted_iota(jnp.int32, (n + 8, n), 1)
    wide = jnp.where(lane < n - right, pltpu.roll(box[:, :n], turn, axis=1), pltpu.roll(box[:, n:], turn, axis=1))
    groups = pltpu.roll(wide.reshape(n // 8 + 1, 8, n), lax.rem(8 - down, 8), axis=1)
    line = lax.broadcasted_iota(jnp.int32, (n // 8, 8, n), 1)
    return jnp.where(line < 8 - down, groups[:-1], groups[1:]).reshape(n, n)


def placed(value, down, right):
    n = value.shape[0]
    groups = pltpu.roll(value.reshape(n // 8, 8, n), down, axis=1)
    empty = jnp.zeros((1, 8, n), jnp.float32)
    line = lax.broadcasted_iota(jnp.int32, (n // 8 + 1, 8, n), 1)
    tall = jnp.where(
        line >= down, jnp.concatenate([groups, empty], axis=0), jnp.concatenate([empty, groups], axis=0)
    ).reshape(n + 8, n)
    tall = pltpu.roll(tall, lax.rem(right, n), axis=1)
    lane = lax.broadcasted_iota(jnp.int32, (n + 8, n), 1)
    return jnp.concatenate([jnp.where(lane >= right, tall, 0.0), jnp.where(lane < right, tall, 0.0)], axis=1)


def stage_kernel(own, probe, own_copy, probe_copy):
    own_copy[...] = own[...]
    probe_copy[...] = probe[...]


def lit(slots, places, probe, canvas):
    n = probe.shape[1]
    columns = canvas.shape[1]
    power = probe[0] * probe[0] + probe[1] * probe[1]
    rows, cols, (live, *_) = scalars(places, slots)
    for slot in range(slots):
        at, down, right = spot(rows[slot], cols[slot], columns, n)
        canvas[at] = canvas[at] + placed(jnp.where(slot < live, power, 0.0), down, right)


def light_kernel(slots, info, probe, light, canvas):
    canvas[...] = jnp.ones_like(canvas)
    lit(slots, info[...], probe, canvas)
    light[...] = canvas[: light.shape[0]]


def window_kernel(info, own, following, out, ext):
    cuts, pair, _, n, _ = out.shape
    stripe, columns = own.shape[1:]
    rows, cols, _ = scalars(info[...], cuts * pair)
    ext[:, :stripe] = own[...]
    ext[:, stripe:] = following[...]
    for target in range(cuts):
        for which in range(pair):
            slot = target + which * cuts
            at, down, right = spot(rows[slot], cols[slot], columns, n)
            for part in range(2):
                out[target, which, part] = cut_out(ext[(part, *at)], down, right)


def wave_kernel(scale, info, probe, amplitude, tables, patch, *rest):
    cuts, pair, _, n, _ = patch.shape
    sent, (probe_out, terms, amp, sems) = rest[:cuts], rest[cuts:]
    _, _, (live, me, *_) = scalars(info[...], cuts * pair)
    copies = [
        pltpu.make_async_copy(amplitude.at[me + which * cuts], amp.at[which], sems.at[which]) for which in range(pair)
    ]
    for copy in copies:
        copy.start()

    def patch_of(layer):
        return patch[layer, :, 0], patch[layer, :, 1]

    wave = tuple(jnp.broadcast_to(probe[part][None], (pair, n, n)) for part in range(2))
    incident = []
    for layer in range(cuts):
        incident.append(wave)
        wave = complex_mult(wave, patch_of(layer))
        if layer < cuts - 1:
            wave = both_sides(wave, tables, 0)
    far = both_sides(wave, tables, 2)
    for copy in copies:
        copy.wait()
    magnitude = jnp.sqrt(far[0] * far[0] + far[1] * far[1])
    slot = me + cuts * lax.broadcasted_iota(jnp.int32, (pair, n, n), 0)
    weight = (slot < live).astype(jnp.float32)
    factor = weight * (1.0 - amp[...] / jnp.maximum(magnitude, 1.0))
    back = both_sides((factor * far[0], factor * far[1]), tables, 3)
    for layer in range(cuts - 1, -1, -1):
        value = conj_mult(incident[layer], back)
        terms[layer, :, 0] = value[0]
        terms[layer, :, 1] = value[1]
        carry = conj_mult(patch_of(layer), back)
        if layer > 0:
            back = both_sides(carry, tables, 1)
    for away in range(cuts):
        sent[away][...] = terms[lax.rem(me + away, cuts)]
    rows = n // cuts
    share = probe_out.shape[1]
    total = [jnp.sum(carry[part], axis=0) * scale for part in range(2)]
    for cut in range(cuts):
        block = jnp.concatenate([total[part][cut * rows : (cut + 1) * rows] for part in range(2)], axis=0)
        for group in range(2 * rows // share):
            probe_out[group * cuts + cut] = block[group * share : (group + 1) * share]


def scatter_kernel(info, *rest):
    arrived, (inner, rim, canvas) = rest[:-3], rest[-3:]
    cuts = len(arrived)
    pair, _, n, _ = arrived[0].shape
    stripe, columns = inner.shape[1:]
    rows, cols, (_, me, *_) = scalars(info[...], cuts * pair)
    canvas[...] = jnp.zeros_like(canvas)
    for away in range(cuts):
        source = lax.rem(me + cuts - away, cuts)
        for which in range(pair):
            mine = slice(which * cuts, (which + 1) * cuts)
            at, down, right = spot(choose(rows[mine], source), choose(cols[mine], source), columns, n)
            for part in range(2):
                spread = placed(arrived[away][which, part], down, right)
                canvas[(part, *at)] = canvas[(part, *at)] + spread
    inner[...] = canvas[:, :stripe]
    rim[:, :n] = canvas[:, stripe:]
    rim[:, n:] = jnp.zeros_like(rim[:, n:])
    rim[0, n:, :n] = info[...].astype(jnp.float32)


def total_kernel(rows, out):
    out[...] = jnp.broadcast_to(jnp.sum(rows[...], axis=0)[None], out.shape)


def final_kernel(slots, inner, rim, light, probe, rows, slice_grad, probe_grad, canvas):
    n = probe.shape[1]
    stripe = light.shape[0]
    canvas[:stripe] = jnp.zeros_like(light)
    canvas[stripe:] = light[...]
    lit(slots, rim[0, n:, :n].astype(jnp.int32), probe, canvas)
    whole = canvas[stripe:]
    for part in range(2):
        slice_grad[part, 0] = (inner[part] + rim[part, :n]) / whole
    probe_grad[...] = rows[...].reshape(probe_grad.shape)


def along(block, distance):
    devices = range(lax.axis_size(POS))
    return lax.ppermute(block, POS, [(i - distance, i) for i in devices if i - distance in devices])


def around(block, distance):
    count = lax.axis_size("cuts")
    return lax.ppermute(block, "cuts", [(i, (i + distance) % count) for i in range(count)])


def swap(block, axes):
    return lax.all_to_all(block, axes, 0, 0)


def after(block, *first):
    return lax.optimization_barrier((block, *first))[0]


def local(specimen, probe, amplitude, offsets, live):
    n = probe.shape[1]
    stripe, columns = specimen.shape[2:]
    slots = amplitude.shape[0]
    across = lax.axis_size(POS)
    cuts = lax.axis_size("cuts")
    pair = slots // cuts
    me = lax.axis_index("cuts")
    own = specimen[:, 0]
    following = along(own, -1)
    row = offsets[0] - lax.axis_index(POS) * stripe
    extra = jnp.zeros((slots,), jnp.int32).at[0].set(live[0]).at[1].set(me)
    info = jnp.pad(jnp.stack([row, offsets[1], extra]), ((0, 5), (0, n - slots)))
    vmem = pl.BlockSpec(memory_space=pltpu.VMEM)
    hbm = pl.BlockSpec(memory_space=pltpu.HBM)
    tables = jnp.asarray(table_stack(n))
    stripe_shape = jax.ShapeDtypeStruct((2, stripe, columns), jnp.float32)
    plane_shape = jax.ShapeDtypeStruct((stripe, columns), jnp.float32)
    packet = jax.ShapeDtypeStruct((cuts, pair, 2, n, n), jnp.float32)

    own, probe = pl.pallas_call(
        stage_kernel,
        out_shape=[stripe_shape, jax.ShapeDtypeStruct(probe.shape, jnp.float32)],
        in_specs=[vmem] * 2,
        out_specs=[vmem] * 2,
        compiler_params=VMEM,
        name="stage",
    )(own, probe)
    light = pl.pallas_call(
        functools.partial(light_kernel, slots),
        out_shape=plane_shape,
        in_specs=[vmem] * 2,
        out_specs=vmem,
        scratch_shapes=[pltpu.VMEM((stripe + n, columns), jnp.float32)],
        compiler_params=VMEM,
        name="light",
    )(info, probe)

    windows = pl.pallas_call(
        window_kernel,
        out_shape=packet,
        in_specs=[vmem] * 3,
        out_specs=vmem,
        scratch_shapes=[pltpu.VMEM((2, 2 * stripe, columns), jnp.float32)],
        compiler_params=VMEM,
        name="windows",
    )(after(info, light), own, following)
    patches = swap(windows, "cuts")

    shares = lax.axis_size(("z", "cuts"))
    packet = jax.ShapeDtypeStruct((pair, 2, n, n), jnp.float32)
    *terms, probe_parts = pl.pallas_call(
        functools.partial(wave_kernel, 1.0 / math.sqrt(slots * across)),
        out_shape=[packet] * cuts + [jax.ShapeDtypeStruct((shares, 2 * n // shares, n), jnp.float32)],
        in_specs=[vmem, vmem, hbm, vmem, vmem],
        out_specs=[vmem] * (cuts + 1),
        scratch_shapes=[
            pltpu.VMEM((cuts, pair, 2, n, n), jnp.float32),
            pltpu.VMEM((pair, n, n), jnp.float32),
            pltpu.SemaphoreType.DMA((pair,)),
        ],
        compiler_params=VMEM,
        name="waves",
    )(info, probe, amplitude, tables, patches)
    def total(rows, axes, **kwargs):
        return pl.pallas_call(
            total_kernel,
            out_shape=jax.ShapeDtypeStruct((lax.axis_size(axes), *rows.shape[1:]), jnp.float32),
            in_specs=[vmem],
            out_specs=vmem,
            compiler_params=VMEM,
            name="total",
            **kwargs,
        )(rows)

    gathered = [terms[0]] + [around(terms[away], away) for away in range(1, cuts)]
    probe_rows = swap(probe_parts, ("z", "cuts"))
    probe_rows, gathered[2] = lax.optimization_barrier((probe_rows, gathered[2]))
    probe_rows = total(probe_rows, ("y", "core"))
    later = after(info, probe_rows)
    estimate = pl.CostEstimate(flops=10**11, bytes_accessed=10**8, transcendentals=0)
    probe_rows = total(swap(probe_rows, ("y", "core")), "z", cost_estimate=estimate)

    inner, rim = pl.pallas_call(
        scatter_kernel,
        out_shape=[stripe_shape, jax.ShapeDtypeStruct((2, n + 8, columns), jnp.float32)],
        in_specs=[vmem] * (cuts + 1),
        out_specs=[vmem] * 2,
        scratch_shapes=[pltpu.VMEM((2, stripe + n, columns), jnp.float32)],
        compiler_params=VMEM,
        name="scatter",
    )(later, *gathered)
    rim_in = along(rim, 1)
    probe_rows = swap(probe_rows, "z")
    slice_grad, probe_grad = pl.pallas_call(
        functools.partial(final_kernel, slots),
        out_shape=[
            jax.ShapeDtypeStruct((2, 1, stripe, columns), jnp.float32),
            jax.ShapeDtypeStruct((2, n // cuts, n), jnp.float32),
        ],
        in_specs=[vmem] * 5,
        out_specs=[vmem] * 2,
        scratch_shapes=[pltpu.VMEM((stripe + n, columns), jnp.float32)],
        compiler_params=VMEM,
        name="final",
    )(inner, rim_in, light, probe, probe_rows)
    return slice_grad, probe_grad


def solution(mesh):
    across, cuts = mesh.devices.shape
    y = min(8, across // 2)
    split = Mesh(mesh.devices.reshape(across // 2 // y, y, 2, cuts), ("z", "y", "core", "cuts"))
    in_specs = (P(None, "cuts", POS, None), P(), P(POS, None, None), P(None, POS), P(POS))
    out_specs = (P(None, "cuts", POS, None), P(None, "cuts", None))
    return jax.shard_map(local, mesh=split, in_specs=in_specs, out_specs=out_specs, check_vma=False)
```

```python
import functools
import math

import jax
import jax.numpy as jnp
import numpy as np
from jax import lax
from jax.experimental import pallas as pl
from jax.experimental.pallas import tpu as pltpu
from jax.sharding import Mesh
from jax.sharding import PartitionSpec as P

FRESNEL = 0.7
POS = ("z", "y", "core")
VMEM = pltpu.CompilerParams(vmem_limit_bytes=16 * 1024 * 1024)


def make_tables(n):
    index = np.arange(n)
    four = np.exp(-2j * math.pi / n * (index[:, None] * index[None, :] % n)) / math.sqrt(n)
    signed = np.where(index < n // 2, index, index - n)
    spacing = (index[:, None] - index[None, :]) % n
    turns = spacing[:, :, None] * index[None, None, :] % n
    phase = FRESNEL * math.pi / n * (signed * signed)
    prop = np.mean(np.exp(1j * (phase[None, None, :] + 2.0 * math.pi / n * turns)), axis=2)
    return four, prop


def split_pair(table):
    whole = np.block([[table.real, table.imag], [-table.imag, table.real]]).astype(np.float32)
    lead = whole.astype(jnp.bfloat16)
    return np.stack([lead, (whole - lead.astype(np.float32)).astype(jnp.bfloat16)])


def table_stack(n):
    four, prop = make_tables(n)
    return np.stack([split_pair(prop), split_pair(prop.conj()), split_pair(four), split_pair(four.conj())])


def parts(x):
    lead = x.astype(jnp.bfloat16)
    return lead, (x - lead.astype(jnp.float32)).astype(jnp.bfloat16)


def dot(a, b):
    return jnp.dot(a, b, preferred_element_type=jnp.float32)


def both_sides(wave, tables, which):
    real, imag = wave
    n = real.shape[1]
    right_lead, right_trail = tables[which, 0], tables[which, 1]
    left_lead, left_trail = tables[which ^ 1, 0], tables[which ^ 1, 1]
    halves = []
    for p in range(real.shape[0]):
        lead, trail = parts(jnp.concatenate([real[p], imag[p]], axis=1))
        mid = dot(lead, right_lead) + (dot(trail, right_lead) + dot(lead, right_trail))
        halves.append(parts(jnp.concatenate([mid[:, :n], mid[:, n:]], axis=0)))
    outs = []
    for lead, trail in halves:
        both = dot(left_lead, jnp.concatenate([lead, trail], axis=1))
        outs.append(both[:, :n] + (both[:, n:] + dot(left_trail, lead)))
    return jnp.stack([out[:n] for out in outs]), jnp.stack([out[n:] for out in outs])


def complex_mult(a, b):
    return a[0] * b[0] - a[1] * b[1], a[0] * b[1] + a[1] * b[0]


def conj_mult(a, b):
    return a[0] * b[0] + a[1] * b[1], a[0] * b[1] - a[1] * b[0]


def scalars(info, slots):
    return [[info[line, slot] for slot in range(slots)] for line in range(3)]


def choose(values, index):
    chosen = values[0]
    for position in range(1, len(values)):
        chosen = jnp.where(index == position, values[position], chosen)
    return chosen


def spot(row, col, columns, n):
    top = pl.multiple_of(row // 8 * 8, 8)
    band = pl.multiple_of(jnp.minimum(col // n * n, columns - 2 * n), n)
    return (pl.ds(top, n + 8), pl.ds(band, 2 * n)), row - top, col - band


def cut_out(box, down, right):
    n = box.shape[1] // 2
    turn = lax.rem(n - right, n)
    lane = lax.broadcasted_iota(jnp.int32, (n + 8, n), 1)
    wide = jnp.where(lane < n - right, pltpu.roll(box[:, :n], turn, axis=1), pltpu.roll(box[:, n:], turn, axis=1))
    groups = pltpu.roll(wide.reshape(n // 8 + 1, 8, n), lax.rem(8 - down, 8), axis=1)
    line = lax.broadcasted_iota(jnp.int32, (n // 8, 8, n), 1)
    return jnp.where(line < 8 - down, groups[:-1], groups[1:]).reshape(n, n)


def placed(value, down, right):
    n = value.shape[0]
    groups = pltpu.roll(value.reshape(n // 8, 8, n), down, axis=1)
    empty = jnp.zeros((1, 8, n), jnp.float32)
    line = lax.broadcasted_iota(jnp.int32, (n // 8 + 1, 8, n), 1)
    tall = jnp.where(
        line >= down, jnp.concatenate([groups, empty], axis=0), jnp.concatenate([empty, groups], axis=0)
    ).reshape(n + 8, n)
    tall = pltpu.roll(tall, lax.rem(right, n), axis=1)
    lane = lax.broadcasted_iota(jnp.int32, (n + 8, n), 1)
    return jnp.concatenate([jnp.where(lane >= right, tall, 0.0), jnp.where(lane < right, tall, 0.0)], axis=1)


def stage_kernel(own, probe, own_copy, probe_copy):
    own_copy[...] = own[...]
    probe_copy[...] = probe[...]


def lit(slots, places, probe, canvas):
    n = probe.shape[1]
    columns = canvas.shape[1]
    power = probe[0] * probe[0] + probe[1] * probe[1]
    rows, cols, (live, *_) = scalars(places, slots)
    for slot in range(slots):
        at, down, right = spot(rows[slot], cols[slot], columns, n)
        canvas[at] = canvas[at] + placed(jnp.where(slot < live, power, 0.0), down, right)


def light_kernel(slots, info, probe, light, canvas):
    canvas[...] = jnp.ones_like(canvas)
    lit(slots, info[...], probe, canvas)
    light[...] = canvas[: light.shape[0]]


def window_kernel(info, own, following, out, ext):
    cuts, pair, _, n, _ = out.shape
    stripe, columns = own.shape[1:]
    rows, cols, _ = scalars(info[...], cuts * pair)
    ext[:, :stripe] = own[...]
    ext[:, stripe:] = following[...]
    for target in range(cuts):
        for which in range(pair):
            slot = target + which * cuts
            at, down, right = spot(rows[slot], cols[slot], columns, n)
            for part in range(2):
                out[target, which, part] = cut_out(ext[(part, *at)], down, right)


def wave_kernel(scale, info, probe, amplitude, tables, patch, *rest):
    cuts, pair, _, n, _ = patch.shape
    sent, (probe_out, terms, amp, sems) = rest[:cuts], rest[cuts:]
    _, _, (live, me, *_) = scalars(info[...], cuts * pair)
    copies = [
        pltpu.make_async_copy(amplitude.at[me + which * cuts], amp.at[which], sems.at[which]) for which in range(pair)
    ]
    for copy in copies:
        copy.start()

    def patch_of(layer):
        return patch[layer, :, 0], patch[layer, :, 1]

    wave = tuple(jnp.broadcast_to(probe[part][None], (pair, n, n)) for part in range(2))
    incident = []
    for layer in range(cuts):
        incident.append(wave)
        wave = complex_mult(wave, patch_of(layer))
        if layer < cuts - 1:
            wave = both_sides(wave, tables, 0)
    far = both_sides(wave, tables, 2)
    for copy in copies:
        copy.wait()
    magnitude = jnp.sqrt(far[0] * far[0] + far[1] * far[1])
    slot = me + cuts * lax.broadcasted_iota(jnp.int32, (pair, n, n), 0)
    weight = (slot < live).astype(jnp.float32)
    factor = weight * (1.0 - amp[...] / jnp.maximum(magnitude, 1.0))
    back = both_sides((factor * far[0], factor * far[1]), tables, 3)
    for layer in range(cuts - 1, -1, -1):
        value = conj_mult(incident[layer], back)
        terms[layer, :, 0] = value[0]
        terms[layer, :, 1] = value[1]
        carry = conj_mult(patch_of(layer), back)
        if layer > 0:
            back = both_sides(carry, tables, 1)
    for away in range(cuts):
        sent[away][...] = terms[lax.rem(me + away, cuts)]
    rows = n // cuts
    share = probe_out.shape[1]
    total = [jnp.sum(carry[part], axis=0) * scale for part in range(2)]
    for cut in range(cuts):
        block = jnp.concatenate([total[part][cut * rows : (cut + 1) * rows] for part in range(2)], axis=0)
        for group in range(2 * rows // share):
            probe_out[group * cuts + cut] = block[group * share : (group + 1) * share]


def scatter_kernel(info, *rest):
    arrived, (inner, rim, canvas) = rest[:-3], rest[-3:]
    cuts = len(arrived)
    pair, _, n, _ = arrived[0].shape
    stripe, columns = inner.shape[1:]
    rows, cols, (_, me, *_) = scalars(info[...], cuts * pair)
    canvas[...] = jnp.zeros_like(canvas)
    for away in range(cuts):
        source = lax.rem(me + cuts - away, cuts)
        for which in range(pair):
            mine = slice(which * cuts, (which + 1) * cuts)
            at, down, right = spot(choose(rows[mine], source), choose(cols[mine], source), columns, n)
            for part in range(2):
                spread = placed(arrived[away][which, part], down, right)
                canvas[(part, *at)] = canvas[(part, *at)] + spread
    inner[...] = canvas[:, :stripe]
    rim[:, :n] = canvas[:, stripe:]
    rim[:, n:] = jnp.zeros_like(rim[:, n:])
    rim[0, n:, :n] = info[...].astype(jnp.float32)


def total_kernel(rows, out):
    out[...] = jnp.broadcast_to(jnp.sum(rows[...], axis=0)[None], out.shape)


def final_kernel(slots, inner, rim, light, probe, rows, slice_grad, probe_grad, canvas):
    n = probe.shape[1]
    stripe = light.shape[0]
    canvas[:stripe] = jnp.zeros_like(light)
    canvas[stripe:] = light[...]
    lit(slots, rim[0, n:, :n].astype(jnp.int32), probe, canvas)
    whole = canvas[stripe:]
    for part in range(2):
        slice_grad[part, 0] = (inner[part] + rim[part, :n]) / whole
    probe_grad[...] = rows[...].reshape(probe_grad.shape)


def along(block, distance):
    devices = range(lax.axis_size(POS))
    return lax.ppermute(block, POS, [(i - distance, i) for i in devices if i - distance in devices])


def around(block, distance):
    count = lax.axis_size("cuts")
    return lax.ppermute(block, "cuts", [(i, (i + distance) % count) for i in range(count)])


def swap(block, axes):
    return lax.all_to_all(block, axes, 0, 0)


def after(block, *first):
    return lax.optimization_barrier((block, *first))[0]


def local(specimen, probe, amplitude, offsets, live):
    n = probe.shape[1]
    stripe, columns = specimen.shape[2:]
    slots = amplitude.shape[0]
    across = lax.axis_size(POS)
    cuts = lax.axis_size("cuts")
    pair = slots // cuts
    me = lax.axis_index("cuts")
    own = specimen[:, 0]
    following = along(own, -1)
    row = offsets[0] - lax.axis_index(POS) * stripe
    extra = jnp.zeros((slots,), jnp.int32).at[0].set(live[0]).at[1].set(me)
    info = jnp.pad(jnp.stack([row, offsets[1], extra]), ((0, 5), (0, n - slots)))
    vmem = pl.BlockSpec(memory_space=pltpu.VMEM)
    hbm = pl.BlockSpec(memory_space=pltpu.HBM)
    tables = jnp.asarray(table_stack(n))
    stripe_shape = jax.ShapeDtypeStruct((2, stripe, columns), jnp.float32)
    plane_shape = jax.ShapeDtypeStruct((stripe, columns), jnp.float32)
    packet = jax.ShapeDtypeStruct((cuts, pair, 2, n, n), jnp.float32)

    own, probe = pl.pallas_call(
        stage_kernel,
        out_shape=[stripe_shape, jax.ShapeDtypeStruct(probe.shape, jnp.float32)],
        in_specs=[vmem] * 2,
        out_specs=[vmem] * 2,
        compiler_params=VMEM,
        name="stage",
    )(own, probe)
    light = pl.pallas_call(
        functools.partial(light_kernel, slots),
        out_shape=plane_shape,
        in_specs=[vmem] * 2,
        out_specs=vmem,
        scratch_shapes=[pltpu.VMEM((stripe + n, columns), jnp.float32)],
        compiler_params=VMEM,
        name="light",
    )(info, probe)

    windows = pl.pallas_call(
        window_kernel,
        out_shape=packet,
        in_specs=[vmem] * 3,
        out_specs=vmem,
        scratch_shapes=[pltpu.VMEM((2, 2 * stripe, columns), jnp.float32)],
        compiler_params=VMEM,
        name="windows",
    )(after(info, light), own, following)
    patches = swap(windows, "cuts")

    shares = lax.axis_size(("y", "cuts"))
    packet = jax.ShapeDtypeStruct((pair, 2, n, n), jnp.float32)
    *terms, probe_parts = pl.pallas_call(
        functools.partial(wave_kernel, 1.0 / math.sqrt(slots * across)),
        out_shape=[packet] * cuts + [jax.ShapeDtypeStruct((shares, 2 * n // shares, n), jnp.float32)],
        in_specs=[vmem, vmem, hbm, vmem, vmem],
        out_specs=[vmem] * (cuts + 1),
        scratch_shapes=[
            pltpu.VMEM((cuts, pair, 2, n, n), jnp.float32),
            pltpu.VMEM((pair, n, n), jnp.float32),
            pltpu.SemaphoreType.DMA((pair,)),
        ],
        compiler_params=VMEM,
        name="waves",
    )(info, probe, amplitude, tables, patches)
    def total(rows, axes, **kwargs):
        return pl.pallas_call(
            total_kernel,
            out_shape=jax.ShapeDtypeStruct((lax.axis_size(axes), *rows.shape[1:]), jnp.float32),
            in_specs=[vmem],
            out_specs=vmem,
            compiler_params=VMEM,
            name="total",
            **kwargs,
        )(rows)

    gathered = [terms[0]] + [around(terms[away], away) for away in range(1, cuts)]
    probe_rows = swap(probe_parts, ("y", "cuts"))
    probe_rows, gathered[2] = lax.optimization_barrier((probe_rows, gathered[2]))
    probe_rows = total(probe_rows, ("z", "core"))
    later = after(info, probe_rows)
    estimate = pl.CostEstimate(flops=10**11, bytes_accessed=10**8, transcendentals=0)
    probe_rows = total(swap(probe_rows, ("z", "core")), "y", cost_estimate=estimate)

    inner, rim = pl.pallas_call(
        scatter_kernel,
        out_shape=[stripe_shape, jax.ShapeDtypeStruct((2, n + 8, columns), jnp.float32)],
        in_specs=[vmem] * (cuts + 1),
        out_specs=[vmem] * 2,
        scratch_shapes=[pltpu.VMEM((2, stripe + n, columns), jnp.float32)],
        compiler_params=VMEM,
        name="scatter",
    )(later, *gathered)
    rim_in = along(rim, 1)
    probe_rows = swap(probe_rows, "y")
    slice_grad, probe_grad = pl.pallas_call(
        functools.partial(final_kernel, slots),
        out_shape=[
            jax.ShapeDtypeStruct((2, 1, stripe, columns), jnp.float32),
            jax.ShapeDtypeStruct((2, n // cuts, n), jnp.float32),
        ],
        in_specs=[vmem] * 5,
        out_specs=[vmem] * 2,
        scratch_shapes=[pltpu.VMEM((stripe + n, columns), jnp.float32)],
        compiler_params=VMEM,
        name="final",
    )(inner, rim_in, light, probe, probe_rows)
    return slice_grad, probe_grad


def solution(mesh):
    across, cuts = mesh.devices.shape
    y = min(8, across // 2)
    split = Mesh(mesh.devices.reshape(across // 2 // y, y, 2, cuts), ("z", "y", "core", "cuts"))
    in_specs = (P(None, "cuts", POS, None), P(), P(POS, None, None), P(None, POS), P(POS))
    out_specs = (P(None, "cuts", POS, None), P(None, "cuts", None))
    return jax.shard_map(local, mesh=split, in_specs=in_specs, out_specs=out_specs, check_vma=False)
```

```python
import functools
import math

import jax
import jax.numpy as jnp
import numpy as np
from jax import lax
from jax.experimental import pallas as pl
from jax.experimental.pallas import tpu as pltpu
from jax.sharding import Mesh
from jax.sharding import PartitionSpec as P

FRESNEL = 0.7
POS = ("z", "y", "core")
VMEM = pltpu.CompilerParams(vmem_limit_bytes=16 * 1024 * 1024)


def make_tables(n):
    index = np.arange(n)
    four = np.exp(-2j * math.pi / n * (index[:, None] * index[None, :] % n)) / math.sqrt(n)
    signed = np.where(index < n // 2, index, index - n)
    spacing = (index[:, None] - index[None, :]) % n
    turns = spacing[:, :, None] * index[None, None, :] % n
    phase = FRESNEL * math.pi / n * (signed * signed)
    prop = np.mean(np.exp(1j * (phase[None, None, :] + 2.0 * math.pi / n * turns)), axis=2)
    return four, prop


def split_pair(table):
    whole = np.block([[table.real, table.imag], [-table.imag, table.real]]).astype(np.float32)
    lead = whole.astype(jnp.bfloat16)
    return np.stack([lead, (whole - lead.astype(np.float32)).astype(jnp.bfloat16)])


def table_stack(n):
    four, prop = make_tables(n)
    return np.stack([split_pair(prop), split_pair(prop.conj()), split_pair(four), split_pair(four.conj())])


def parts(x):
    lead = x.astype(jnp.bfloat16)
    return lead, (x - lead.astype(jnp.float32)).astype(jnp.bfloat16)


def dot(a, b):
    return jnp.dot(a, b, preferred_element_type=jnp.float32)


def both_sides(wave, tables, which):
    real, imag = wave
    n = real.shape[1]
    right_lead, right_trail = tables[which, 0], tables[which, 1]
    left_lead, left_trail = tables[which ^ 1, 0], tables[which ^ 1, 1]
    halves = []
    for p in range(real.shape[0]):
        lead, trail = parts(jnp.concatenate([real[p], imag[p]], axis=1))
        mid = dot(lead, right_lead) + (dot(trail, right_lead) + dot(lead, right_trail))
        halves.append(parts(jnp.concatenate([mid[:, :n], mid[:, n:]], axis=0)))
    outs = []
    for lead, trail in halves:
        both = dot(left_lead, jnp.concatenate([lead, trail], axis=1))
        outs.append(both[:, :n] + (both[:, n:] + dot(left_trail, lead)))
    return jnp.stack([out[:n] for out in outs]), jnp.stack([out[n:] for out in outs])


def complex_mult(a, b):
    return a[0] * b[0] - a[1] * b[1], a[0] * b[1] + a[1] * b[0]


def conj_mult(a, b):
    return a[0] * b[0] + a[1] * b[1], a[0] * b[1] - a[1] * b[0]


def scalars(info, slots):
    return [[info[line, slot] for slot in range(slots)] for line in range(3)]


def choose(values, index):
    chosen = values[0]
    for position in range(1, len(values)):
        chosen = jnp.where(index == position, values[position], chosen)
    return chosen


def spot(row, col, columns, n):
    top = pl.multiple_of(row // 8 * 8, 8)
    band = pl.multiple_of(jnp.minimum(col // n * n, columns - 2 * n), n)
    return (pl.ds(top, n + 8), pl.ds(band, 2 * n)), row - top, col - band


def cut_out(box, down, right):
    n = box.shape[1] // 2
    lane = lax.broadcasted_iota(jnp.int32, (n + 8, n), 1)
    wide = jnp.where(lane >= right, box[:, :n], box[:, n:])
    groups = pltpu.roll(wide, lax.rem(n - right, n), axis=1).reshape(n // 8 + 1, 8, n)
    line = lax.broadcasted_iota(jnp.int32, (n // 8, 8, n), 1)
    chosen = jnp.where(line >= down, groups[:-1], groups[1:])
    return pltpu.roll(chosen, lax.rem(8 - down, 8), axis=1).reshape(n, n)


def placed(value, down, right):
    n = value.shape[0]
    groups = pltpu.roll(value.reshape(n // 8, 8, n), down, axis=1)
    empty = jnp.zeros((1, 8, n), jnp.float32)
    line = lax.broadcasted_iota(jnp.int32, (n // 8 + 1, 8, n), 1)
    tall = jnp.where(
        line >= down, jnp.concatenate([groups, empty], axis=0), jnp.concatenate([empty, groups], axis=0)
    ).reshape(n + 8, n)
    tall = pltpu.roll(tall, lax.rem(right, n), axis=1)
    lane = lax.broadcasted_iota(jnp.int32, (n + 8, n), 1)
    return jnp.concatenate([jnp.where(lane >= right, tall, 0.0), jnp.where(lane < right, tall, 0.0)], axis=1)


def stage_kernel(own, probe, own_copy, probe_copy):
    own_copy[...] = own[...]
    probe_copy[...] = probe[...]


def lit(slots, places, probe, canvas):
    n = probe.shape[1]
    columns = canvas.shape[1]
    power = probe[0] * probe[0] + probe[1] * probe[1]
    rows, cols, (live, *_) = scalars(places, slots)
    for slot in range(slots):
        at, down, right = spot(rows[slot], cols[slot], columns, n)
        canvas[at] = canvas[at] + placed(jnp.where(slot < live, power, 0.0), down, right)


def light_kernel(slots, info, probe, light, canvas):
    canvas[...] = jnp.ones_like(canvas)
    lit(slots, info[...], probe, canvas)
    light[...] = canvas[: light.shape[0]]


def window_kernel(info, own, following, out, ext):
    cuts, pair, _, n, _ = out.shape
    stripe, columns = own.shape[1:]
    rows, cols, _ = scalars(info[...], cuts * pair)
    ext[:, :stripe] = own[...]
    ext[:, stripe:] = following[...]
    for target in range(cuts):
        for which in range(pair):
            slot = target + which * cuts
            at, down, right = spot(rows[slot], cols[slot], columns, n)
            for part in range(2):
                out[target, which, part] = cut_out(ext[(part, *at)], down, right)


def wave_kernel(scale, info, probe, amplitude, tables, patch, *rest):
    cuts, pair, _, n, _ = patch.shape
    sent, (probe_out, terms, amp, sems) = rest[:cuts], rest[cuts:]
    _, _, (live, me, *_) = scalars(info[...], cuts * pair)
    copies = [
        pltpu.make_async_copy(amplitude.at[me + which * cuts], amp.at[which], sems.at[which]) for which in range(pair)
    ]
    for copy in copies:
        copy.start()

    def patch_of(layer):
        return patch[layer, :, 0], patch[layer, :, 1]

    wave = tuple(jnp.broadcast_to(probe[part][None], (pair, n, n)) for part in range(2))
    incident = []
    for layer in range(cuts):
        incident.append(wave)
        wave = complex_mult(wave, patch_of(layer))
        if layer < cuts - 1:
            wave = both_sides(wave, tables, 0)
    far = both_sides(wave, tables, 2)
    for copy in copies:
        copy.wait()
    magnitude = jnp.sqrt(far[0] * far[0] + far[1] * far[1])
    slot = me + cuts * lax.broadcasted_iota(jnp.int32, (pair, n, n), 0)
    weight = (slot < live).astype(jnp.float32)
    factor = weight * (1.0 - amp[...] / jnp.maximum(magnitude, 1.0))
    back = both_sides((factor * far[0], factor * far[1]), tables, 3)
    for layer in range(cuts - 1, -1, -1):
        value = conj_mult(incident[layer], back)
        terms[layer, :, 0] = value[0]
        terms[layer, :, 1] = value[1]
        carry = conj_mult(patch_of(layer), back)
        if layer > 0:
            back = both_sides(carry, tables, 1)
    for away in range(cuts):
        sent[away][...] = terms[lax.rem(me + away, cuts)]
    rows = n // cuts
    share = probe_out.shape[1]
    total = [jnp.sum(carry[part], axis=0) * scale for part in range(2)]
    for cut in range(cuts):
        block = jnp.concatenate([total[part][cut * rows : (cut + 1) * rows] for part in range(2)], axis=0)
        for group in range(2 * rows // share):
            probe_out[group * cuts + cut] = block[group * share : (group + 1) * share]


def scatter_kernel(info, *rest):
    arrived, (inner, rim, canvas) = rest[:-3], rest[-3:]
    cuts = len(arrived)
    pair, _, n, _ = arrived[0].shape
    stripe, columns = inner.shape[1:]
    rows, cols, (_, me, *_) = scalars(info[...], cuts * pair)
    canvas[...] = jnp.zeros_like(canvas)
    for away in range(cuts):
        source = lax.rem(me + cuts - away, cuts)
        for which in range(pair):
            mine = slice(which * cuts, (which + 1) * cuts)
            at, down, right = spot(choose(rows[mine], source), choose(cols[mine], source), columns, n)
            for part in range(2):
                spread = placed(arrived[away][which, part], down, right)
                canvas[(part, *at)] = canvas[(part, *at)] + spread
    inner[...] = canvas[:, :stripe]
    rim[:, :n] = canvas[:, stripe:]
    rim[:, n:] = jnp.zeros_like(rim[:, n:])
    rim[0, n:, :n] = info[...].astype(jnp.float32)


def total_kernel(rows, out):
    out[...] = jnp.broadcast_to(jnp.sum(rows[...], axis=0)[None], out.shape)


def final_kernel(slots, inner, rim, light, probe, rows, slice_grad, probe_grad, canvas):
    n = probe.shape[1]
    stripe = light.shape[0]
    canvas[:stripe] = jnp.zeros_like(light)
    canvas[stripe:] = light[...]
    lit(slots, rim[0, n:, :n].astype(jnp.int32), probe, canvas)
    whole = canvas[stripe:]
    for part in range(2):
        slice_grad[part, 0] = (inner[part] + rim[part, :n]) / whole
    probe_grad[...] = rows[...].reshape(probe_grad.shape)


def along(block, distance):
    devices = range(lax.axis_size(POS))
    return lax.ppermute(block, POS, [(i - distance, i) for i in devices if i - distance in devices])


def around(block, distance):
    count = lax.axis_size("cuts")
    return lax.ppermute(block, "cuts", [(i, (i + distance) % count) for i in range(count)])


def swap(block, axes):
    return lax.all_to_all(block, axes, 0, 0)


def after(block, *first):
    return lax.optimization_barrier((block, *first))[0]


def local(specimen, probe, amplitude, offsets, live):
    n = probe.shape[1]
    stripe, columns = specimen.shape[2:]
    slots = amplitude.shape[0]
    across = lax.axis_size(POS)
    cuts = lax.axis_size("cuts")
    pair = slots // cuts
    me = lax.axis_index("cuts")
    own = specimen[:, 0]
    following = along(own, -1)
    row = offsets[0] - lax.axis_index(POS) * stripe
    extra = jnp.zeros((slots,), jnp.int32).at[0].set(live[0]).at[1].set(me)
    info = jnp.pad(jnp.stack([row, offsets[1], extra]), ((0, 5), (0, n - slots)))
    vmem = pl.BlockSpec(memory_space=pltpu.VMEM)
    hbm = pl.BlockSpec(memory_space=pltpu.HBM)
    tables = jnp.asarray(table_stack(n))
    stripe_shape = jax.ShapeDtypeStruct((2, stripe, columns), jnp.float32)
    plane_shape = jax.ShapeDtypeStruct((stripe, columns), jnp.float32)
    packet = jax.ShapeDtypeStruct((cuts, pair, 2, n, n), jnp.float32)

    own, probe = pl.pallas_call(
        stage_kernel,
        out_shape=[stripe_shape, jax.ShapeDtypeStruct(probe.shape, jnp.float32)],
        in_specs=[vmem] * 2,
        out_specs=[vmem] * 2,
        compiler_params=VMEM,
        name="stage",
    )(own, probe)
    light = pl.pallas_call(
        functools.partial(light_kernel, slots),
        out_shape=plane_shape,
        in_specs=[vmem] * 2,
        out_specs=vmem,
        scratch_shapes=[pltpu.VMEM((stripe + n, columns), jnp.float32)],
        compiler_params=VMEM,
        name="light",
    )(info, probe)

    windows = pl.pallas_call(
        window_kernel,
        out_shape=packet,
        in_specs=[vmem] * 3,
        out_specs=vmem,
        scratch_shapes=[pltpu.VMEM((2, 2 * stripe, columns), jnp.float32)],
        compiler_params=VMEM,
        name="windows",
    )(after(info, light), own, following)
    patches = swap(windows, "cuts")

    shares = lax.axis_size(("y", "cuts"))
    packet = jax.ShapeDtypeStruct((pair, 2, n, n), jnp.float32)
    *terms, probe_parts = pl.pallas_call(
        functools.partial(wave_kernel, 1.0 / math.sqrt(slots * across)),
        out_shape=[packet] * cuts + [jax.ShapeDtypeStruct((shares, 2 * n // shares, n), jnp.float32)],
        in_specs=[vmem, vmem, hbm, vmem, vmem],
        out_specs=[vmem] * (cuts + 1),
        scratch_shapes=[
            pltpu.VMEM((cuts, pair, 2, n, n), jnp.float32),
            pltpu.VMEM((pair, n, n), jnp.float32),
            pltpu.SemaphoreType.DMA((pair,)),
        ],
        compiler_params=VMEM,
        name="waves",
    )(info, probe, amplitude, tables, patches)
    def total(rows, axes, **kwargs):
        return pl.pallas_call(
            total_kernel,
            out_shape=jax.ShapeDtypeStruct((lax.axis_size(axes), *rows.shape[1:]), jnp.float32),
            in_specs=[vmem],
            out_specs=vmem,
            compiler_params=VMEM,
            name="total",
            **kwargs,
        )(rows)

    gathered = [terms[0]] + [around(terms[away], away) for away in range(1, cuts)]
    probe_rows = swap(probe_parts, ("y", "cuts"))
    probe_rows, gathered[2] = lax.optimization_barrier((probe_rows, gathered[2]))
    probe_rows = total(probe_rows, ("z", "core"))
    later = after(info, probe_rows)
    estimate = pl.CostEstimate(flops=10**11, bytes_accessed=10**8, transcendentals=0)
    probe_rows = total(swap(probe_rows, ("z", "core")), "y", cost_estimate=estimate)

    inner, rim = pl.pallas_call(
        scatter_kernel,
        out_shape=[stripe_shape, jax.ShapeDtypeStruct((2, n + 8, columns), jnp.float32)],
        in_specs=[vmem] * (cuts + 1),
        out_specs=[vmem] * 2,
        scratch_shapes=[pltpu.VMEM((2, stripe + n, columns), jnp.float32)],
        compiler_params=VMEM,
        name="scatter",
    )(later, *gathered)
    rim_in = along(rim, 1)
    probe_rows = swap(probe_rows, "y")
    slice_grad, probe_grad = pl.pallas_call(
        functools.partial(final_kernel, slots),
        out_shape=[
            jax.ShapeDtypeStruct((2, 1, stripe, columns), jnp.float32),
            jax.ShapeDtypeStruct((2, n // cuts, n), jnp.float32),
        ],
        in_specs=[vmem] * 5,
        out_specs=[vmem] * 2,
        scratch_shapes=[pltpu.VMEM((stripe + n, columns), jnp.float32)],
        compiler_params=VMEM,
        name="final",
    )(inner, rim_in, light, probe, probe_rows)
    return slice_grad, probe_grad


def solution(mesh):
    across, cuts = mesh.devices.shape
    y = min(8, across // 2)
    split = Mesh(mesh.devices.reshape(across // 2 // y, y, 2, cuts), ("z", "y", "core", "cuts"))
    in_specs = (P(None, "cuts", POS, None), P(), P(POS, None, None), P(None, POS), P(POS))
    out_specs = (P(None, "cuts", POS, None), P(None, "cuts", None))
    return jax.shard_map(local, mesh=split, in_specs=in_specs, out_specs=out_specs, check_vma=False)
```

```python
import functools
import math

import jax
import jax.numpy as jnp
import numpy as np
from jax import lax
from jax.experimental import pallas as pl
from jax.experimental.pallas import tpu as pltpu
from jax.sharding import Mesh
from jax.sharding import PartitionSpec as P

FRESNEL = 0.7
POS = ("z", "y", "core")
VMEM = pltpu.CompilerParams(vmem_limit_bytes=16 * 1024 * 1024)


def make_tables(n):
    index = np.arange(n)
    four = np.exp(-2j * math.pi / n * (index[:, None] * index[None, :] % n)) / math.sqrt(n)
    signed = np.where(index < n // 2, index, index - n)
    spacing = (index[:, None] - index[None, :]) % n
    turns = spacing[:, :, None] * index[None, None, :] % n
    phase = FRESNEL * math.pi / n * (signed * signed)
    prop = np.mean(np.exp(1j * (phase[None, None, :] + 2.0 * math.pi / n * turns)), axis=2)
    return four, prop


def split_pair(table):
    whole = np.block([[table.real, table.imag], [-table.imag, table.real]]).astype(np.float32)
    lead = whole.astype(jnp.bfloat16)
    return np.stack([lead, (whole - lead.astype(np.float32)).astype(jnp.bfloat16)])


def table_stack(n):
    four, prop = make_tables(n)
    return np.stack([split_pair(prop), split_pair(prop.conj()), split_pair(four), split_pair(four.conj())])


def parts(x):
    lead = x.astype(jnp.bfloat16)
    return lead, (x - lead.astype(jnp.float32)).astype(jnp.bfloat16)


def dot(a, b):
    return jnp.dot(a, b, preferred_element_type=jnp.float32)


def both_sides(wave, tables, which):
    real, imag = wave
    n = real.shape[1]
    right_lead, right_trail = tables[which, 0], tables[which, 1]
    left_lead, left_trail = tables[which ^ 1, 0], tables[which ^ 1, 1]
    halves = []
    for p in range(real.shape[0]):
        lead, trail = parts(jnp.concatenate([real[p], imag[p]], axis=1))
        mid = dot(lead, right_lead) + (dot(trail, right_lead) + dot(lead, right_trail))
        halves.append(parts(jnp.concatenate([mid[:, :n], mid[:, n:]], axis=0)))
    outs = []
    for lead, trail in halves:
        both = dot(left_lead, jnp.concatenate([lead, trail], axis=1))
        outs.append(both[:, :n] + (both[:, n:] + dot(left_trail, lead)))
    return jnp.stack([out[:n] for out in outs]), jnp.stack([out[n:] for out in outs])


def complex_mult(a, b):
    return a[0] * b[0] - a[1] * b[1], a[0] * b[1] + a[1] * b[0]


def conj_mult(a, b):
    return a[0] * b[0] + a[1] * b[1], a[0] * b[1] - a[1] * b[0]


def scalars(info, slots):
    return [[info[line, slot] for slot in range(slots)] for line in range(3)]


def choose(values, index):
    chosen = values[0]
    for position in range(1, len(values)):
        chosen = jnp.where(index == position, values[position], chosen)
    return chosen


def spot(row, col, columns, n):
    top = pl.multiple_of(row // 8 * 8, 8)
    band = pl.multiple_of(jnp.minimum(col // n * n, columns - 2 * n), n)
    return (pl.ds(top, n + 8), pl.ds(band, 2 * n)), row - top, col - band


def cut_out(box, down, right):
    n = box.shape[1] // 2
    lane = lax.broadcasted_iota(jnp.int32, (n + 8, n), 1)
    wide = jnp.where(lane >= right, box[:, :n], box[:, n:])
    groups = pltpu.roll(wide, lax.rem(n - right, n), axis=1).reshape(n // 8 + 1, 8, n)
    line = lax.broadcasted_iota(jnp.int32, (n // 8, 8, n), 1)
    chosen = jnp.where(line >= down, groups[:-1], groups[1:])
    return pltpu.roll(chosen, lax.rem(8 - down, 8), axis=1).reshape(n, n)


def placed(value, down, right):
    n = value.shape[0]
    value = pltpu.roll(value, lax.rem(right, n), axis=1)
    groups = pltpu.roll(value.reshape(n // 8, 8, n), down, axis=1)
    empty = jnp.zeros((1, 8, n), jnp.float32)
    line = lax.broadcasted_iota(jnp.int32, (n // 8 + 1, 8, n), 1)
    tall = jnp.where(
        line >= down, jnp.concatenate([groups, empty], axis=0), jnp.concatenate([empty, groups], axis=0)
    ).reshape(n + 8, n)
    lane = lax.broadcasted_iota(jnp.int32, (n + 8, n), 1)
    return jnp.concatenate([jnp.where(lane >= right, tall, 0.0), jnp.where(lane < right, tall, 0.0)], axis=1)


def stage_kernel(own, probe, own_copy, probe_copy):
    own_copy[...] = own[...]
    probe_copy[...] = probe[...]


def lit(slots, places, probe, canvas):
    n = probe.shape[1]
    columns = canvas.shape[1]
    power = probe[0] * probe[0] + probe[1] * probe[1]
    rows, cols, (live, *_) = scalars(places, slots)
    for slot in range(slots):
        at, down, right = spot(rows[slot], cols[slot], columns, n)
        canvas[at] = canvas[at] + placed(jnp.where(slot < live, power, 0.0), down, right)


def light_kernel(slots, info, probe, light, canvas):
    canvas[...] = jnp.ones_like(canvas)
    lit(slots, info[...], probe, canvas)
    light[...] = canvas[: light.shape[0]]


def window_kernel(info, own, following, out, ext):
    cuts, pair, _, n, _ = out.shape
    stripe, columns = own.shape[1:]
    rows, cols, _ = scalars(info[...], cuts * pair)
    ext[:, :stripe] = own[...]
    ext[:, stripe:] = following[...]
    for target in range(cuts):
        for which in range(pair):
            slot = target + which * cuts
            at, down, right = spot(rows[slot], cols[slot], columns, n)
            for part in range(2):
                out[target, which, part] = cut_out(ext[(part, *at)], down, right)


def wave_kernel(scale, info, probe, amplitude, tables, patch, *rest):
    cuts, pair, _, n, _ = patch.shape
    sent, (probe_out, terms, amp, sems) = rest[:cuts], rest[cuts:]
    _, _, (live, me, *_) = scalars(info[...], cuts * pair)
    copies = [
        pltpu.make_async_copy(amplitude.at[me + which * cuts], amp.at[which], sems.at[which]) for which in range(pair)
    ]
    for copy in copies:
        copy.start()

    def patch_of(layer):
        return patch[layer, :, 0], patch[layer, :, 1]

    wave = tuple(jnp.broadcast_to(probe[part][None], (pair, n, n)) for part in range(2))
    incident = []
    for layer in range(cuts):
        incident.append(wave)
        wave = complex_mult(wave, patch_of(layer))
        if layer < cuts - 1:
            wave = both_sides(wave, tables, 0)
    far = both_sides(wave, tables, 2)
    for copy in copies:
        copy.wait()
    magnitude = jnp.sqrt(far[0] * far[0] + far[1] * far[1])
    slot = me + cuts * lax.broadcasted_iota(jnp.int32, (pair, n, n), 0)
    weight = (slot < live).astype(jnp.float32)
    factor = weight * (1.0 - amp[...] / jnp.maximum(magnitude, 1.0))
    back = both_sides((factor * far[0], factor * far[1]), tables, 3)
    for layer in range(cuts - 1, -1, -1):
        value = conj_mult(incident[layer], back)
        terms[layer, :, 0] = value[0]
        terms[layer, :, 1] = value[1]
        carry = conj_mult(patch_of(layer), back)
        if layer > 0:
            back = both_sides(carry, tables, 1)
    for away in range(cuts):
        sent[away][...] = terms[lax.rem(me + away, cuts)]
    rows = n // cuts
    share = probe_out.shape[1]
    total = [jnp.sum(carry[part], axis=0) * scale for part in range(2)]
    for cut in range(cuts):
        block = jnp.concatenate([total[part][cut * rows : (cut + 1) * rows] for part in range(2)], axis=0)
        for group in range(2 * rows // share):
            probe_out[group * cuts + cut] = block[group * share : (group + 1) * share]


def scatter_kernel(info, *rest):
    arrived, (inner, rim, canvas) = rest[:-3], rest[-3:]
    cuts = len(arrived)
    pair, _, n, _ = arrived[0].shape
    stripe, columns = inner.shape[1:]
    rows, cols, (_, me, *_) = scalars(info[...], cuts * pair)
    canvas[...] = jnp.zeros_like(canvas)
    for away in range(cuts):
        source = lax.rem(me + cuts - away, cuts)
        for which in range(pair):
            mine = slice(which * cuts, (which + 1) * cuts)
            at, down, right = spot(choose(rows[mine], source), choose(cols[mine], source), columns, n)
            for part in range(2):
                spread = placed(arrived[away][which, part], down, right)
                canvas[(part, *at)] = canvas[(part, *at)] + spread
    inner[...] = canvas[:, :stripe]
    rim[:, :n] = canvas[:, stripe:]
    rim[:, n:] = jnp.zeros_like(rim[:, n:])
    rim[0, n:, :n] = info[...].astype(jnp.float32)


def total_kernel(rows, out):
    out[...] = jnp.broadcast_to(jnp.sum(rows[...], axis=0)[None], out.shape)


def final_kernel(slots, inner, rim, light, probe, rows, slice_grad, probe_grad, canvas):
    n = probe.shape[1]
    stripe = light.shape[0]
    canvas[:stripe] = jnp.zeros_like(light)
    canvas[stripe:] = light[...]
    lit(slots, rim[0, n:, :n].astype(jnp.int32), probe, canvas)
    whole = canvas[stripe:]
    for part in range(2):
        slice_grad[part, 0] = (inner[part] + rim[part, :n]) / whole
    probe_grad[...] = rows[...].reshape(probe_grad.shape)


def along(block, distance):
    devices = range(lax.axis_size(POS))
    return lax.ppermute(block, POS, [(i - distance, i) for i in devices if i - distance in devices])


def around(block, distance):
    count = lax.axis_size("cuts")
    return lax.ppermute(block, "cuts", [(i, (i + distance) % count) for i in range(count)])


def swap(block, axes):
    return lax.all_to_all(block, axes, 0, 0)


def after(block, *first):
    return lax.optimization_barrier((block, *first))[0]


def local(specimen, probe, amplitude, offsets, live):
    n = probe.shape[1]
    stripe, columns = specimen.shape[2:]
    slots = amplitude.shape[0]
    across = lax.axis_size(POS)
    cuts = lax.axis_size("cuts")
    pair = slots // cuts
    me = lax.axis_index("cuts")
    own = specimen[:, 0]
    following = along(own, -1)
    row = offsets[0] - lax.axis_index(POS) * stripe
    extra = jnp.zeros((slots,), jnp.int32).at[0].set(live[0]).at[1].set(me)
    info = jnp.pad(jnp.stack([row, offsets[1], extra]), ((0, 5), (0, n - slots)))
    vmem = pl.BlockSpec(memory_space=pltpu.VMEM)
    hbm = pl.BlockSpec(memory_space=pltpu.HBM)
    tables = jnp.asarray(table_stack(n))
    stripe_shape = jax.ShapeDtypeStruct((2, stripe, columns), jnp.float32)
    plane_shape = jax.ShapeDtypeStruct((stripe, columns), jnp.float32)
    packet = jax.ShapeDtypeStruct((cuts, pair, 2, n, n), jnp.float32)

    own, probe = pl.pallas_call(
        stage_kernel,
        out_shape=[stripe_shape, jax.ShapeDtypeStruct(probe.shape, jnp.float32)],
        in_specs=[vmem] * 2,
        out_specs=[vmem] * 2,
        compiler_params=VMEM,
        name="stage",
    )(own, probe)
    light = pl.pallas_call(
        functools.partial(light_kernel, slots),
        out_shape=plane_shape,
        in_specs=[vmem] * 2,
        out_specs=vmem,
        scratch_shapes=[pltpu.VMEM((stripe + n, columns), jnp.float32)],
        compiler_params=VMEM,
        name="light",
    )(info, probe)

    windows = pl.pallas_call(
        window_kernel,
        out_shape=packet,
        in_specs=[vmem] * 3,
        out_specs=vmem,
        scratch_shapes=[pltpu.VMEM((2, 2 * stripe, columns), jnp.float32)],
        compiler_params=VMEM,
        name="windows",
    )(after(info, light), own, following)
    patches = swap(windows, "cuts")

    shares = lax.axis_size(("y", "cuts"))
    packet = jax.ShapeDtypeStruct((pair, 2, n, n), jnp.float32)
    *terms, probe_parts = pl.pallas_call(
        functools.partial(wave_kernel, 1.0 / math.sqrt(slots * across)),
        out_shape=[packet] * cuts + [jax.ShapeDtypeStruct((shares, 2 * n // shares, n), jnp.float32)],
        in_specs=[vmem, vmem, hbm, vmem, vmem],
        out_specs=[vmem] * (cuts + 1),
        scratch_shapes=[
            pltpu.VMEM((cuts, pair, 2, n, n), jnp.float32),
            pltpu.VMEM((pair, n, n), jnp.float32),
            pltpu.SemaphoreType.DMA((pair,)),
        ],
        compiler_params=VMEM,
        name="waves",
    )(info, probe, amplitude, tables, patches)
    def total(rows, axes, **kwargs):
        return pl.pallas_call(
            total_kernel,
            out_shape=jax.ShapeDtypeStruct((lax.axis_size(axes), *rows.shape[1:]), jnp.float32),
            in_specs=[vmem],
            out_specs=vmem,
            compiler_params=VMEM,
            name="total",
            **kwargs,
        )(rows)

    gathered = [terms[0]] + [around(terms[away], away) for away in range(1, cuts)]
    probe_rows = swap(probe_parts, ("y", "cuts"))
    probe_rows, gathered[2] = lax.optimization_barrier((probe_rows, gathered[2]))
    probe_rows = total(probe_rows, ("z", "core"))
    later = after(info, probe_rows)
    estimate = pl.CostEstimate(flops=10**11, bytes_accessed=10**8, transcendentals=0)
    probe_rows = total(swap(probe_rows, ("z", "core")), "y", cost_estimate=estimate)

    inner, rim = pl.pallas_call(
        scatter_kernel,
        out_shape=[stripe_shape, jax.ShapeDtypeStruct((2, n + 8, columns), jnp.float32)],
        in_specs=[vmem] * (cuts + 1),
        out_specs=[vmem] * 2,
        scratch_shapes=[pltpu.VMEM((2, stripe + n, columns), jnp.float32)],
        compiler_params=VMEM,
        name="scatter",
    )(later, *gathered)
    rim_in = along(rim, 1)
    probe_rows = swap(probe_rows, "y")
    slice_grad, probe_grad = pl.pallas_call(
        functools.partial(final_kernel, slots),
        out_shape=[
            jax.ShapeDtypeStruct((2, 1, stripe, columns), jnp.float32),
            jax.ShapeDtypeStruct((2, n // cuts, n), jnp.float32),
        ],
        in_specs=[vmem] * 5,
        out_specs=[vmem] * 2,
        scratch_shapes=[pltpu.VMEM((stripe + n, columns), jnp.float32)],
        compiler_params=VMEM,
        name="final",
    )(inner, rim_in, light, probe, probe_rows)
    return slice_grad, probe_grad


def solution(mesh):
    across, cuts = mesh.devices.shape
    y = min(8, across // 2)
    split = Mesh(mesh.devices.reshape(across // 2 // y, y, 2, cuts), ("z", "y", "core", "cuts"))
    in_specs = (P(None, "cuts", POS, None), P(), P(POS, None, None), P(None, POS), P(POS))
    out_specs = (P(None, "cuts", POS, None), P(None, "cuts", None))
    return jax.shard_map(local, mesh=split, in_specs=in_specs, out_specs=out_specs, check_vma=False)
```
